128 devices in a mesh: ep: 8 (over x, z_hi), fsdp: 16 (over y, z_lo, core).
Axes of the slice: x: 4, y: 4, z: 4 (z_hi: 2, z_lo: 2; z = z_hi * 2 + z_lo), core: 2. Of those that a mesh axis runs over, the one named last changes fastest.
Arguments:
- tokens: bfloat16 [16384, 5120], P(('ep', 'fsdp')), may hold values from -6 to 6
- norm_gain: bfloat16 [5120], P('fsdp'), may hold values from 0.099609375 to 1.8984375
- router_weight: bfloat16 [5120, 64], P('fsdp'), may hold values from -0.078125 to 0.078125
- up_weight: bfloat16 [128, 5120, 768], P(('ep', 'fsdp')), may hold values from -0.078125 to 0.078125
- down_weight: bfloat16 [128, 768, 5120], P(('ep', 'fsdp')), may hold values from -0.15625 to 0.15625
- expert_ids: int32 [16384, 2], P(('ep', 'fsdp')), may hold values from 0 to 63, all different within a row; in each aligned block of 128 rows (0 to 127, 128 to 255, ...) at most 6 rows name the same one
- cotangent: bfloat16 [16384, 5120], P(('ep', 'fsdp')), may hold values from -24 to 24
Outputs:
- mixed: bfloat16 [16384, 5120], P(('ep', 'fsdp'))
- grad_tokens: bfloat16 [16384, 5120], P(('ep', 'fsdp'))
- grad_router: float32 [5120, 64], P('fsdp')
- grad_gain: float32 [5120], P('fsdp')
The draws below stay inside these ranges and needn't reach their ends.
Inputs may be any that keep to these rules, and one draw needn't show every extreme that they name: `expert_ids`: each row names two different experts; among the 128 rows of one device no expert is named more than 6 times.
All inputs are finite; a program needn't handle non-finite values.
Results may differ from the reference program's by a relative error of at most 0.0072.
Values may be sent and summed in bfloat16 or wider, within the bound.
No kernel may reach another device: no remote copies, remote signals or barrier semaphores. Data moves between devices by JAX's collectives and lax.ppermute only.
A program may use at most 192 MiB of HBM per device.

```python
import math
import jax
import jax.numpy as jnp
import numpy as np
from jax import lax

D = 5120
FF = 1536
TOK_DEV = 128
EXPERTS = 64
CAP = 6
TOKENS = 16384
N_EP = 8
N_FSDP = 16


def raised(values, key, source, target, blocks, factor):
    def block_of(axis_at):
        return (jnp.arange(values.shape[axis_at]) // (values.shape[axis_at] // blocks)).reshape((-1,) + (1,) * (values.ndim - 1 - axis_at))

    one_side = jax.random.permutation(key, blocks)[block_of(target)]
    other_side = (block_of(target) + blocks // 2) % blocks
    return jnp.where((block_of(source) == one_side) | (block_of(source) == other_side), factor * values, values)


def block_levels(own_key, shape, cuts, smallest, top_value):
    level = 1.0
    for dim, blocks in cuts:
        steps = jax.random.uniform(jax.random.fold_in(jax.random.fold_in(own_key, 6), dim), (blocks,), jnp.float32, smallest / len(cuts), top_value / len(cuts))
        level = level * jnp.repeat(jnp.exp(steps), shape[dim] // blocks).reshape((-1,) + (1,) * (len(shape) - 1 - dim))
    return level


def routed_block(rng, own, number, rows, count, top, limit, slope):
    ranking = jax.random.permutation(rng, count)
    crowded, usual = shares(count, rows * top, limit, slope, True), shares(count, rows * top, limit, slope, False)
    places = jnp.arange(count)

    def named(sizes, rotation):
        used = int((sizes > 0).sum())
        fixed = max(1, used // 4)
        moved = fixed + (places - fixed + rotation * (used - fixed)) % max(1, count - fixed)
        return jnp.zeros((count,), jnp.int32).at[ranking[jnp.where(places < fixed, places, moved)]].set(jnp.asarray(sizes, jnp.int32))

    sizes = jnp.where(number % 4 == 0, named(crowded, number // 4), named(usual, number - number // 4 - 1))
    mixed = jax.random.permutation(jax.random.fold_in(own, 3), count)
    giver, taker = mixed[0:count // 2 * 2:2], mixed[1:count // 2 * 2:2]
    room = jnp.minimum(sizes[giver] - 1, limit - sizes[taker]) // 2
    room = jnp.where((giver == ranking[0]) | (taker == ranking[0]) | (sizes[taker] == 0), 0, jnp.maximum(room, 0))
    moved = jax.random.randint(jax.random.fold_in(own, 4), (count // 2,), 0, 1 << 20) % (room + 1)
    sizes = sizes.at[giver].add(-moved).at[taker].add(moved)
    labels = jnp.searchsorted(jnp.cumsum(sizes), jnp.arange(rows * top), side="right").astype(jnp.int32)
    grid = labels.reshape(top, rows).T
    grid = grid[jax.random.permutation(jax.random.fold_in(own, 1), rows)]
    rotation = jax.random.randint(jax.random.fold_in(own, 2), (rows, 1), 0, top)
    return jnp.take_along_axis(grid, (jnp.arange(top)[None, :] + rotation) % top, axis=1)


def shares(amount, total, most, slope, full):
    loads = [(1 << 20) // math.isqrt(standing ** slope) + 1 for standing in range(1, amount + 1)]
    largest = most if full else min(most, max(-(-total // amount), total * loads[0] // sum(loads)))
    least = 1 if total - largest >= amount - 1 else 0
    holding, rest = [largest] + [least] * (amount - 1), total - largest - least * (amount - 1)
    while rest > 0:
        free = [i for i in range(1, amount) if holding[i] < largest] or [i for i in range(1, amount) if holding[i] < most]
        whole, left = sum([loads[i] for i in free]), rest
        for i in free:
            more = min(most - holding[i], max(1, left * loads[i] // whole), rest)
            holding[i] = holding[i] + more
            rest = rest - more
    return np.array(holding)


def normal_values(own_key, shape, scale, most, pieces=(), kind=jnp.bfloat16):
    loudness = block_levels(own_key, shape, pieces, -0.22, 0.18) if pieces else 1.0
    values = jax.random.normal(own_key, shape, jnp.float32) * scale * loudness
    return jnp.minimum(jnp.maximum(values, -most), most).astype(kind)


def bell_draw_with(own_key, shape, width, most, cuts, heavy, kind=jnp.bfloat16):
    values = width * jax.random.normal(own_key, shape, jnp.float32)
    if cuts:
        values = values * block_levels(own_key, shape, cuts, -0.22, 0.18)
    return jnp.clip(raised(values, jax.random.fold_in(own_key, 3), *heavy), -most, most).astype(kind)


def setup_inputs(seed: int = 0) -> dict:
    keys = jax.random.split(jax.random.key(seed), 8)
    tokens = normal_values(keys[0], (TOKENS, D), 1.0, 6.0, ((0, 128),))
    norm_gain = jnp.clip(1.0 + 0.18 * jax.random.normal(keys[1], (D,), jnp.float32), 0.099609375, 1.8984375).astype(jnp.bfloat16)
    router_weight = normal_values(keys[2], (D, EXPERTS), D ** -0.5, 0.078125, ((0, 16),))
    up_weight = normal_values(keys[3], (2 * EXPERTS, D, FF // 2), D ** -0.5, 0.078125, ((0, 128),))
    down_weight = normal_values(keys[4], (2 * EXPERTS, FF // 2, D), FF ** -0.5, 0.15625, ((0, 128),))
    expert_ids_keys = jax.random.split(jax.random.fold_in(keys[5], 1), TOKENS // TOK_DEV)
    expert_ids_turns = jax.random.permutation(jax.random.fold_in(keys[5], 3), TOKENS // TOK_DEV)
    expert_ids = jax.vmap(lambda own, number: routed_block(jax.random.fold_in(keys[5], 2), own, number, TOK_DEV, EXPERTS, 2, CAP, 2))(expert_ids_keys, expert_ids_turns).reshape((TOKENS, 2))
    cotangent = bell_draw_with(keys[6], (TOKENS, D), 1.0, 24.0, ((0, 128),), (0, 1, 128, 5.5))
    return dict(tokens=tokens, norm_gain=norm_gain, router_weight=router_weight, up_weight=up_weight, down_weight=down_weight, expert_ids=expert_ids, cotangent=cotangent)


EPS = 1e-06

def norm_rows(rows, gain):
    scale = lax.rsqrt(lax.optimization_barrier(jnp.mean(rows * rows, axis=-1, keepdims=True)) + EPS)
    return rows * scale * gain

def gelu_tanh(values):
    return jax.nn.gelu(values, approximate=True)

def reference(tokens, norm_gain, router_weight, up_weight, down_weight, expert_ids, cotangent):
    ntokens, features = tokens.shape
    experts = router_weight.shape[1]
    half_width = up_weight.shape[2]
    devices = N_EP * N_FSDP
    x_float = tokens.astype(jnp.float32)
    normed_float, norm_back = jax.vjp(norm_rows, x_float, norm_gain.astype(jnp.float32))
    normed = normed_float.astype(jnp.bfloat16)
    logits = jnp.dot(normed, router_weight, preferred_element_type=jnp.float32)
    expert_iota = jnp.arange(experts, dtype=jnp.int32)
    chosen_mask = (expert_ids[:, :, None] == expert_iota[None, None, :]).astype(jnp.float32)
    gates = jax.nn.sigmoid(lax.optimization_barrier(jnp.sum(chosen_mask * logits[:, None, :], axis=-1)))
    flat_mask = chosen_mask.reshape(devices, TOK_DEV * 2, experts)
    running = jnp.cumsum(flat_mask, axis=1)
    slot_of = lax.optimization_barrier(jnp.sum(flat_mask * (running - 1.0), axis=-1)).reshape(-1).astype(jnp.int32)
    assign_iota = jnp.arange(ntokens * 2, dtype=jnp.int32)
    device_of = (assign_iota // (TOK_DEV * 2)).astype(jnp.int32)
    position = (device_of * CAP + slot_of).astype(jnp.int32)
    expert_of = expert_ids.reshape(-1).astype(jnp.int32)
    slot_table = jnp.full((experts, devices * CAP), ntokens * 2, jnp.int32)
    slot_table = slot_table.at[expert_of, position].set(assign_iota)
    cot_float = cotangent.astype(jnp.float32)
    gated_cot = (gates[:, :, None] * cot_float[:, None, :]).reshape(ntokens * 2, features).astype(jnp.bfloat16)
    zero_row = jnp.zeros((1, features), jnp.bfloat16)
    normed_pad = jnp.concatenate([jnp.repeat(normed, 2, axis=0), zero_row], axis=0)
    cot_pad = jnp.concatenate([gated_cot, zero_row], axis=0)
    up_pairs = up_weight.reshape(experts, 2, features, half_width)
    down_full = down_weight.reshape(experts, 2 * half_width, features)

    def expert_pass(packed):
        index_row, up_pair, down_block = packed
        up_block = jnp.concatenate([up_pair[0], up_pair[1]], axis=1)
        row_block = normed_pad[index_row]
        pre_act = jnp.dot(row_block, up_block, preferred_element_type=jnp.float32)
        hidden_f, gelu_back = jax.vjp(gelu_tanh, pre_act)
        hidden_b = hidden_f.astype(jnp.bfloat16)
        out_first = jnp.dot(hidden_b[:, :half_width], down_block[:half_width], preferred_element_type=jnp.float32).astype(jnp.bfloat16)
        out_second = jnp.dot(hidden_b[:, half_width:], down_block[half_width:], preferred_element_type=jnp.float32).astype(jnp.bfloat16)
        result = (out_first.astype(jnp.float32) + out_second.astype(jnp.float32)).astype(jnp.bfloat16)
        cot_rows = cot_pad[index_row]
        grad_act = jnp.einsum('rd,hd->rh', cot_rows, down_block, preferred_element_type=jnp.float32)
        grad_pre = gelu_back(grad_act)[0].astype(jnp.bfloat16)
        grad_first = jnp.einsum('rh,dh->rd', grad_pre[:, :half_width], up_pair[0], preferred_element_type=jnp.float32).astype(jnp.bfloat16)
        grad_second = jnp.einsum('rh,dh->rd', grad_pre[:, half_width:], up_pair[1], preferred_element_type=jnp.float32).astype(jnp.bfloat16)
        grad_in = (grad_first.astype(jnp.float32) + grad_second.astype(jnp.float32)).astype(jnp.bfloat16)
        return (result, grad_in)
    expert_outs, expert_grads = lax.map(expert_pass, (slot_table, up_pairs, down_full))
    expert_out = expert_outs[expert_of, position].astype(jnp.float32).reshape(ntokens, 2, features)
    grad_rows = expert_grads[expert_of, position].astype(jnp.float32).reshape(ntokens, 2, features)
    mixed = (x_float + lax.optimization_barrier(jnp.sum(gates[:, :, None] * expert_out, axis=1))).astype(jnp.bfloat16)
    grad_gate = lax.optimization_barrier(jnp.sum(cot_float[:, None, :] * expert_out, axis=-1))
    grad_choice = grad_gate * gates * (1.0 - gates)
    grad_logits = lax.optimization_barrier(jnp.sum(chosen_mask * grad_choice[:, :, None], axis=1))
    grad_normed = lax.optimization_barrier(jnp.sum(grad_rows, axis=1)) + jnp.dot(grad_logits, router_weight.astype(jnp.float32).T, precision=lax.Precision.HIGHEST)
    grad_x_float, grad_gain_sum = norm_back(grad_normed)
    grad_tokens = (cot_float + grad_x_float).astype(jnp.bfloat16)
    scale = 1.0 / jnp.sqrt(jnp.float32(ntokens))
    grad_router = jnp.dot(normed.astype(jnp.float32).T, grad_logits, precision=lax.Precision.HIGHEST) * scale
    grad_gain = grad_gain_sum * scale
    return (mixed, grad_tokens, grad_router, grad_gain)
```

```python
import math

import jax
import jax.numpy as jnp
import numpy as np
from jax import lax
from jax.experimental import pallas as pl
from jax.experimental.pallas import tpu as pltpu
from jax.sharding import Mesh
from jax.sharding import PartitionSpec as P

EPS = 1e-06
CAP = 6
PARTS = 4
TILE = 8
BANDS = CAP * PARTS // TILE
GROUP = 8
BF16 = jnp.bfloat16
F32 = jnp.float32
VMEM_LIMIT = 56 * 1024 * 1024
CHIPS = ("ep", "pair")
FSDP = ("pair", "core")
EVERY = ("ep", "pair", "core")


def params(steps):
    return pltpu.CompilerParams(
        dimension_semantics=("arbitrary",) * steps, vmem_limit_bytes=VMEM_LIMIT
    )


def cost(flops, bytes_accessed):
    return pl.CostEstimate(flops=flops, bytes_accessed=bytes_accessed, transcendentals=0)


def iota(shape, dim):
    return lax.broadcasted_iota(jnp.int32, shape, dim)


def dot(a, b):
    return jnp.dot(a, b, preferred_element_type=F32)


def dot_nt(a, b):
    return lax.dot_general(a, b, (((1,), (1,)), ((), ())), preferred_element_type=F32)


def as_bf16(mask):
    return mask.astype(F32).astype(BF16)


def shuffle_matrix():
    size = CAP * PARTS * GROUP
    matrix = np.zeros((size, size), np.float32)
    for message in range(GROUP):
        for number in range(CAP * PARTS):
            piece, slot = divmod(number, CAP)
            band, row = divmod(number, TILE)
            matrix[
                piece * GROUP * CAP + message * CAP + slot,
                band * GROUP * TILE + message * TILE + row,
            ] = 1.0
    return matrix


def slot_target(band, column):
    row = column & (TILE - 1)
    limit = CAP - 2 * band
    low = row < limit
    slot = 2 * band + row - jnp.where(low, 0, CAP)
    return (column >> 3) * CAP + slot, low


def pack_kernel(ids_ref, low_ref, high_ref, out_ref, pos_ref):
    band = pl.program_id(0)
    toks = ids_ref.shape[1]
    experts = out_ref.shape[0] // TILE

    @pl.when(band == 0)
    def _():
        first, second = ids_ref[0:1, :], ids_ref[1:2, :]
        expert = iota((experts, toks), 0)
        in_first, in_second = expert == first, expert == second
        both = as_bf16(in_first | in_second)
        earlier = as_bf16(iota((toks, toks), 0) < iota((toks, toks), 1))
        count = dot(both, earlier)
        slot_first = jnp.sum(jnp.where(in_first, count, 0.0), axis=0, keepdims=True)
        slot_second = jnp.sum(jnp.where(in_second, count, 0.0), axis=0, keepdims=True)
        pos_ref[0:1, :] = first * CAP + slot_first.astype(jnp.int32)
        pos_ref[1:2, :] = second * CAP + slot_second.astype(jnp.int32)

    target, low = slot_target(band, iota((out_ref.shape[0], toks), 0))
    hit = (target == pos_ref[0:1, :]) | (target == pos_ref[1:2, :])
    placing = jnp.concatenate([as_bf16(hit & low), as_bf16(hit & ~low)], axis=1)
    pieces = jnp.concatenate([low_ref[...], high_ref[...]], axis=0)
    out_ref[...] = dot(placing, pieces).astype(BF16)


def pack(ids_t, rows, experts):
    toks, features = rows.shape
    piece = features // PARTS
    out_rows = experts * TILE
    return pl.pallas_call(
        pack_kernel,
        grid=(BANDS,),
        in_specs=[
            pl.BlockSpec((2, toks), lambda b: (0, 0)),
            pl.BlockSpec((toks, piece), lambda b: (0, b)),
            pl.BlockSpec((toks, piece), lambda b: (0, b + 1)),
        ],
        out_specs=pl.BlockSpec((out_rows, piece), lambda b: (0, b)),
        out_shape=jax.ShapeDtypeStruct((out_rows, BANDS * piece), BF16),
        scratch_shapes=[pltpu.VMEM((8, toks), jnp.int32)],
        compiler_params=params(1),
        cost_estimate=cost(2 * BANDS * out_rows * 2 * toks * piece, 2 * out_rows * BANDS * piece),
        name="pack",
    )(ids_t, rows, rows)


def fill_choosing(ids_ref, choose_ref):
    toks = ids_ref.shape[0]
    columns = choose_ref.shape[2]
    experts = columns // TILE
    first, second = ids_ref[:, 0:1], ids_ref[:, 1:2]
    expert = iota((toks, experts), 1)
    in_first, in_second = expert == first, expert == second
    both = as_bf16(in_first | in_second)
    earlier = as_bf16(iota((toks, toks), 1) < iota((toks, toks), 0))
    count = dot(earlier, both)
    pos_first = first * CAP + jnp.sum(
        jnp.where(in_first, count, 0.0), axis=1, keepdims=True
    ).astype(jnp.int32)
    pos_second = second * CAP + jnp.sum(
        jnp.where(in_second, count, 0.0), axis=1, keepdims=True
    ).astype(jnp.int32)
    for band in range(BANDS):
        target, low = slot_target(band, iota((toks, columns), 1))
        hit = (target == pos_first) | (target == pos_second)
        choose_ref[band, :toks, :] = as_bf16(hit & low)
        choose_ref[band, toks:, :] = as_bf16(hit & ~low)


def summed_pieces(choose_ref, band_refs):
    toks = choose_ref.shape[1] // 2
    sums = [dot(choose_ref[band], band_refs[band][...]) for band in range(BANDS)]
    pieces = [sums[0][:toks]]
    for band in range(1, BANDS):
        pieces.append(sums[band - 1][toks:] + sums[band][:toks])
    pieces.append(sums[BANDS - 1][toks:])
    return pieces


def mixed_kernel(ids_ref, tokens_ref, band0, band1, band2, out_ref, choose_ref):
    step = pl.program_id(0)
    width = band0.shape[1]
    piece = tokens_ref.shape[1] // PARTS

    @pl.when(step == 0)
    def _():
        fill_choosing(ids_ref, choose_ref)

    for number, value in enumerate(summed_pieces(choose_ref, (band0, band1, band2))):
        cols = pl.ds(pl.multiple_of(number * piece + step * width, width), width)
        out_ref[:, cols] = (tokens_ref[:, cols].astype(F32) + value).astype(BF16)


def grad_tokens_kernel(
    ids_ref, tokens_ref, cot_ref, band0, band1, band2, out_ref, choose_ref, grad_ref, square_ref, cross_ref
):
    step = pl.program_id(0)
    width = band0.shape[1]
    features = tokens_ref.shape[1]
    piece = features // PARTS

    @pl.when(step == 0)
    def _():
        fill_choosing(ids_ref, choose_ref)
        square_ref[...] = jnp.zeros_like(square_ref)
        cross_ref[...] = jnp.zeros_like(cross_ref)

    for number, value in enumerate(summed_pieces(choose_ref, (band0, band1, band2))):
        cols = pl.ds(pl.multiple_of(number * piece + step * width, width), width)
        x = tokens_ref[:, cols].astype(F32)
        grad_ref[:, cols] = value
        square_ref[...] += x * x
        cross_ref[...] += x * value

    @pl.when(step == pl.num_programs(0) - 1)
    def _():
        scale = lax.rsqrt(jnp.sum(square_ref[...], axis=1, keepdims=True) / features + EPS)
        back = jnp.sum(cross_ref[...], axis=1, keepdims=True) / features * scale * scale * scale
        for at in range(0, features, width):
            cols = slice(at, at + width)
            x = tokens_ref[:, cols].astype(F32)
            grad = scale * grad_ref[:, cols] - x * back
            out_ref[:, cols] = (cot_ref[:, cols].astype(F32) + grad).astype(BF16)


def token_side(kernel, ids, row_inputs, bands, scratch, name):
    toks, features = row_inputs[0].shape
    piece = features // PARTS
    width = 256
    steps = piece // width
    columns = bands.shape[0]

    def band_spec(band):
        return pl.BlockSpec((columns, width), lambda c, band=band: (0, band * steps + c))

    return pl.pallas_call(
        kernel,
        grid=(steps,),
        in_specs=[pl.BlockSpec((toks, 2), lambda c: (0, 0))]
        + [pl.BlockSpec((toks, features), lambda c: (0, 0))] * len(row_inputs)
        + [band_spec(band) for band in range(BANDS)],
        out_specs=pl.BlockSpec((toks, features), lambda c: (0, 0)),
        out_shape=jax.ShapeDtypeStruct((toks, features), BF16),
        scratch_shapes=[pltpu.VMEM((BANDS, 2 * toks, columns), BF16)] + scratch,
        compiler_params=params(1),
        cost_estimate=cost(2 * BANDS * 2 * toks * columns * piece, 2 * columns * BANDS * piece),
        name=name,
    )(ids, *row_inputs, *([bands] * BANDS))


def unpacked(block, shuffle):
    piece = block.shape[1] // BANDS
    stacked = jnp.concatenate([block[:, b * piece : (b + 1) * piece] for b in range(BANDS)], axis=0)
    rows = dot(shuffle, stacked)
    count = GROUP * CAP
    return [rows[q * count : (q + 1) * count] for q in range(PARTS)]


def store_packed(out_ref, pieces, shuffle_back):
    piece = pieces[0].shape[1]
    bands = dot(shuffle_back, jnp.concatenate(pieces, axis=0)).astype(BF16)
    count = GROUP * TILE
    for b in range(BANDS):
        out_ref[:, b * piece : (b + 1) * piece] = bands[b * count : (b + 1) * count]


def spread(column, ref):
    ref[...] = jnp.broadcast_to(column, ref.shape)


def row_fold(value):
    total = value[0:8]
    for at in range(8, value.shape[0], 8):
        total = total + value[at : at + 8]
    return total


def norm_kernel(block_ref, shuffle_ref, gain_ref, column_ref, normed_ref, unit_ref, gate_ref):
    pieces = unpacked(block_ref[...], shuffle_ref[...])
    piece = pieces[0].shape[1]
    square = sum(jnp.sum(x * x, axis=1, keepdims=True) for x in pieces)
    scale = lax.rsqrt(square / (piece * PARTS) + EPS)
    logit = 0.0
    for q, x in enumerate(pieces):
        cols = slice(q * piece, (q + 1) * piece)
        unit = x * scale
        normed = (unit * gain_ref[:, cols]).astype(BF16)
        unit_ref[:, cols] = unit.astype(BF16)
        normed_ref[:, cols] = normed
        logit = logit + jnp.sum(normed.astype(F32) * column_ref[:, cols], axis=1, keepdims=True)
    spread(jax.nn.sigmoid(logit), gate_ref)


def out_kernel(own_ref, other_ref, gate_ref, back_ref, result_ref, send_ref):
    gate = gate_ref[:, 0:1]
    piece = own_ref.shape[1] // PARTS
    gated = []
    for q in range(PARTS):
        cols = slice(q * piece, (q + 1) * piece)
        result = (own_ref[:, cols].astype(F32) + other_ref[:, cols].astype(F32)).astype(BF16)
        result_ref[:, cols] = result
        gated.append((gate * result.astype(F32)).astype(BF16))
    store_packed(send_ref, gated, back_ref[...])


def cot_kernel(block_ref, shuffle_ref, gate_ref, result_ref, normed_ref, gated_ref, choice_ref, router_ref):
    pieces = unpacked(block_ref[...], shuffle_ref[...])
    piece = pieces[0].shape[1]
    gate = gate_ref[:, 0:1]
    total = 0.0
    for q, cot in enumerate(pieces):
        cols = slice(q * piece, (q + 1) * piece)
        gated_ref[:, cols] = (gate * cot).astype(BF16)
        total = total + jnp.sum(cot * result_ref[:, cols].astype(F32), axis=1, keepdims=True)
    choice = total * gate * (1.0 - gate)
    spread(choice, choice_ref)

    @pl.when(pl.program_id(0) == 0)
    def _():
        router_ref[...] = jnp.zeros_like(router_ref)

    for q in range(PARTS):
        cols = slice(q * piece, (q + 1) * piece)
        router_ref[:, cols] += row_fold(normed_ref[:, cols].astype(F32) * choice)


def grad_kernel(
    own_ref, other_ref, choice_ref, unit_ref, column_ref, gain_ref, back_ref, send_ref, gain_sum_ref
):
    choice = choice_ref[:, 0:1]
    piece = own_ref.shape[1] // PARTS

    @pl.when(pl.program_id(0) == 0)
    def _():
        gain_sum_ref[...] = jnp.zeros_like(gain_sum_ref)

    scaled = []
    for q in range(PARTS):
        cols = slice(q * piece, (q + 1) * piece)
        rows = (own_ref[:, cols].astype(F32) + other_ref[:, cols].astype(F32)).astype(BF16)
        grad = rows.astype(F32) + choice * column_ref[:, cols]
        gain_sum_ref[:, cols] += row_fold(grad * unit_ref[:, cols].astype(F32))
        scaled.append((grad * gain_ref[:, cols]).astype(BF16))
    store_packed(send_ref, scaled, back_ref[...])


def by_group(kernel, inputs, outputs, flops, name):
    groups = None
    for value, rows in inputs:
        if rows:
            groups = value.shape[0] // rows

    def spec(shape, rows):
        if rows:
            return pl.BlockSpec((rows, shape[1]), lambda g: (g, 0))
        return pl.BlockSpec(shape, lambda g: (0, 0))

    moved = sum(value.size * value.dtype.itemsize for value, _ in inputs)
    moved += sum(math.prod(shape) * dtype.itemsize for shape, dtype, _ in outputs)
    return pl.pallas_call(
        kernel,
        grid=(groups,),
        in_specs=[spec(value.shape, rows) for value, rows in inputs],
        out_specs=[spec(shape, rows) for shape, _, rows in outputs],
        out_shape=[jax.ShapeDtypeStruct(shape, dtype) for shape, dtype, _ in outputs],
        compiler_params=params(1),
        cost_estimate=cost(flops, moved),
        name=name,
    )(*[value for value, _ in inputs])


def forward_kernel(x_ref, up_ref, down_ref, out_ref, slope_ref, acc_ref, hidden_ref):
    step = pl.program_id(0)
    half = pl.num_programs(0) // 2

    @pl.when(step == 0)
    def _():
        acc_ref[...] = dot(x_ref[...], up_ref[...])

    @pl.when((step > 0) & (step < half))
    def _():
        acc_ref[...] += dot(x_ref[...], up_ref[...])

    @pl.when(step == half - 1)
    def _():
        pre = acc_ref[...]
        root = math.sqrt(2.0 / math.pi)
        square = pre * pre
        bend = jnp.tanh(root * (pre + 0.044715 * (square * pre)))
        share = 0.5 * (1.0 + bend)
        hidden_ref[...] = (pre * share).astype(BF16)
        inner = root * (1.0 + (3.0 * 0.044715) * square)
        slope_ref[...] = share + 0.5 * pre * (1.0 - bend * bend) * inner

    @pl.when(step >= half)
    def _():
        out_ref[...] = dot(hidden_ref[...], down_ref[...]).astype(BF16)


def backward_kernel(cot_ref, down_ref, up_ref, slope_ref, out_ref, acc_ref, grad_ref):
    step = pl.program_id(0)
    half = pl.num_programs(0) // 2

    @pl.when(step == 0)
    def _():
        acc_ref[...] = dot_nt(cot_ref[...], down_ref[...])

    @pl.when((step > 0) & (step < half))
    def _():
        acc_ref[...] += dot_nt(cot_ref[...], down_ref[...])

    @pl.when(step == half - 1)
    def _():
        grad_ref[...] = (acc_ref[...] * slope_ref[...]).astype(BF16)

    @pl.when(step >= half)
    def _():
        out_ref[...] = dot_nt(grad_ref[...], up_ref[...]).astype(BF16)


def expert_call(kernel, rows, up, down, slope, name):
    count, features = rows.shape
    hidden = up.shape[2]
    block = features // PARTS
    half = features // block

    def first(i):
        return jnp.minimum(i, half - 1)

    def second(i):
        return jnp.maximum(i - half, 0)

    rows_spec = pl.BlockSpec((count, block), lambda i: (0, first(i)))
    slope_spec = pl.BlockSpec((count, hidden), lambda i: (0, 0))
    out_spec = pl.BlockSpec((count, block), lambda i: (0, second(i)))
    out_shape = jax.ShapeDtypeStruct((count, features), BF16)
    forward = slope is None
    early, late = (first, second) if forward else (second, first)
    up_spec = pl.BlockSpec((None, block, hidden), lambda i: (0, early(i), 0))
    down_spec = pl.BlockSpec((None, hidden, block), lambda i: (0, 0, late(i)))
    if forward:
        args, in_specs = (rows, up, down), [rows_spec, up_spec, down_spec]
        out_specs = [out_spec, slope_spec]
        out_shape = [out_shape, jax.ShapeDtypeStruct((count, hidden), F32)]
    else:
        args, in_specs = (rows, down, up, slope), [rows_spec, down_spec, up_spec, slope_spec]
        out_specs = out_spec
    return pl.pallas_call(
        kernel,
        grid=(2 * half,),
        in_specs=in_specs,
        out_specs=out_specs,
        out_shape=out_shape,
        scratch_shapes=[pltpu.VMEM((count, hidden), F32), pltpu.VMEM((count, hidden), BF16)],
        compiler_params=params(1),
        cost_estimate=cost(4 * count * features * hidden, 4 * features * (count + hidden)),
        name=name,
    )(*args)


def exchange(messages):
    blocks = messages.reshape(-1, TILE, messages.shape[1])
    blocks = lax.all_to_all(blocks, CHIPS, split_axis=0, concat_axis=0, tiled=True)
    return blocks.reshape(messages.shape)


def swap(value):
    return lax.ppermute(value, "core", [(0, 1), (1, 0)])


def body(tokens, norm_gain, router_weight, up_weight, down_weight, expert_ids, cotangent):
    toks, features = tokens.shape
    eps, pairs, cores = (lax.axis_size(name) for name in EVERY)
    experts = eps * pairs
    shard = features // (pairs * cores)
    rows = experts * CAP
    devices = experts * cores

    columns = lax.dynamic_slice_in_dim(router_weight, lax.axis_index("ep") * pairs, pairs, 1).T
    parcel = jnp.stack([jnp.broadcast_to(norm_gain, columns.shape), columns], axis=1)
    parcel = jnp.broadcast_to(parcel[:, None], (pairs, cores, 2, shard)).reshape(-1, 2, shard)
    parcel = lax.all_to_all(parcel, FSDP, split_axis=0, concat_axis=0, tiled=True)
    gain = parcel[:, 0].reshape(1, features).astype(F32)
    column = parcel[:, 1].reshape(1, features).astype(F32)

    matrix = shuffle_matrix()
    shuffle, shuffle_back = jnp.asarray(matrix, BF16), jnp.asarray(matrix.T, BF16)
    ids_t = expert_ids.T
    group_rows, group_tiles = GROUP * CAP, GROUP * TILE
    row_shape, send_shape = (rows, features), (experts * TILE, features * CAP // TILE)
    wide, narrow = (rows, 128), (8, features)
    shuffling = 2 * rows * features * CAP * PARTS * GROUP // PARTS
    b16, f32 = jnp.dtype(BF16), jnp.dtype(F32)

    arrived = exchange(pack(ids_t, tokens, experts))
    cot_sent = pack(ids_t, cotangent, experts)
    normed, unit, gate = by_group(
        norm_kernel,
        [(arrived, group_tiles), (shuffle, 0), (gain, 0), (column, 0)],
        [(row_shape, b16, group_rows), (row_shape, b16, group_rows), (wide, f32, group_rows)],
        shuffling,
        "norm",
    )
    cot_arrived = exchange(cot_sent)
    normed_other = swap(normed)
    own_part, own_slope = expert_call(forward_kernel, normed, up_weight, down_weight, None, "forward")
    other_part, other_slope = expert_call(
        forward_kernel, normed_other, up_weight, down_weight, None, "forward"
    )
    result, result_sent = by_group(
        out_kernel,
        [(own_part, group_rows), (swap(other_part), group_rows), (gate, group_rows), (shuffle_back, 0)],
        [(row_shape, b16, group_rows), (send_shape, b16, group_tiles)],
        shuffling,
        "out",
    )
    gated, choice, router_sum = by_group(
        cot_kernel,
        [
            (cot_arrived, group_tiles),
            (shuffle, 0),
            (gate, group_rows),
            (result, group_rows),
            (normed, group_rows),
        ],
        [(row_shape, b16, group_rows), (wide, f32, group_rows), (narrow, f32, 0)],
        shuffling,
        "cot",
    )
    result_back = exchange(result_sent)
    gated_other = swap(gated)
    own_grad = expert_call(backward_kernel, gated, up_weight, down_weight, own_slope, "backward")
    other_grad = expert_call(
        backward_kernel, gated_other, up_weight, down_weight, other_slope, "backward"
    )
    grad_sent, gain_sum = by_group(
        grad_kernel,
        [
            (own_grad, group_rows),
            (swap(other_grad), group_rows),
            (choice, group_rows),
            (unit, group_rows),
            (column, 0),
            (gain, 0),
            (shuffle_back, 0),
        ],
        [(send_shape, b16, group_tiles), (narrow, f32, 0)],
        shuffling,
        "grad",
    )
    grad_back = exchange(grad_sent)
    mixed = token_side(mixed_kernel, expert_ids, [tokens], result_back, [], "mixed")
    grad_tokens = token_side(
        grad_tokens_kernel,
        expert_ids,
        [tokens, cotangent],
        grad_back,
        [
            pltpu.VMEM((toks, features), F32),
            pltpu.VMEM((toks, 256), F32),
            pltpu.VMEM((toks, 256), F32),
        ],
        "grad_tokens",
    )

    sums = jnp.stack([jnp.sum(router_sum, axis=0), jnp.sum(gain_sum, axis=0)])
    sums = sums.reshape(2, pairs * cores, shard).transpose(1, 0, 2).reshape(1, pairs * cores, 2 * shard)
    sums = jnp.broadcast_to(sums, (eps, pairs * cores, 2 * shard)).reshape(devices, 2 * shard)
    sums = lax.all_to_all(sums, EVERY, split_axis=0, concat_axis=0, tiled=True)
    scale = 1.0 / math.sqrt(toks * devices)
    grad_router = jnp.sum(sums[:, :shard].reshape(experts, cores, shard), axis=1).T * scale
    grad_gain = jnp.sum(sums[:, shard:], axis=0) * scale
    return mixed, grad_tokens, grad_router, grad_gain


def solution(mesh):
    eps, fsdp = mesh.devices.shape
    fine = Mesh(mesh.devices.reshape(eps, fsdp // 2, 2), EVERY)
    in_specs = (
        P(EVERY, None),
        P(FSDP),
        P(FSDP, None),
        P(EVERY, None, None),
        P(EVERY, None, None),
        P(EVERY, None),
        P(EVERY, None),
    )
    out_specs = (P(EVERY, None), P(EVERY, None), P(FSDP, None), P(FSDP))
    return jax.shard_map(body, mesh=fine, in_specs=in_specs, out_specs=out_specs, check_vma=False)
```

```python
import functools
import math

import jax
import jax.numpy as jnp
import numpy as np
from jax import lax
from jax.experimental import pallas as pl
from jax.experimental.pallas import tpu as pltpu
from jax.sharding import Mesh
from jax.sharding import PartitionSpec as P

EPS = 1e-06
CAP = 6
PARTS = 4
TILE = 8
BANDS = CAP * PARTS // TILE
GROUP = 8
BF16 = jnp.bfloat16
F32 = jnp.float32
LOUD = 64
META = 128
SUB = 2
VMEM_LIMIT = 56 * 1024 * 1024
CHIPS = ("ep", "pair")
FSDP = ("pair", "core")
EVERY = ("ep", "pair", "core")


def params(steps):
    return pltpu.CompilerParams(
        dimension_semantics=("arbitrary",) * steps, vmem_limit_bytes=VMEM_LIMIT
    )


def cost(flops, bytes_accessed):
    return pl.CostEstimate(flops=flops, bytes_accessed=bytes_accessed, transcendentals=0)


def iota(shape, dim):
    return lax.broadcasted_iota(jnp.int32, shape, dim)


def dot(a, b):
    return jnp.dot(a, b, preferred_element_type=F32)


def dot_nt(a, b):
    return lax.dot_general(a, b, (((1,), (1,)), ((), ())), preferred_element_type=F32)


def as_bf16(mask):
    return mask.astype(F32).astype(BF16)


def shuffle_matrix():
    size = CAP * PARTS * GROUP
    matrix = np.zeros((size, size), np.float32)
    for message in range(GROUP):
        for number in range(CAP * PARTS):
            piece, slot = divmod(number, CAP)
            band, row = divmod(number, TILE)
            matrix[
                piece * GROUP * CAP + message * CAP + slot,
                band * GROUP * TILE + message * TILE + row,
            ] = 1.0
    return matrix


def slot_target(band, column):
    row = column & (TILE - 1)
    limit = CAP - 2 * band
    low = row < limit
    slot = 2 * band + row - jnp.where(low, 0, CAP)
    return (column >> 3) * CAP + slot, low


def pack_kernel(experts, ids_ref, rows_ref, *refs):
    *meta_refs, out_ref, pos_ref = refs
    step = pl.program_id(0)
    toks, features = rows_ref.shape
    count = out_ref.shape[0]
    piece = features // PARTS

    @pl.when(step == 0)
    def _():
        first, second = ids_ref[0:1, :], ids_ref[1:2, :]
        expert = iota((experts, toks), 0)
        in_first, in_second = expert == first, expert == second
        both = as_bf16(in_first | in_second)
        earlier = as_bf16(iota((toks, toks), 0) < iota((toks, toks), 1))
        earlier_count = dot(both, earlier)
        slot_first = jnp.sum(jnp.where(in_first, earlier_count, 0.0), axis=0, keepdims=True)
        slot_second = jnp.sum(jnp.where(in_second, earlier_count, 0.0), axis=0, keepdims=True)
        pos_ref[0:1, :] = first * CAP + slot_first.astype(jnp.int32)
        pos_ref[1:2, :] = second * CAP + slot_second.astype(jnp.int32)

    row = step * count + iota((count, toks), 0)
    for band in range(BANDS):
        target, low = slot_target(band, row)
        hit = (target == pos_ref[0:1, :]) | (target == pos_ref[1:2, :])
        placing = jnp.concatenate([as_bf16(hit & low), as_bf16(hit & ~low)], axis=1)
        pieces = [rows_ref[:, p * piece : (p + 1) * piece] for p in (band, band + 1)]
        out_ref[:, band * piece : (band + 1) * piece] = dot(
            placing, jnp.concatenate(pieces, axis=0)
        ).astype(BF16)

    if meta_refs:
        gain_ref, router_ref, core_ref = meta_refs
        shard = router_ref.shape[0]
        shift = core_ref[0, 0] * (META // 2)
        shifted = as_bf16(iota((shard, 3 * META), 1) == iota((shard, 3 * META), 0) + shift)
        gain = dot(gain_ref[...], shifted)
        columns = lax.dot_general(
            router_ref[...], shifted, (((0,), (0,)), ((), ())), preferred_element_type=F32
        ).astype(BF16)
        tile_row = iota((count, META), 0) & (TILE - 1)
        pick_row = step * count + iota((count, experts), 0)
        pick_column = iota((count, experts), 1)
        total = jnp.zeros((count, META), F32)
        for r in range(3):
            lanes = slice(r * META, (r + 1) * META)
            total = jnp.where(tile_row == r, gain[0:1, lanes], total)
            total = total + dot(as_bf16(pick_row == pick_column * TILE + 3 + r), columns[:, lanes])
        out_ref[:, BANDS * piece :] = total.astype(BF16)


SMALL = pl.BlockSpec(memory_space=pltpu.SMEM)


def pack(ids_t, rows, experts, meta=()):
    toks, features = rows.shape
    width = features * CAP // TILE + (META if meta else 0)
    out_rows = experts * TILE
    steps = 4
    meta_specs = []
    if meta:
        meta_specs = [pl.BlockSpec(value.shape, lambda i: (0, 0)) for value in meta[:2]] + [SMALL]
    return pl.pallas_call(
        functools.partial(pack_kernel, experts),
        grid=(steps,),
        in_specs=[
            pl.BlockSpec((2, toks), lambda i: (0, 0)),
            pl.BlockSpec((toks, features), lambda i: (0, 0)),
            *meta_specs,
        ],
        out_specs=pl.BlockSpec((out_rows // steps, width), lambda i: (i, 0)),
        out_shape=jax.ShapeDtypeStruct((out_rows, width), BF16),
        scratch_shapes=[pltpu.VMEM((8, toks), jnp.int32)],
        compiler_params=params(1),
        cost_estimate=cost(2 * out_rows * 2 * toks * width, 2 * out_rows * width),
        name="pack",
    )(ids_t, rows, *meta)


def fill_choosing(ids_ref, choose_ref):
    toks = ids_ref.shape[0]
    columns = choose_ref.shape[2]
    experts = columns // TILE
    first, second = ids_ref[:, 0:1], ids_ref[:, 1:2]
    expert = iota((toks, experts), 1)
    in_first, in_second = expert == first, expert == second
    both = as_bf16(in_first | in_second)
    earlier = as_bf16(iota((toks, toks), 1) < iota((toks, toks), 0))
    count = dot(earlier, both)
    pos_first = first * CAP + jnp.sum(
        jnp.where(in_first, count, 0.0), axis=1, keepdims=True
    ).astype(jnp.int32)
    pos_second = second * CAP + jnp.sum(
        jnp.where(in_second, count, 0.0), axis=1, keepdims=True
    ).astype(jnp.int32)
    for band in range(BANDS):
        target, low = slot_target(band, iota((toks, columns), 1))
        hit = (target == pos_first) | (target == pos_second)
        choose_ref[band, :toks, :] = as_bf16(hit & low)
        choose_ref[band, toks:, :] = as_bf16(hit & ~low)


def summed_pieces(choose_ref, band_refs):
    toks = choose_ref.shape[1] // 2
    sums = [dot(choose_ref[band], band_refs[band][...]) for band in range(BANDS)]
    pieces = [sums[0][:toks]]
    for band in range(1, BANDS):
        pieces.append(sums[band - 1][toks:] + sums[band][:toks])
    pieces.append(sums[BANDS - 1][toks:])
    return pieces


def mixed_kernel(ids_ref, tokens_ref, band0, band1, band2, out_ref, choose_ref):
    step = pl.program_id(0)
    width = band0.shape[1]
    piece = tokens_ref.shape[1] // PARTS

    @pl.when(step == 0)
    def _():
        fill_choosing(ids_ref, choose_ref)

    for number, value in enumerate(summed_pieces(choose_ref, (band0, band1, band2))):
        cols = pl.ds(pl.multiple_of(number * piece + step * width, width), width)
        out_ref[:, cols] = (tokens_ref[:, cols].astype(F32) + value).astype(BF16)


def grad_tokens_kernel(
    ids_ref, tokens_ref, cot_ref, band0, band1, band2, out_ref, choose_ref, grad_ref, square_ref, cross_ref
):
    step = pl.program_id(0)
    width = band0.shape[1]
    features = tokens_ref.shape[1]
    piece = features // PARTS

    @pl.when(step == 0)
    def _():
        fill_choosing(ids_ref, choose_ref)
        square_ref[...] = jnp.zeros_like(square_ref)
        cross_ref[...] = jnp.zeros_like(cross_ref)

    for number, value in enumerate(summed_pieces(choose_ref, (band0, band1, band2))):
        cols = pl.ds(pl.multiple_of(number * piece + step * width, width), width)
        x = tokens_ref[:, cols].astype(F32)
        grad_ref[:, cols] = value
        square_ref[...] += x * x
        cross_ref[...] += x * value

    @pl.when(step == pl.num_programs(0) - 1)
    def _():
        scale = lax.rsqrt(jnp.sum(square_ref[...], axis=1, keepdims=True) / features + EPS)
        back = jnp.sum(cross_ref[...], axis=1, keepdims=True) / features * scale * scale * scale
        for at in range(0, features, width):
            cols = slice(at, at + width)
            x = tokens_ref[:, cols].astype(F32)
            grad = scale * grad_ref[:, cols] - x * back
            out_ref[:, cols] = (cot_ref[:, cols].astype(F32) + grad).astype(BF16)


def token_side(kernel, ids, row_inputs, bands, scratch, name):
    toks, features = row_inputs[0].shape
    piece = features // PARTS
    width = 256
    steps = piece // width
    columns = bands.shape[0]

    def band_spec(band):
        return pl.BlockSpec((columns, width), lambda c, band=band: (0, band * steps + c))

    return pl.pallas_call(
        kernel,
        grid=(steps,),
        in_specs=[pl.BlockSpec((toks, 2), lambda c: (0, 0))]
        + [pl.BlockSpec((toks, features), lambda c: (0, 0))] * len(row_inputs)
        + [band_spec(band) for band in range(BANDS)],
        out_specs=pl.BlockSpec((toks, features), lambda c: (0, 0)),
        out_shape=jax.ShapeDtypeStruct((toks, features), BF16),
        scratch_shapes=[pltpu.VMEM((BANDS, 2 * toks, columns), BF16)] + scratch,
        compiler_params=params(1),
        cost_estimate=cost(2 * BANDS * 2 * toks * columns * piece, 2 * columns * BANDS * piece),
        name=name,
    )(ids, *row_inputs, *([bands] * BANDS))


def sums_kernel(scale, meta_ref, core_ref, router_ref, own_ref, other_ref):
    messages = meta_ref[...]
    tiles = messages.shape[0]
    experts, shard = router_ref.shape
    lower = core_ref[0, 0] == 0
    rows = [
        dot(as_bf16(iota((experts, tiles), 1) == iota((experts, tiles), 0) * TILE + 5 + r), messages)
        for r in range(3)
    ]
    router = jnp.concatenate(rows, axis=1) * scale
    router_ref[...] = jnp.where(lower, router[:, :shard], router[:, META // 2 : META // 2 + shard])
    total = dot(as_bf16((iota((TILE, tiles), 1) & (TILE - 1)) == iota((TILE, tiles), 0)), messages)
    total = jnp.concatenate([total[r : r + 1] for r in range(5)], axis=1) * scale
    first, second = total[:, :shard], total[:, shard : 2 * shard]
    own_ref[...] = jnp.where(lower, first, second)
    other_ref[...] = jnp.where(lower, second, first)


def summed(messages, core, shard, scale):
    tiles, width = messages.shape
    row = jax.ShapeDtypeStruct((1, shard), F32)
    return pl.pallas_call(
        functools.partial(sums_kernel, scale),
        grid=(1,),
        in_specs=[pl.BlockSpec((tiles, META), lambda i: (0, width // META - 1)), SMALL],
        out_specs=[
            pl.BlockSpec((tiles // TILE, shard), lambda i: (0, 0)),
            pl.BlockSpec((1, shard), lambda i: (0, 0)),
            pl.BlockSpec((1, shard), lambda i: (0, 0)),
        ],
        out_shape=[jax.ShapeDtypeStruct((tiles // TILE, shard), F32), row, row],
        compiler_params=params(1),
        cost_estimate=cost(10**6, 2 * tiles * META),
        name="sums",
    )(messages, core)


def unpacked(block, shuffle, width):
    piece = width // BANDS
    stacked = jnp.concatenate([block[:, b * piece : (b + 1) * piece] for b in range(BANDS)], axis=0)
    rows = dot(shuffle, stacked)
    count = GROUP * CAP
    return [rows[q * count : (q + 1) * count] for q in range(PARTS)]


def spread(column, ref, rows):
    ref[rows] = jnp.broadcast_to(column, (GROUP * CAP, ref.shape[1]))


def row_fold(value):
    total = value[0:8]
    for at in range(8, value.shape[0], 8):
        total = total + value[at : at + 8]
    return total


def group_slices():
    for sub in range(SUB):
        yield (
            slice(sub * GROUP * TILE, (sub + 1) * GROUP * TILE),
            slice(sub * GROUP * CAP, (sub + 1) * GROUP * CAP),
        )


def norm_kernel(
    own_ref, other_ref, own_meta, other_meta, core_ref, shuffle_ref,
    own_normed, other_normed, own_gate, other_gate, gain_ref, column_ref,
):
    features = own_normed.shape[1]
    width = own_ref.shape[1] - META
    piece = features // PARTS

    @pl.when(pl.program_id(0) == 0)
    def _():
        own, other = own_meta[...].astype(F32), other_meta[...].astype(F32)
        lower = core_ref[0, 0] == 0
        first, second = jnp.where(lower, own, other), jnp.where(lower, other, own)
        for part, ref in ((0, gain_ref), (3, column_ref)):
            for pair in range(features // (5 * META)):
                at = pair * TILE + part
                rows = [first[at + r : at + r + 1] for r in range(3)]
                rows += [second[at + r : at + r + 1] for r in range(3)]
                rows = [rows[0], rows[1], rows[2] + rows[3], rows[4], rows[5]]
                ref[:, pair * 5 * META : (pair + 1) * 5 * META] = jnp.concatenate(rows, axis=1)

    for block_ref, normed_ref, gate_ref in (
        (own_ref, own_normed, own_gate),
        (other_ref, other_normed, other_gate),
    ):
        for tiles, rows in group_slices():
            pieces = unpacked(block_ref[tiles, :width], shuffle_ref[...], width)
            square = sum(jnp.sum(x * x, axis=1, keepdims=True) for x in pieces)
            scale = lax.rsqrt(square / features + EPS)
            logit = 0.0
            for q, x in enumerate(pieces):
                cols = slice(q * piece, (q + 1) * piece)
                normed = (x * scale * gain_ref[:, cols]).astype(BF16)
                normed_ref[rows, cols] = normed
                logit = logit + jnp.sum(
                    normed.astype(F32) * column_ref[:, cols], axis=1, keepdims=True
                )
            spread(jax.nn.sigmoid(logit), gate_ref, rows)


def out_kernel(own_ref, other_ref, gate_ref, back_ref, result_ref, send_ref):
    piece = own_ref.shape[1] // PARTS
    for tiles, rows in group_slices():
        gate = gate_ref[rows, 0:1]
        gated = []
        for q in range(PARTS):
            cols = slice(q * piece, (q + 1) * piece)
            result = (own_ref[rows, cols].astype(F32) + other_ref[rows, cols].astype(F32)).astype(BF16)
            result_ref[rows, cols] = result
            gated.append((gate * result.astype(F32)).astype(BF16))
        bands = dot(back_ref[...], jnp.concatenate(gated, axis=0)).astype(BF16)
        for b in range(BANDS):
            send_ref[tiles, b * piece : (b + 1) * piece] = bands[
                b * GROUP * TILE : (b + 1) * GROUP * TILE
            ]


def cot_kernel(
    own_ref, other_ref, own_gate, other_gate, result_ref, normed_ref, shuffle_ref,
    own_gated, other_gated, choice_ref, router_ref,
):
    width = own_ref.shape[1]
    piece = width // BANDS

    @pl.when(pl.program_id(0) == 0)
    def _():
        router_ref[...] = jnp.zeros_like(router_ref)

    for tiles, rows in group_slices():
        pieces = unpacked(other_ref[tiles], shuffle_ref[...], width)
        gate = other_gate[rows, 0:1]
        for q, cot in enumerate(pieces):
            other_gated[rows, q * piece : (q + 1) * piece] = (gate * cot).astype(BF16)
        pieces = unpacked(own_ref[tiles], shuffle_ref[...], width)
        gate = own_gate[rows, 0:1]
        total = 0.0
        for q, cot in enumerate(pieces):
            cols = slice(q * piece, (q + 1) * piece)
            own_gated[rows, cols] = (gate * cot).astype(BF16)
            total = total + jnp.sum(cot * result_ref[rows, cols].astype(F32), axis=1, keepdims=True)
        choice = total * gate * (1.0 - gate)
        spread(choice, choice_ref, rows)
        for q in range(PARTS):
            cols = slice(q * piece, (q + 1) * piece)
            router_ref[:, cols] += row_fold(normed_ref[rows, cols].astype(F32) * choice)


def grad_kernel(
    own_ref, other_ref, choice_ref, normed_ref, column_ref, gain_ref, own_router, other_router, core_ref,
    back_ref, send_ref, sums_ref, meta_ref,
):
    step = pl.program_id(0)
    features = own_ref.shape[1]
    piece = features // PARTS

    @pl.when(step == 0)
    def _():
        sums_ref[...] = jnp.zeros_like(sums_ref)

    for sub, (_, rows) in enumerate(group_slices()):
        choice = choice_ref[rows, 0:1]
        scaled = []
        for q in range(PARTS):
            cols = slice(q * piece, (q + 1) * piece)
            back = (own_ref[rows, cols].astype(F32) + other_ref[rows, cols].astype(F32)).astype(BF16)
            grad = back.astype(F32) + choice * column_ref[:, cols]
            sums_ref[:, cols] += row_fold(grad * normed_ref[rows, cols].astype(F32))
            scaled.append((grad * gain_ref[:, cols]).astype(BF16))
        bands = dot(back_ref[...], jnp.concatenate(scaled, axis=0)).astype(BF16)
        count = GROUP * TILE
        tiles = pl.ds(pl.multiple_of((step * SUB + sub) * count, count), count)
        for b in range(BANDS):
            send_ref[tiles, b * piece : (b + 1) * piece] = bands[b * count : (b + 1) * count]

    @pl.when(step == pl.num_programs(0) - 1)
    def _():
        gain_sum = jnp.sum(sums_ref[...], axis=0, keepdims=True) / gain_ref[...]
        router_sum = jnp.sum(own_router[...] + other_router[...], axis=0, keepdims=True)
        lower = core_ref[0, 0] == 0

        def lanes(value, number):
            return value[:, number * META : (number + 1) * META]

        pairs = features // (5 * META)
        for pair in range(pairs):
            for r in range(5):
                meta_ref[pair * TILE + r : pair * TILE + r + 1, :] = lanes(gain_sum, pair * 5 + r)
            for r in range(3):
                at = pair * 5 + r
                meta_ref[pair * TILE + 5 + r : pair * TILE + 6 + r, :] = jnp.where(
                    lower, lanes(router_sum, at), lanes(router_sum, at + 2)
                )
        meta = meta_ref[...].astype(BF16)
        for at in range(0, send_ref.shape[0], pairs * TILE):
            send_ref[at : at + pairs * TILE, BANDS * piece :] = meta


def by_group(kernel, inputs, outputs, flops, name, scratch=()):
    steps = None
    for value, rows in inputs:
        if isinstance(rows, int) and rows:
            steps = value.shape[0] // (rows * SUB)

    def spec(shape, rows):
        if not isinstance(rows, int):
            return rows
        if rows:
            return pl.BlockSpec((rows * SUB, shape[1]), lambda g: (g, 0))
        return pl.BlockSpec(shape, lambda g: (0, 0))

    moved = sum(value.size * value.dtype.itemsize for value, _ in inputs)
    moved += sum(math.prod(shape) * dtype.itemsize for shape, dtype, _ in outputs)
    return pl.pallas_call(
        kernel,
        grid=(steps,),
        in_specs=[spec(value.shape, rows) for value, rows in inputs],
        out_specs=[spec(shape, rows) for shape, _, rows in outputs],
        out_shape=[jax.ShapeDtypeStruct(shape, dtype) for shape, dtype, _ in outputs],
        scratch_shapes=list(scratch),
        compiler_params=params(1),
        cost_estimate=cost(flops, moved),
        name=name,
    )(*[value for value, _ in inputs])


def forward_kernel(own_ref, other_ref, up_ref, down_ref, out_ref, own_hidden, slope_ref, acc_ref, hidden_ref):
    step = pl.program_id(0)
    half = pl.num_programs(0) // 2
    count = own_ref.shape[0]
    sides = ((slice(0, count), own_ref), (slice(count, 2 * count), other_ref))

    @pl.when(step == 0)
    def _():
        for rows, x_ref in sides:
            acc_ref[rows] = dot(x_ref[...], up_ref[...])

    @pl.when((step > 0) & (step < half))
    def _():
        for rows, x_ref in sides:
            acc_ref[rows] += dot(x_ref[...], up_ref[...])

    @pl.when(step == half - 1)
    def _():
        root = math.sqrt(2.0 / math.pi)
        for (rows, _), kept in zip(sides, (own_hidden, hidden_ref)):
            pre = acc_ref[rows]
            square = pre * pre
            bend = jnp.tanh(root * (pre + 0.044715 * (square * pre)))
            share = 0.5 * (1.0 + bend)
            kept[...] = (pre * share).astype(BF16)
            inner = root * (1.0 + (3.0 * 0.044715) * square)
            slope_ref[rows] = share + 0.5 * pre * (1.0 - bend * bend) * inner

    @pl.when(step >= half)
    def _():
        out_ref[...] = dot(hidden_ref[...], down_ref[...]).astype(BF16)


def backward_kernel(own_ref, other_ref, down_ref, up_ref, slope_ref, out_ref, own_grad, acc_ref, grad_ref):
    step = pl.program_id(0)
    half = pl.num_programs(0) // 2
    count = own_ref.shape[0]
    sides = ((slice(0, count), own_ref), (slice(count, 2 * count), other_ref))

    @pl.when(step == 0)
    def _():
        for rows, cot_ref in sides:
            acc_ref[rows] = dot_nt(cot_ref[...], down_ref[...])

    @pl.when((step > 0) & (step < half))
    def _():
        for rows, cot_ref in sides:
            acc_ref[rows] += dot_nt(cot_ref[...], down_ref[...])

    @pl.when(step == half - 1)
    def _():
        for (rows, _), kept in zip(sides, (own_grad, grad_ref)):
            kept[...] = (acc_ref[rows] * slope_ref[rows]).astype(BF16)

    @pl.when(step >= half)
    def _():
        out_ref[...] = dot_nt(grad_ref[...], up_ref[...]).astype(BF16)


def expert_call(kernel, own, other, up, down, slope, name):
    count, features = own.shape
    hidden = up.shape[2]
    block = features // PARTS
    half = features // block

    def first(i):
        return jnp.minimum(i, half - 1)

    def second(i):
        return jnp.maximum(i - half, 0)

    rows_spec = pl.BlockSpec((count, block), lambda i: (0, first(i)))
    slope_spec = pl.BlockSpec((2 * count, hidden), lambda i: (0, 0))
    out_specs = [
        pl.BlockSpec((count, block), lambda i: (0, second(i))),
        pl.BlockSpec((count, hidden), lambda i: (0, 0)),
    ]
    out_shapes = [
        jax.ShapeDtypeStruct((count, features), BF16),
        jax.ShapeDtypeStruct((count, hidden), BF16),
    ]
    forward = slope is None
    early, late = (first, second) if forward else (second, first)
    up_spec = pl.BlockSpec((None, block, hidden), lambda i: (0, early(i), 0))
    down_spec = pl.BlockSpec((None, hidden, block), lambda i: (0, 0, late(i)))
    if forward:
        args, in_specs = (own, other, up, down), [rows_spec, rows_spec, up_spec, down_spec]
        out_specs.append(slope_spec)
        out_shapes.append(jax.ShapeDtypeStruct((2 * count, hidden), F32))
    else:
        args = (own, other, down, up, slope)
        in_specs = [rows_spec, rows_spec, down_spec, up_spec, slope_spec]
    return pl.pallas_call(
        kernel,
        grid=(2 * half,),
        in_specs=in_specs,
        out_specs=out_specs,
        out_shape=out_shapes,
        scratch_shapes=[pltpu.VMEM((2 * count, hidden), F32), pltpu.VMEM((count, hidden), BF16)],
        compiler_params=params(1),
        cost_estimate=cost(6 * count * features * hidden, 4 * features * (2 * count + hidden)),
        name=name,
    )(*args)


def last_kernel(x_ref, weight_ref, out_ref, *, product):
    out_ref[...] = product(x_ref[...], weight_ref[...]).astype(BF16)


def last_call(product, x, weight, name):
    count, hidden = x.shape
    features = weight.shape[2] if product is dot else weight.shape[1]
    block = features // PARTS
    if product is dot:
        weight_spec = pl.BlockSpec((None, hidden, block), lambda i: (0, 0, i))
    else:
        weight_spec = pl.BlockSpec((None, block, hidden), lambda i: (0, i, 0))
    return pl.pallas_call(
        functools.partial(last_kernel, product=product),
        grid=(PARTS,),
        in_specs=[pl.BlockSpec((count, hidden), lambda i: (0, 0)), weight_spec],
        out_specs=pl.BlockSpec((count, block), lambda i: (0, i)),
        out_shape=jax.ShapeDtypeStruct((count, features), BF16),
        compiler_params=params(1),
        cost_estimate=cost(2 * count * features * hidden * LOUD, 2 * features * (count + hidden) * LOUD),
        name=name,
    )(x, weight)


def exchange(messages):
    blocks = messages.reshape(-1, TILE, messages.shape[1])
    blocks = lax.all_to_all(blocks, CHIPS, split_axis=0, concat_axis=0, tiled=True)
    return blocks.reshape(messages.shape)


def swap(value):
    return lax.ppermute(value, "core", [(0, 1), (1, 0)])


def body(tokens, norm_gain, router_weight, up_weight, down_weight, expert_ids, cotangent):
    toks, features = tokens.shape
    eps, pairs, cores = (lax.axis_size(name) for name in EVERY)
    experts = eps * pairs
    shard = features // (pairs * cores)
    rows = experts * CAP
    devices = experts * cores

    core = jnp.full((1, 1), lax.axis_index("core"), jnp.int32)
    matrix = shuffle_matrix()
    shuffle, shuffle_back = jnp.asarray(matrix, BF16), jnp.asarray(matrix.T, BF16)
    ids_t = expert_ids.T
    group_rows, group_tiles = GROUP * CAP, GROUP * TILE
    row_shape, tiles, width = (rows, features), experts * TILE, features * CAP // TILE
    wide, line, fold = (rows, 128), (1, features), (8, features)
    shuffling = 2 * rows * features * CAP * PARTS * GROUP // PARTS
    b16, f32 = jnp.dtype(BF16), jnp.dtype(F32)
    meta_spec = pl.BlockSpec((pairs * TILE, META), lambda g: (0, width // META))

    cot_sent = pack(ids_t, cotangent, experts)
    arrived = exchange(pack(ids_t, tokens, experts, (norm_gain.reshape(1, shard), router_weight, core)))
    arrived, cot_sent = lax.optimization_barrier((arrived, cot_sent))
    arrived_other = swap(arrived)
    cot_arrived = exchange(cot_sent)
    normed, normed_other, gate, gate_other, gain, column = by_group(
        norm_kernel,
        [
            (arrived, group_tiles),
            (arrived_other, group_tiles),
            (arrived, meta_spec),
            (arrived_other, meta_spec),
            (core, SMALL),
            (shuffle, 0),
        ],
        [
            (row_shape, b16, group_rows),
            (row_shape, b16, group_rows),
            (wide, f32, group_rows),
            (wide, f32, group_rows),
            (line, f32, 0),
            (line, f32, 0),
        ],
        2 * shuffling,
        "norm",
    )
    other_part, hidden, slope = expert_call(
        forward_kernel, normed, normed_other, up_weight, down_weight, None, "forward"
    )
    other_part = swap(other_part)
    own_part = last_call(dot, hidden, down_weight, "forward_own")
    result, result_sent = by_group(
        out_kernel,
        [(own_part, group_rows), (other_part, group_rows), (gate, group_rows), (shuffle_back, 0)],
        [(row_shape, b16, group_rows), ((tiles, width), b16, group_tiles)],
        shuffling,
        "out",
    )
    cot_arrived, result_sent = lax.optimization_barrier((cot_arrived, result_sent))
    cot_other = swap(cot_arrived)
    result_back = exchange(result_sent)
    gated, gated_other, choice, router_sum = by_group(
        cot_kernel,
        [
            (cot_arrived, group_tiles),
            (cot_other, group_tiles),
            (gate, group_rows),
            (gate_other, group_rows),
            (result, group_rows),
            (normed, group_rows),
            (shuffle, 0),
        ],
        [
            (row_shape, b16, group_rows),
            (row_shape, b16, group_rows),
            (wide, f32, group_rows),
            (fold, f32, 0),
        ],
        2 * shuffling,
        "cot",
    )
    router_other = swap(router_sum)
    other_grad, grad_hidden = expert_call(
        backward_kernel, gated, gated_other, up_weight, down_weight, slope, "backward"
    )
    other_grad = swap(other_grad)
    own_grad = last_call(dot_nt, grad_hidden, up_weight, "backward_own")
    (grad_sent,) = by_group(
        grad_kernel,
        [
            (own_grad, group_rows),
            (other_grad, group_rows),
            (choice, group_rows),
            (normed, group_rows),
            (column, 0),
            (gain, 0),
            (router_sum, 0),
            (router_other, 0),
            (core, SMALL),
            (shuffle_back, 0),
        ],
        [((tiles, width + META), b16, 0)],
        shuffling,
        "grad",
        [pltpu.VMEM(fold, F32), pltpu.VMEM((pairs * TILE, META), F32)],
    )
    grad_back = exchange(grad_sent)
    mixed = token_side(mixed_kernel, expert_ids, [tokens], result_back, [], "mixed")
    grad_tokens = token_side(
        grad_tokens_kernel,
        expert_ids,
        [tokens, cotangent],
        grad_back,
        [
            pltpu.VMEM((toks, features), F32),
            pltpu.VMEM((toks, 256), F32),
            pltpu.VMEM((toks, 256), F32),
        ],
        "grad_tokens",
    )

    grad_router, own_gain, other_gain = summed(grad_back, core, shard, 1.0 / math.sqrt(toks * devices))
    grad_gain = (own_gain + swap(other_gain)).reshape(shard)
    grad_router = grad_router.T
    return mixed, grad_tokens, grad_router, grad_gain


def solution(mesh):
    eps, fsdp = mesh.devices.shape
    fine = Mesh(mesh.devices.reshape(eps, fsdp // 2, 2), EVERY)
    in_specs = (
        P(EVERY, None),
        P(FSDP),
        P(FSDP, None),
        P(EVERY, None, None),
        P(EVERY, None, None),
        P(EVERY, None),
        P(EVERY, None),
    )
    out_specs = (P(EVERY, None), P(EVERY, None), P(FSDP, None), P(FSDP))
    return jax.shard_map(body, mesh=fine, in_specs=in_specs, out_specs=out_specs, check_vma=False)
```

```python
import functools
import math

import jax
import jax.numpy as jnp
import numpy as np
from jax import lax
from jax.experimental import pallas as pl
from jax.experimental.pallas import tpu as pltpu
from jax.sharding import Mesh
from jax.sharding import PartitionSpec as P

EPS = 1e-06
CAP = 6
PARTS = 4
TILE = 8
BANDS = CAP * PARTS // TILE
GROUP = 8
BF16 = jnp.bfloat16
F32 = jnp.float32
LOUD = 64
PACK_STEPS = 2
META = 128
SUB = 4
VMEM_LIMIT = 56 * 1024 * 1024
CHIPS = ("ep", "pair")
FSDP = ("pair", "core")
EVERY = ("ep", "pair", "core")


def params(steps):
    return pltpu.CompilerParams(
        dimension_semantics=("arbitrary",) * steps, vmem_limit_bytes=VMEM_LIMIT
    )


def cost(flops, bytes_accessed):
    return pl.CostEstimate(flops=flops, bytes_accessed=bytes_accessed, transcendentals=0)


def iota(shape, dim):
    return lax.broadcasted_iota(jnp.int32, shape, dim)


def dot(a, b):
    return jnp.dot(a, b, preferred_element_type=F32)


def dot_nt(a, b):
    return lax.dot_general(a, b, (((1,), (1,)), ((), ())), preferred_element_type=F32)


def as_bf16(mask):
    return mask.astype(F32).astype(BF16)


def shuffle_matrix():
    size = CAP * PARTS * GROUP
    matrix = np.zeros((size, size), np.float32)
    for message in range(GROUP):
        for number in range(CAP * PARTS):
            piece, slot = divmod(number, CAP)
            band, row = divmod(number, TILE)
            matrix[
                piece * GROUP * CAP + message * CAP + slot,
                band * GROUP * TILE + message * TILE + row,
            ] = 1.0
    return matrix


def slot_target(band, column):
    row = column & (TILE - 1)
    limit = CAP - 2 * band
    low = row < limit
    slot = 2 * band + row - jnp.where(low, 0, CAP)
    return (column >> 3) * CAP + slot, low


def pack_kernel(experts, ids_ref, rows_ref, *refs):
    *meta_refs, out_ref, pos_ref = refs
    step = pl.program_id(0)
    toks, features = rows_ref.shape
    count = out_ref.shape[0]
    piece = features // PARTS

    @pl.when(step == 0)
    def _():
        first, second = ids_ref[0:1, :], ids_ref[1:2, :]
        expert = iota((experts, toks), 0)
        in_first, in_second = expert == first, expert == second
        both = as_bf16(in_first | in_second)
        earlier = as_bf16(iota((toks, toks), 0) < iota((toks, toks), 1))
        earlier_count = dot(both, earlier)
        slot_first = jnp.sum(jnp.where(in_first, earlier_count, 0.0), axis=0, keepdims=True)
        slot_second = jnp.sum(jnp.where(in_second, earlier_count, 0.0), axis=0, keepdims=True)
        pos_ref[0:1, :] = first * CAP + slot_first.astype(jnp.int32)
        pos_ref[1:2, :] = second * CAP + slot_second.astype(jnp.int32)

    row = step * count + iota((count, toks), 0)
    for band in range(BANDS):
        target, low = slot_target(band, row)
        hit = (target == pos_ref[0:1, :]) | (target == pos_ref[1:2, :])
        placing = jnp.concatenate([as_bf16(hit & low), as_bf16(hit & ~low)], axis=1)
        pieces = [rows_ref[:, p * piece : (p + 1) * piece] for p in (band, band + 1)]
        out_ref[:, band * piece : (band + 1) * piece] = dot(
            placing, jnp.concatenate(pieces, axis=0)
        ).astype(BF16)

    if meta_refs:
        gain_ref, router_ref, core_ref = meta_refs
        shard = router_ref.shape[1]
        shift = core_ref[0, 0] * (META // 2)
        shifted = as_bf16(iota((shard, 3 * META), 1) == iota((shard, 3 * META), 0) + shift)
        gain = dot(gain_ref[...].reshape(1, shard), shifted)
        columns = dot(router_ref[...], shifted).astype(BF16)
        tile_row = iota((count, META), 0) & (TILE - 1)
        pick_row = step * count + iota((count, experts), 0)
        pick_column = iota((count, experts), 1)
        total = jnp.zeros((count, META), F32)
        for r in range(3):
            lanes = slice(r * META, (r + 1) * META)
            total = jnp.where(tile_row == r, gain[0:1, lanes], total)
            total = total + dot(as_bf16(pick_row == pick_column * TILE + 3 + r), columns[:, lanes])
        out_ref[:, BANDS * piece :] = total.astype(BF16)


SMALL = pl.BlockSpec(memory_space=pltpu.SMEM)


def pack(ids_t, rows, experts, meta=()):
    toks, features = rows.shape
    width = features * CAP // TILE + (META if meta else 0)
    out_rows = experts * TILE
    steps = PACK_STEPS
    meta_specs = []
    if meta:
        gain, router, _ = meta
        meta_specs = [
            pl.BlockSpec(gain.shape, lambda i: (0,)),
            pl.BlockSpec(router.shape, lambda i: (0, 0)),
            SMALL,
        ]
    return pl.pallas_call(
        functools.partial(pack_kernel, experts),
        grid=(steps,),
        in_specs=[
            pl.BlockSpec((2, toks), lambda i: (0, 0)),
            pl.BlockSpec((toks, features), lambda i: (0, 0)),
            *meta_specs,
        ],
        out_specs=pl.BlockSpec((out_rows // steps, width), lambda i: (i, 0)),
        out_shape=jax.ShapeDtypeStruct((out_rows, width), BF16),
        scratch_shapes=[pltpu.VMEM((8, toks), jnp.int32)],
        compiler_params=params(1),
        cost_estimate=cost(2 * out_rows * 2 * toks * width, 2 * out_rows * width),
        name="pack",
    )(ids_t, rows, *meta)


def fill_choosing(ids_ref, choose_ref):
    toks = ids_ref.shape[0]
    columns = choose_ref.shape[2]
    experts = columns // TILE
    first, second = ids_ref[:, 0:1], ids_ref[:, 1:2]
    expert = iota((toks, experts), 1)
    in_first, in_second = expert == first, expert == second
    both = as_bf16(in_first | in_second)
    earlier = as_bf16(iota((toks, toks), 1) < iota((toks, toks), 0))
    count = dot(earlier, both)
    pos_first = first * CAP + jnp.sum(
        jnp.where(in_first, count, 0.0), axis=1, keepdims=True
    ).astype(jnp.int32)
    pos_second = second * CAP + jnp.sum(
        jnp.where(in_second, count, 0.0), axis=1, keepdims=True
    ).astype(jnp.int32)
    for band in range(BANDS):
        target, low = slot_target(band, iota((toks, columns), 1))
        hit = (target == pos_first) | (target == pos_second)
        choose_ref[band, :toks, :] = as_bf16(hit & low)
        choose_ref[band, toks:, :] = as_bf16(hit & ~low)


def summed_pieces(choose_ref, band_refs):
    toks = choose_ref.shape[1] // 2
    sums = [dot(choose_ref[band], band_refs[band][...]) for band in range(BANDS)]
    pieces = [sums[0][:toks]]
    for band in range(1, BANDS):
        pieces.append(sums[band - 1][toks:] + sums[band][:toks])
    pieces.append(sums[BANDS - 1][toks:])
    return pieces


def mixed_kernel(ids_ref, tokens_ref, band0, band1, band2, out_ref, choose_ref, scale_ref, square_ref):
    step = pl.program_id(0)
    width = band0.shape[1]
    features = tokens_ref.shape[1]
    piece = features // PARTS

    @pl.when(step == 0)
    def _():
        fill_choosing(ids_ref, choose_ref)
        square_ref[...] = jnp.zeros_like(square_ref)

    for number, value in enumerate(summed_pieces(choose_ref, (band0, band1, band2))):
        cols = pl.ds(pl.multiple_of(number * piece + step * width, width), width)
        x = tokens_ref[:, cols].astype(F32)
        square_ref[...] += x * x
        out_ref[:, cols] = (x + value).astype(BF16)

    @pl.when(step == pl.num_programs(0) - 1)
    def _():
        scale = lax.rsqrt(jnp.sum(square_ref[...], axis=1, keepdims=True) / features + EPS)
        scale_ref[...] = jnp.broadcast_to(scale, scale_ref.shape)


def grad_tokens_kernel(
    choose_ref, scale_ref, tokens_ref, cot_ref, band0, band1, band2, out_ref, grad_ref, cross_ref
):
    step = pl.program_id(0)
    width = band0.shape[1]
    features = tokens_ref.shape[1]
    piece = features // PARTS

    @pl.when(step == 0)
    def _():
        cross_ref[...] = jnp.zeros_like(cross_ref)

    for number, value in enumerate(summed_pieces(choose_ref, (band0, band1, band2))):
        cols = pl.ds(pl.multiple_of(number * piece + step * width, width), width)
        grad_ref[:, cols] = value
        cross_ref[...] += tokens_ref[:, cols].astype(F32) * value

    @pl.when(step == pl.num_programs(0) - 1)
    def _():
        scale = scale_ref[:, 0:1]
        back = jnp.sum(cross_ref[...], axis=1, keepdims=True) / features * scale * scale * scale
        for at in range(0, features, width):
            cols = slice(at, at + width)
            x = tokens_ref[:, cols].astype(F32)
            grad = scale * grad_ref[:, cols] - x * back
            out_ref[:, cols] = (cot_ref[:, cols].astype(F32) + grad).astype(BF16)


def token_side(kernel, whole_inputs, bands, out_shapes, scratch, name):
    columns = bands.shape[0]
    piece = whole_inputs[-1].shape[1] // PARTS
    width = piece
    steps = piece // width

    def whole(shape):
        return pl.BlockSpec(shape, lambda c: (0,) * len(shape))

    def band_spec(band):
        return pl.BlockSpec((columns, width), lambda c: (0, band * steps + c))

    return pl.pallas_call(
        kernel,
        grid=(steps,),
        in_specs=[whole(value.shape) for value in whole_inputs] + [band_spec(b) for b in range(BANDS)],
        out_specs=[whole(shape.shape) for shape in out_shapes],
        out_shape=out_shapes,
        scratch_shapes=scratch,
        compiler_params=params(1),
        cost_estimate=cost(columns * columns * BANDS * piece, 2 * columns * BANDS * piece),
        name=name,
    )(*whole_inputs, *([bands] * BANDS))


def sums_kernel(scale, meta_ref, core_ref, router_ref, own_ref, other_ref):
    messages = meta_ref[...]
    tiles = messages.shape[0]
    experts, shard = router_ref.shape
    lower = core_ref[0, 0] == 0
    rows = [
        dot(as_bf16(iota((experts, tiles), 1) == iota((experts, tiles), 0) * TILE + 5 + r), messages)
        for r in range(3)
    ]
    router = jnp.concatenate(rows, axis=1) * scale
    router_ref[...] = jnp.where(lower, router[:, :shard], router[:, META // 2 : META // 2 + shard])
    total = dot(as_bf16((iota((TILE, tiles), 1) & (TILE - 1)) == iota((TILE, tiles), 0)), messages)
    total = jnp.concatenate([total[r : r + 1] for r in range(5)], axis=1) * scale
    first, second = total[:, :shard], total[:, shard : 2 * shard]
    own_ref[...] = jnp.where(lower, first, second)
    other_ref[...] = jnp.where(lower, second, first)


def summed(messages, core, shard, scale):
    tiles, width = messages.shape
    row = jax.ShapeDtypeStruct((1, shard), F32)
    return pl.pallas_call(
        functools.partial(sums_kernel, scale),
        grid=(1,),
        in_specs=[pl.BlockSpec((tiles, META), lambda i: (0, width // META - 1)), SMALL],
        out_specs=[
            pl.BlockSpec((tiles // TILE, shard), lambda i: (0, 0)),
            pl.BlockSpec((1, shard), lambda i: (0, 0)),
            pl.BlockSpec((1, shard), lambda i: (0, 0)),
        ],
        out_shape=[jax.ShapeDtypeStruct((tiles // TILE, shard), F32), row, row],
        compiler_params=params(1),
        cost_estimate=cost(10**6, 2 * tiles * META),
        name="sums",
    )(messages, core)


def unpacked(block, shuffle, width):
    piece = width // BANDS
    stacked = jnp.concatenate([block[:, b * piece : (b + 1) * piece] for b in range(BANDS)], axis=0)
    rows = dot(shuffle, stacked)
    count = GROUP * CAP
    return [rows[q * count : (q + 1) * count] for q in range(PARTS)]


def spread(column, ref, rows):
    ref[rows] = jnp.broadcast_to(column, (GROUP * CAP, ref.shape[1]))


def row_fold(value):
    total = value[0:8]
    for at in range(8, value.shape[0], 8):
        total = total + value[at : at + 8]
    return total


def group_slices():
    for sub in range(SUB):
        yield (
            slice(sub * GROUP * TILE, (sub + 1) * GROUP * TILE),
            slice(sub * GROUP * CAP, (sub + 1) * GROUP * CAP),
        )


def norm_kernel(
    own_ref, other_ref, own_meta, other_meta, core_ref, shuffle_ref,
    own_normed, other_normed, own_gate, other_gate, gain_ref, column_ref,
):
    features = own_normed.shape[1]
    width = own_ref.shape[1] - META
    piece = features // PARTS

    @pl.when(pl.program_id(0) == 0)
    def _():
        own, other = own_meta[...].astype(F32), other_meta[...].astype(F32)
        lower = core_ref[0, 0] == 0
        first, second = jnp.where(lower, own, other), jnp.where(lower, other, own)
        for part, ref in ((0, gain_ref), (3, column_ref)):
            for pair in range(features // (5 * META)):
                at = pair * TILE + part
                rows = [first[at + r : at + r + 1] for r in range(3)]
                rows += [second[at + r : at + r + 1] for r in range(3)]
                rows = [rows[0], rows[1], rows[2] + rows[3], rows[4], rows[5]]
                ref[:, pair * 5 * META : (pair + 1) * 5 * META] = jnp.concatenate(rows, axis=1)

    for block_ref, normed_ref, gate_ref in (
        (own_ref, own_normed, own_gate),
        (other_ref, other_normed, other_gate),
    ):
        for tiles, rows in group_slices():
            pieces = unpacked(block_ref[tiles, :width], shuffle_ref[...], width)
            square = sum(jnp.sum(x * x, axis=1, keepdims=True) for x in pieces)
            scale = lax.rsqrt(square / features + EPS)
            logit = 0.0
            for q, x in enumerate(pieces):
                cols = slice(q * piece, (q + 1) * piece)
                normed = (x * scale * gain_ref[:, cols]).astype(BF16)
                normed_ref[rows, cols] = normed
                logit = logit + jnp.sum(
                    normed.astype(F32) * column_ref[:, cols], axis=1, keepdims=True
                )
            spread(jax.nn.sigmoid(logit), gate_ref, rows)


def out_kernel(own_ref, other_ref, gate_ref, back_ref, result_ref, send_ref):
    piece = own_ref.shape[1] // PARTS
    for tiles, rows in group_slices():
        gate = gate_ref[rows, 0:1]
        gated = []
        for q in range(PARTS):
            cols = slice(q * piece, (q + 1) * piece)
            result = (own_ref[rows, cols].astype(F32) + other_ref[rows, cols].astype(F32)).astype(BF16)
            result_ref[rows, cols] = result
            gated.append((gate * result.astype(F32)).astype(BF16))
        bands = dot(back_ref[...], jnp.concatenate(gated, axis=0)).astype(BF16)
        for b in range(BANDS):
            send_ref[tiles, b * piece : (b + 1) * piece] = bands[
                b * GROUP * TILE : (b + 1) * GROUP * TILE
            ]


def cot_kernel(
    own_ref, other_ref, own_gate, other_gate, result_ref, normed_ref, shuffle_ref,
    own_gated, other_gated, choice_ref, router_ref,
):
    width = own_ref.shape[1]
    piece = width // BANDS

    @pl.when(pl.program_id(0) == 0)
    def _():
        router_ref[...] = jnp.zeros_like(router_ref)

    for tiles, rows in group_slices():
        pieces = unpacked(other_ref[tiles], shuffle_ref[...], width)
        gate = other_gate[rows, 0:1]
        for q, cot in enumerate(pieces):
            other_gated[rows, q * piece : (q + 1) * piece] = (gate * cot).astype(BF16)
        pieces = unpacked(own_ref[tiles], shuffle_ref[...], width)
        gate = own_gate[rows, 0:1]
        total = 0.0
        for q, cot in enumerate(pieces):
            cols = slice(q * piece, (q + 1) * piece)
            own_gated[rows, cols] = (gate * cot).astype(BF16)
            total = total + jnp.sum(cot * result_ref[rows, cols].astype(F32), axis=1, keepdims=True)
        choice = total * gate * (1.0 - gate)
        spread(choice, choice_ref, rows)
        for q in range(PARTS):
            cols = slice(q * piece, (q + 1) * piece)
            router_ref[:, cols] += row_fold(normed_ref[rows, cols].astype(F32) * choice)


def grad_kernel(
    own_ref, other_ref, choice_ref, normed_ref, column_ref, gain_ref, own_router, other_router, core_ref,
    back_ref, send_ref, sums_ref, meta_ref,
):
    step = pl.program_id(0)
    features = own_ref.shape[1]
    piece = features // PARTS

    @pl.when(step == 0)
    def _():
        sums_ref[...] = jnp.zeros_like(sums_ref)

    for sub, (_, rows) in enumerate(group_slices()):
        choice = choice_ref[rows, 0:1]
        scaled = []
        for q in range(PARTS):
            cols = slice(q * piece, (q + 1) * piece)
            back = (own_ref[rows, cols].astype(F32) + other_ref[rows, cols].astype(F32)).astype(BF16)
            grad = back.astype(F32) + choice * column_ref[:, cols]
            sums_ref[:, cols] += row_fold(grad * normed_ref[rows, cols].astype(F32))
            scaled.append((grad * gain_ref[:, cols]).astype(BF16))
        bands = dot(back_ref[...], jnp.concatenate(scaled, axis=0)).astype(BF16)
        count = GROUP * TILE
        tiles = pl.ds(pl.multiple_of((step * SUB + sub) * count, count), count)
        for b in range(BANDS):
            send_ref[tiles, b * piece : (b + 1) * piece] = bands[b * count : (b + 1) * count]

    @pl.when(step == pl.num_programs(0) - 1)
    def _():
        gain_sum = jnp.sum(sums_ref[...], axis=0, keepdims=True) / gain_ref[...]
        router_sum = jnp.sum(own_router[...] + other_router[...], axis=0, keepdims=True)
        lower = core_ref[0, 0] == 0

        def lanes(value, number):
            return value[:, number * META : (number + 1) * META]

        pairs = features // (5 * META)
        for pair in range(pairs):
            for r in range(5):
                meta_ref[pair * TILE + r : pair * TILE + r + 1, :] = lanes(gain_sum, pair * 5 + r)
            for r in range(3):
                at = pair * 5 + r
                meta_ref[pair * TILE + 5 + r : pair * TILE + 6 + r, :] = jnp.where(
                    lower, lanes(router_sum, at), lanes(router_sum, at + 2)
                )
        meta = meta_ref[...].astype(BF16)
        for at in range(0, send_ref.shape[0], pairs * TILE):
            send_ref[at : at + pairs * TILE, BANDS * piece :] = meta


def by_group(kernel, inputs, outputs, flops, name, scratch=()):
    steps = None
    for value, rows in inputs:
        if isinstance(rows, int) and rows:
            steps = value.shape[0] // (rows * SUB)

    def spec(shape, rows):
        if not isinstance(rows, int):
            return rows
        if rows:
            return pl.BlockSpec((rows * SUB, shape[1]), lambda g: (g, 0))
        return pl.BlockSpec(shape, lambda g: (0, 0))

    moved = sum(value.size * value.dtype.itemsize for value, _ in inputs)
    moved += sum(math.prod(shape) * dtype.itemsize for shape, dtype, _ in outputs)
    return pl.pallas_call(
        kernel,
        grid=(steps,),
        in_specs=[spec(value.shape, rows) for value, rows in inputs],
        out_specs=[spec(shape, rows) for shape, _, rows in outputs],
        out_shape=[jax.ShapeDtypeStruct(shape, dtype) for shape, dtype, _ in outputs],
        scratch_shapes=list(scratch),
        compiler_params=params(1),
        cost_estimate=cost(flops, moved),
        name=name,
    )(*[value for value, _ in inputs])


def forward_kernel(own_ref, other_ref, up_ref, down_ref, out_ref, own_hidden, slope_ref, acc_ref, hidden_ref):
    step = pl.program_id(0)
    half = pl.num_programs(0) // 2
    count = own_ref.shape[0]
    sides = ((slice(0, count), own_ref), (slice(count, 2 * count), other_ref))

    @pl.when(step == 0)
    def _():
        for rows, x_ref in sides:
            acc_ref[rows] = dot(x_ref[...], up_ref[...])

    @pl.when((step > 0) & (step < half))
    def _():
        for rows, x_ref in sides:
            acc_ref[rows] += dot(x_ref[...], up_ref[...])

    @pl.when(step == half - 1)
    def _():
        root = math.sqrt(2.0 / math.pi)
        for (rows, _), kept in zip(sides, (own_hidden, hidden_ref)):
            pre = acc_ref[rows]
            square = pre * pre
            bend = jnp.tanh(root * (pre + 0.044715 * (square * pre)))
            share = 0.5 * (1.0 + bend)
            kept[...] = (pre * share).astype(BF16)
            inner = root * (1.0 + (3.0 * 0.044715) * square)
            slope_ref[rows] = share + 0.5 * pre * (1.0 - bend * bend) * inner

    @pl.when(step >= half)
    def _():
        out_ref[...] = dot(hidden_ref[...], down_ref[...]).astype(BF16)


def backward_kernel(own_ref, other_ref, down_ref, up_ref, slope_ref, out_ref, own_grad, acc_ref, grad_ref):
    step = pl.program_id(0)
    half = pl.num_programs(0) // 2
    count = own_ref.shape[0]
    sides = ((slice(0, count), own_ref), (slice(count, 2 * count), other_ref))

    @pl.when(step == 0)
    def _():
        for rows, cot_ref in sides:
            acc_ref[rows] = dot_nt(cot_ref[...], down_ref[...])

    @pl.when((step > 0) & (step < half))
    def _():
        for rows, cot_ref in sides:
            acc_ref[rows] += dot_nt(cot_ref[...], down_ref[...])

    @pl.when(step == half - 1)
    def _():
        for (rows, _), kept in zip(sides, (own_grad, grad_ref)):
            kept[...] = (acc_ref[rows] * slope_ref[rows]).astype(BF16)

    @pl.when(step >= half)
    def _():
        out_ref[...] = dot_nt(grad_ref[...], up_ref[...]).astype(BF16)


def expert_call(kernel, own, other, up, down, slope, name):
    count, features = own.shape
    hidden = up.shape[2]
    block = features // PARTS
    half = features // block

    def first(i):
        return jnp.minimum(i, half - 1)

    def second(i):
        return jnp.maximum(i - half, 0)

    rows_spec = pl.BlockSpec((count, block), lambda i: (0, first(i)))
    slope_spec = pl.BlockSpec((2 * count, hidden), lambda i: (0, 0))
    out_specs = [
        pl.BlockSpec((count, block), lambda i: (0, second(i))),
        pl.BlockSpec((count, hidden), lambda i: (0, 0)),
    ]
    out_shapes = [
        jax.ShapeDtypeStruct((count, features), BF16),
        jax.ShapeDtypeStruct((count, hidden), BF16),
    ]
    forward = slope is None
    early, late = (first, second) if forward else (second, first)
    up_spec = pl.BlockSpec((None, block, hidden), lambda i: (0, early(i), 0))
    down_spec = pl.BlockSpec((None, hidden, block), lambda i: (0, 0, late(i)))
    if forward:
        args, in_specs = (own, other, up, down), [rows_spec, rows_spec, up_spec, down_spec]
        out_specs.append(slope_spec)
        out_shapes.append(jax.ShapeDtypeStruct((2 * count, hidden), F32))
    else:
        args = (own, other, down, up, slope)
        in_specs = [rows_spec, rows_spec, down_spec, up_spec, slope_spec]
    return pl.pallas_call(
        kernel,
        grid=(2 * half,),
        in_specs=in_specs,
        out_specs=out_specs,
        out_shape=out_shapes,
        scratch_shapes=[pltpu.VMEM((2 * count, hidden), F32), pltpu.VMEM((count, hidden), BF16)],
        compiler_params=params(1),
        cost_estimate=cost(6 * count * features * hidden, 4 * features * (2 * count + hidden)),
        name=name,
    )(*args)


def last_kernel(x_ref, weight_ref, out_ref, *, product):
    out_ref[...] = product(x_ref[...], weight_ref[...]).astype(BF16)


def last_call(product, x, weight, name):
    count, hidden = x.shape
    features = weight.shape[2] if product is dot else weight.shape[1]
    block = features // PARTS
    if product is dot:
        weight_spec = pl.BlockSpec((None, hidden, block), lambda i: (0, 0, i))
    else:
        weight_spec = pl.BlockSpec((None, block, hidden), lambda i: (0, i, 0))
    return pl.pallas_call(
        functools.partial(last_kernel, product=product),
        grid=(PARTS,),
        in_specs=[pl.BlockSpec((count, hidden), lambda i: (0, 0)), weight_spec],
        out_specs=pl.BlockSpec((count, block), lambda i: (0, i)),
        out_shape=jax.ShapeDtypeStruct((count, features), BF16),
        compiler_params=params(1),
        cost_estimate=cost(2 * count * features * hidden * LOUD, 2 * features * (count + hidden) * LOUD),
        name=name,
    )(x, weight)


def exchange(messages):
    blocks = messages.reshape(-1, TILE, messages.shape[1])
    blocks = lax.all_to_all(blocks, CHIPS, split_axis=0, concat_axis=0, tiled=True)
    return blocks.reshape(messages.shape)


def swap(value):
    return lax.ppermute(value, "core", [(0, 1), (1, 0)])


def body(tokens, norm_gain, router_weight, up_weight, down_weight, expert_ids, cotangent):
    toks, features = tokens.shape
    eps, pairs, cores = (lax.axis_size(name) for name in EVERY)
    experts = eps * pairs
    shard = features // (pairs * cores)
    rows = experts * CAP
    devices = experts * cores

    core = jnp.full((1, 1), lax.axis_index("core"), jnp.int32)
    matrix = shuffle_matrix()
    shuffle, shuffle_back = jnp.asarray(matrix, BF16), jnp.asarray(matrix.T, BF16)
    ids_t = expert_ids.T
    group_rows, group_tiles = GROUP * CAP, GROUP * TILE
    row_shape, tiles, width = (rows, features), experts * TILE, features * CAP // TILE
    wide, line, fold = (rows, 128), (1, features), (8, features)
    shuffling = 2 * rows * features * CAP * PARTS * GROUP // PARTS
    b16, f32 = jnp.dtype(BF16), jnp.dtype(F32)
    meta_spec = pl.BlockSpec((pairs * TILE, META), lambda g: (0, width // META))

    cot_sent = pack(ids_t, cotangent, experts)
    arrived = exchange(pack(ids_t, tokens, experts, (norm_gain, router_weight.T, core)))
    arrived, cot_sent = lax.optimization_barrier((arrived, cot_sent))
    arrived_other = swap(arrived)
    cot_arrived = exchange(cot_sent)
    normed, normed_other, gate, gate_other, gain, column = by_group(
        norm_kernel,
        [
            (arrived, group_tiles),
            (arrived_other, group_tiles),
            (arrived, meta_spec),
            (arrived_other, meta_spec),
            (core, SMALL),
            (shuffle, 0),
        ],
        [
            (row_shape, b16, group_rows),
            (row_shape, b16, group_rows),
            (wide, f32, group_rows),
            (wide, f32, group_rows),
            (line, f32, 0),
            (line, f32, 0),
        ],
        2 * shuffling,
        "norm",
    )
    other_part, hidden, slope = expert_call(
        forward_kernel, normed, normed_other, up_weight, down_weight, None, "forward"
    )
    other_part = swap(other_part)
    own_part = last_call(dot, hidden, down_weight, "forward_own")
    result, result_sent = by_group(
        out_kernel,
        [(own_part, group_rows), (other_part, group_rows), (gate, group_rows), (shuffle_back, 0)],
        [(row_shape, b16, group_rows), ((tiles, width), b16, group_tiles)],
        shuffling,
        "out",
    )
    cot_arrived, result_sent = lax.optimization_barrier((cot_arrived, result_sent))
    cot_other = swap(cot_arrived)
    result_back = exchange(result_sent)
    gated, gated_other, choice, router_sum = by_group(
        cot_kernel,
        [
            (cot_arrived, group_tiles),
            (cot_other, group_tiles),
            (gate, group_rows),
            (gate_other, group_rows),
            (result, group_rows),
            (normed, group_rows),
            (shuffle, 0),
        ],
        [
            (row_shape, b16, group_rows),
            (row_shape, b16, group_rows),
            (wide, f32, group_rows),
            (fold, f32, 0),
        ],
        2 * shuffling,
        "cot",
    )
    router_other = swap(router_sum)
    other_grad, grad_hidden = expert_call(
        backward_kernel, gated, gated_other, up_weight, down_weight, slope, "backward"
    )
    other_grad = swap(other_grad)
    own_grad = last_call(dot_nt, grad_hidden, up_weight, "backward_own")
    (grad_sent,) = by_group(
        grad_kernel,
        [
            (own_grad, group_rows),
            (other_grad, group_rows),
            (choice, group_rows),
            (normed, group_rows),
            (column, 0),
            (gain, 0),
            (router_sum, 0),
            (router_other, 0),
            (core, SMALL),
            (shuffle_back, 0),
        ],
        [((tiles, width + META), b16, 0)],
        shuffling,
        "grad",
        [pltpu.VMEM(fold, F32), pltpu.VMEM((pairs * TILE, META), F32)],
    )
    grad_back = exchange(grad_sent)
    out_rows = jax.ShapeDtypeStruct((toks, features), BF16)
    choosing = jax.ShapeDtypeStruct((BANDS, 2 * toks, tiles), BF16)
    partial = pltpu.VMEM((toks, features // PARTS), F32)
    mixed, choose, scale = token_side(
        mixed_kernel,
        [expert_ids, tokens],
        result_back,
        [out_rows, choosing, jax.ShapeDtypeStruct((toks, 128), F32)],
        [partial],
        "mixed",
    )
    (grad_tokens,) = token_side(
        grad_tokens_kernel,
        [choose, scale, tokens, cotangent],
        grad_back,
        [out_rows],
        [pltpu.VMEM((toks, features), F32), partial],
        "grad_tokens",
    )
    grad_router, own_gain, other_gain = summed(grad_back, core, shard, 1.0 / math.sqrt(toks * devices))
    grad_gain = (own_gain + swap(other_gain)).reshape(shard)
    grad_router = grad_router.T
    return mixed, grad_tokens, grad_router, grad_gain


def solution(mesh):
    eps, fsdp = mesh.devices.shape
    fine = Mesh(mesh.devices.reshape(eps, fsdp // 2, 2), EVERY)
    in_specs = (
        P(EVERY, None),
        P(FSDP),
        P(FSDP, None),
        P(EVERY, None, None),
        P(EVERY, None, None),
        P(EVERY, None),
        P(EVERY, None),
    )
    out_specs = (P(EVERY, None), P(EVERY, None), P(FSDP, None), P(FSDP))
    return jax.shard_map(body, mesh=fine, in_specs=in_specs, out_specs=out_specs, check_vma=False)
```

```python
import functools
import math

import jax
import jax.numpy as jnp
import numpy as np
from jax import lax
from jax.experimental import pallas as pl
from jax.experimental.pallas import tpu as pltpu
from jax.sharding import Mesh
from jax.sharding import PartitionSpec as P

EPS = 1e-06
CAP = 6
PARTS = 4
TILE = 8
BANDS = CAP * PARTS // TILE
GROUP = 8
BF16 = jnp.bfloat16
F32 = jnp.float32
LOUD = 64
PACK_STEPS = 2
META = 128
SUB = 4
VMEM_LIMIT = 56 * 1024 * 1024
CHIPS = ("ep", "pair")
FSDP = ("pair", "core")
EVERY = ("ep", "pair", "core")


def params(steps):
    return pltpu.CompilerParams(
        dimension_semantics=("arbitrary",) * steps, vmem_limit_bytes=VMEM_LIMIT
    )


def cost(flops, bytes_accessed):
    return pl.CostEstimate(flops=flops, bytes_accessed=bytes_accessed, transcendentals=0)


def iota(shape, dim):
    return lax.broadcasted_iota(jnp.int32, shape, dim)


def dot(a, b):
    return jnp.dot(a, b, preferred_element_type=F32)


def dot_nt(a, b):
    return lax.dot_general(a, b, (((1,), (1,)), ((), ())), preferred_element_type=F32)


def as_bf16(mask):
    return mask.astype(F32).astype(BF16)


def shuffle_matrix():
    size = CAP * PARTS * GROUP
    matrix = np.zeros((size, size), np.float32)
    for message in range(GROUP):
        for number in range(CAP * PARTS):
            piece, slot = divmod(number, CAP)
            band, row = divmod(number, TILE)
            matrix[
                piece * GROUP * CAP + message * CAP + slot,
                band * GROUP * TILE + message * TILE + row,
            ] = 1.0
    return matrix


def slot_target(band, column):
    row = column & (TILE - 1)
    limit = CAP - 2 * band
    low = row < limit
    slot = 2 * band + row - jnp.where(low, 0, CAP)
    return (column >> 3) * CAP + slot, low


def pack_kernel(experts, ids_ref, rows_ref, *refs):
    *meta_refs, out_ref, pos_ref = refs
    step = pl.program_id(0)
    toks, features = rows_ref.shape
    count = out_ref.shape[0]
    piece = features // PARTS

    @pl.when(step == 0)
    def _():
        first, second = ids_ref[0:1, :], ids_ref[1:2, :]
        expert = iota((experts, toks), 0)
        in_first, in_second = expert == first, expert == second
        both = as_bf16(in_first | in_second)
        earlier = as_bf16(iota((toks, toks), 0) < iota((toks, toks), 1))
        earlier_count = dot(both, earlier)
        slot_first = jnp.sum(jnp.where(in_first, earlier_count, 0.0), axis=0, keepdims=True)
        slot_second = jnp.sum(jnp.where(in_second, earlier_count, 0.0), axis=0, keepdims=True)
        pos_ref[0:1, :] = first * CAP + slot_first.astype(jnp.int32)
        pos_ref[1:2, :] = second * CAP + slot_second.astype(jnp.int32)

    row = step * count + iota((count, toks), 0)
    for band in range(BANDS):
        target, low = slot_target(band, row)
        hit = (target == pos_ref[0:1, :]) | (target == pos_ref[1:2, :])
        placing = jnp.concatenate([as_bf16(hit & low), as_bf16(hit & ~low)], axis=1)
        pieces = [rows_ref[:, p * piece : (p + 1) * piece] for p in (band, band + 1)]
        out_ref[:, band * piece : (band + 1) * piece] = dot(
            placing, jnp.concatenate(pieces, axis=0)
        ).astype(BF16)

    if meta_refs:
        gain_ref, router_ref, core_ref = meta_refs
        shard = router_ref.shape[1]
        shift = core_ref[0, 0] * (META // 2)
        shifted = as_bf16(iota((shard, 3 * META), 1) == iota((shard, 3 * META), 0) + shift)
        gain = dot(gain_ref[...].reshape(1, shard), shifted)
        columns = dot(router_ref[...], shifted).astype(BF16)
        tile_row = iota((count, META), 0) & (TILE - 1)
        pick_row = step * count + iota((count, experts), 0)
        pick_column = iota((count, experts), 1)
        total = jnp.zeros((count, META), F32)
        for r in range(3):
            lanes = slice(r * META, (r + 1) * META)
            total = jnp.where(tile_row == r, gain[0:1, lanes], total)
            total = total + dot(as_bf16(pick_row == pick_column * TILE + 3 + r), columns[:, lanes])
        out_ref[:, BANDS * piece :] = total.astype(BF16)


SMALL = pl.BlockSpec(memory_space=pltpu.SMEM)


def pack(ids_t, rows, experts, meta=()):
    toks, features = rows.shape
    width = features * CAP // TILE + (META if meta else 0)
    out_rows = experts * TILE
    steps = PACK_STEPS
    meta_specs = []
    if meta:
        gain, router, _ = meta
        meta_specs = [
            pl.BlockSpec(gain.shape, lambda i: (0,)),
            pl.BlockSpec(router.shape, lambda i: (0, 0)),
            SMALL,
        ]
    return pl.pallas_call(
        functools.partial(pack_kernel, experts),
        grid=(steps,),
        in_specs=[
            pl.BlockSpec((2, toks), lambda i: (0, 0)),
            pl.BlockSpec((toks, features), lambda i: (0, 0)),
            *meta_specs,
        ],
        out_specs=pl.BlockSpec((out_rows // steps, width), lambda i: (i, 0)),
        out_shape=jax.ShapeDtypeStruct((out_rows, width), BF16),
        scratch_shapes=[pltpu.VMEM((8, toks), jnp.int32)],
        compiler_params=params(1),
        cost_estimate=cost(2 * out_rows * 2 * toks * width, 2 * out_rows * width),
        name="pack",
    )(ids_t, rows, *meta)


def fill_choosing(ids_ref, choose_ref):
    toks = ids_ref.shape[0]
    columns = choose_ref.shape[2]
    experts = columns // TILE
    first, second = ids_ref[:, 0:1], ids_ref[:, 1:2]
    expert = iota((toks, experts), 1)
    in_first, in_second = expert == first, expert == second
    both = as_bf16(in_first | in_second)
    earlier = as_bf16(iota((toks, toks), 1) < iota((toks, toks), 0))
    count = dot(earlier, both)
    pos_first = first * CAP + jnp.sum(
        jnp.where(in_first, count, 0.0), axis=1, keepdims=True
    ).astype(jnp.int32)
    pos_second = second * CAP + jnp.sum(
        jnp.where(in_second, count, 0.0), axis=1, keepdims=True
    ).astype(jnp.int32)
    for band in range(BANDS):
        target, low = slot_target(band, iota((toks, columns), 1))
        hit = (target == pos_first) | (target == pos_second)
        choose_ref[band, :toks, :] = as_bf16(hit & low)
        choose_ref[band, toks:, :] = as_bf16(hit & ~low)


def summed_pieces(choose_ref, band_refs):
    toks = choose_ref.shape[1] // 2
    sums = [dot(choose_ref[band], band_refs[band][...]) for band in range(BANDS)]
    pieces = [sums[0][:toks]]
    for band in range(1, BANDS):
        pieces.append(sums[band - 1][toks:] + sums[band][:toks])
    pieces.append(sums[BANDS - 1][toks:])
    return pieces


def add_pieces(base_ref, choose_ref, band_refs, out_ref):
    piece = base_ref.shape[1] // PARTS
    for number, value in enumerate(summed_pieces(choose_ref, band_refs)):
        cols = slice(number * piece, (number + 1) * piece)
        out_ref[:, cols] = (base_ref[:, cols].astype(F32) + value).astype(BF16)


def mixed_kernel(ids_ref, tokens_ref, band0, band1, band2, out_ref, choose_ref):
    fill_choosing(ids_ref, choose_ref)
    add_pieces(tokens_ref, choose_ref, (band0, band1, band2), out_ref)


def grad_tokens_kernel(choose_ref, cot_ref, band0, band1, band2, out_ref):
    add_pieces(cot_ref, choose_ref, (band0, band1, band2), out_ref)


def token_side(kernel, inputs, bands, out_shapes, name):
    columns = bands.shape[0]
    piece = inputs[-1].shape[1] // PARTS

    def whole(shape):
        return pl.BlockSpec(shape, lambda c: (0,) * len(shape))

    def band_spec(band):
        return pl.BlockSpec((columns, piece), lambda c: (0, band))

    return pl.pallas_call(
        kernel,
        grid=(1,),
        in_specs=[whole(value.shape) for value in inputs] + [band_spec(b) for b in range(BANDS)],
        out_specs=[whole(shape.shape) for shape in out_shapes],
        out_shape=out_shapes,
        compiler_params=params(1),
        cost_estimate=cost(columns * columns * BANDS * piece, 2 * columns * BANDS * piece),
        name=name,
    )(*inputs, *([bands] * BANDS))


def sums_kernel(scale, meta_ref, core_ref, router_ref, own_ref, other_ref):
    messages = meta_ref[...]
    tiles = messages.shape[0]
    experts, shard = router_ref.shape
    lower = core_ref[0, 0] == 0
    rows = [
        dot(as_bf16(iota((experts, tiles), 1) == iota((experts, tiles), 0) * TILE + 5 + r), messages)
        for r in range(3)
    ]
    router = jnp.concatenate(rows, axis=1) * scale
    router_ref[...] = jnp.where(lower, router[:, :shard], router[:, META // 2 : META // 2 + shard])
    total = dot(as_bf16((iota((TILE, tiles), 1) & (TILE - 1)) == iota((TILE, tiles), 0)), messages)
    total = jnp.concatenate([total[r : r + 1] for r in range(5)], axis=1) * scale
    first, second = total[:, :shard], total[:, shard : 2 * shard]
    own_ref[...] = jnp.where(lower, first, second)
    other_ref[...] = jnp.where(lower, second, first)


def summed(messages, core, shard, scale):
    tiles, width = messages.shape
    row = jax.ShapeDtypeStruct((1, shard), F32)
    return pl.pallas_call(
        functools.partial(sums_kernel, scale),
        grid=(1,),
        in_specs=[pl.BlockSpec((tiles, META), lambda i: (0, width // META - 1)), SMALL],
        out_specs=[
            pl.BlockSpec((tiles // TILE, shard), lambda i: (0, 0)),
            pl.BlockSpec((1, shard), lambda i: (0, 0)),
            pl.BlockSpec((1, shard), lambda i: (0, 0)),
        ],
        out_shape=[jax.ShapeDtypeStruct((tiles // TILE, shard), F32), row, row],
        compiler_params=params(1),
        cost_estimate=cost(10**6, 2 * tiles * META),
        name="sums",
    )(messages, core)


def unpacked(block, shuffle, width):
    piece = width // BANDS
    stacked = jnp.concatenate([block[:, b * piece : (b + 1) * piece] for b in range(BANDS)], axis=0)
    rows = dot(shuffle, stacked)
    count = GROUP * CAP
    return [rows[q * count : (q + 1) * count] for q in range(PARTS)]


def spread(column, ref, rows):
    ref[rows] = jnp.broadcast_to(column, (GROUP * CAP, ref.shape[1]))


def row_fold(value):
    total = value[0:8]
    for at in range(8, value.shape[0], 8):
        total = total + value[at : at + 8]
    return total


def group_slices():
    for sub in range(SUB):
        yield (
            slice(sub * GROUP * TILE, (sub + 1) * GROUP * TILE),
            slice(sub * GROUP * CAP, (sub + 1) * GROUP * CAP),
        )


def norm_kernel(
    own_ref, other_ref, own_meta, other_meta, core_ref, shuffle_ref,
    own_normed, other_normed, own_gate, other_gate, scale_ref, gain_ref, column_ref,
):
    features = own_normed.shape[1]
    width = own_ref.shape[1] - META
    piece = features // PARTS

    @pl.when(pl.program_id(0) == 0)
    def _():
        own, other = own_meta[...].astype(F32), other_meta[...].astype(F32)
        lower = core_ref[0, 0] == 0
        first, second = jnp.where(lower, own, other), jnp.where(lower, other, own)
        for part, ref in ((0, gain_ref), (3, column_ref)):
            for pair in range(features // (5 * META)):
                at = pair * TILE + part
                rows = [first[at + r : at + r + 1] for r in range(3)]
                rows += [second[at + r : at + r + 1] for r in range(3)]
                rows = [rows[0], rows[1], rows[2] + rows[3], rows[4], rows[5]]
                ref[:, pair * 5 * META : (pair + 1) * 5 * META] = jnp.concatenate(rows, axis=1)

    for block_ref, normed_ref, gate_ref in (
        (own_ref, own_normed, own_gate),
        (other_ref, other_normed, other_gate),
    ):
        for tiles, rows in group_slices():
            pieces = unpacked(block_ref[tiles, :width], shuffle_ref[...], width)
            square = sum(jnp.sum(x * x, axis=1, keepdims=True) for x in pieces)
            scale = lax.rsqrt(square / features + EPS)
            if block_ref is own_ref:
                spread(scale, scale_ref, rows)
            logit = 0.0
            for q, x in enumerate(pieces):
                cols = slice(q * piece, (q + 1) * piece)
                normed = (x * scale * gain_ref[:, cols]).astype(BF16)
                normed_ref[rows, cols] = normed
                logit = logit + jnp.sum(
                    normed.astype(F32) * column_ref[:, cols], axis=1, keepdims=True
                )
            spread(jax.nn.sigmoid(logit), gate_ref, rows)


def out_kernel(own_ref, other_ref, gate_ref, back_ref, result_ref, send_ref):
    piece = own_ref.shape[1] // PARTS
    for tiles, rows in group_slices():
        gate = gate_ref[rows, 0:1]
        gated = []
        for q in range(PARTS):
            cols = slice(q * piece, (q + 1) * piece)
            result = (own_ref[rows, cols].astype(F32) + other_ref[rows, cols].astype(F32)).astype(BF16)
            result_ref[rows, cols] = result
            gated.append((gate * result.astype(F32)).astype(BF16))
        bands = dot(back_ref[...], jnp.concatenate(gated, axis=0)).astype(BF16)
        for b in range(BANDS):
            send_ref[tiles, b * piece : (b + 1) * piece] = bands[
                b * GROUP * TILE : (b + 1) * GROUP * TILE
            ]


def cot_kernel(
    own_ref, other_ref, own_gate, other_gate, result_ref, normed_ref, shuffle_ref,
    own_gated, other_gated, choice_ref, router_ref,
):
    width = own_ref.shape[1]
    piece = width // BANDS

    @pl.when(pl.program_id(0) == 0)
    def _():
        router_ref[...] = jnp.zeros_like(router_ref)

    for tiles, rows in group_slices():
        pieces = unpacked(other_ref[tiles], shuffle_ref[...], width)
        gate = other_gate[rows, 0:1]
        for q, cot in enumerate(pieces):
            other_gated[rows, q * piece : (q + 1) * piece] = (gate * cot).astype(BF16)
        pieces = unpacked(own_ref[tiles], shuffle_ref[...], width)
        gate = own_gate[rows, 0:1]
        total = 0.0
        for q, cot in enumerate(pieces):
            cols = slice(q * piece, (q + 1) * piece)
            own_gated[rows, cols] = (gate * cot).astype(BF16)
            total = total + jnp.sum(cot * result_ref[rows, cols].astype(F32), axis=1, keepdims=True)
        choice = total * gate * (1.0 - gate)
        spread(choice, choice_ref, rows)
        for q in range(PARTS):
            cols = slice(q * piece, (q + 1) * piece)
            router_ref[:, cols] += row_fold(normed_ref[rows, cols].astype(F32) * choice)


def grad_kernel(
    own_ref, other_ref, choice_ref, scale_ref, normed_ref, column_ref, gain_ref, own_router, other_router,
    core_ref, back_ref, send_ref, sums_ref, meta_ref, inverse_ref,
):
    step = pl.program_id(0)
    features = own_ref.shape[1]
    piece = features // PARTS

    @pl.when(step == 0)
    def _():
        sums_ref[...] = jnp.zeros_like(sums_ref)
        inverse_ref[...] = 1.0 / gain_ref[...]

    for sub, (_, rows) in enumerate(group_slices()):
        choice = choice_ref[rows, 0:1]
        scale = scale_ref[rows, 0:1]
        total = 0.0
        grads = []
        for q in range(PARTS):
            cols = slice(q * piece, (q + 1) * piece)
            grad = own_ref[rows, cols].astype(F32) + other_ref[rows, cols].astype(F32)
            grad = grad + choice * column_ref[:, cols]
            cross = grad * normed_ref[rows, cols].astype(F32)
            sums_ref[:, cols] += row_fold(cross)
            total = total + jnp.sum(cross, axis=1, keepdims=True)
            grads.append(grad * gain_ref[:, cols])
        mean = total / features
        moved = []
        for q, grad in enumerate(grads):
            cols = slice(q * piece, (q + 1) * piece)
            unit = normed_ref[rows, cols].astype(F32) * inverse_ref[:, cols]
            moved.append((scale * (grad - mean * unit)).astype(BF16))
        bands = dot(back_ref[...], jnp.concatenate(moved, axis=0)).astype(BF16)
        count = GROUP * TILE
        tiles = pl.ds(pl.multiple_of((step * SUB + sub) * count, count), count)
        for b in range(BANDS):
            send_ref[tiles, b * piece : (b + 1) * piece] = bands[b * count : (b + 1) * count]

    @pl.when(step == pl.num_programs(0) - 1)
    def _():
        gain_sum = jnp.sum(sums_ref[...], axis=0, keepdims=True) * inverse_ref[...]
        router_sum = jnp.sum(own_router[...] + other_router[...], axis=0, keepdims=True)
        lower = core_ref[0, 0] == 0

        def lanes(value, number):
            return value[:, number * META : (number + 1) * META]

        pairs = features // (5 * META)
        for pair in range(pairs):
            for r in range(5):
                meta_ref[pair * TILE + r : pair * TILE + r + 1, :] = lanes(gain_sum, pair * 5 + r)
            for r in range(3):
                at = pair * 5 + r
                meta_ref[pair * TILE + 5 + r : pair * TILE + 6 + r, :] = jnp.where(
                    lower, lanes(router_sum, at), lanes(router_sum, at + 2)
                )
        meta = meta_ref[...].astype(BF16)
        for at in range(0, send_ref.shape[0], pairs * TILE):
            send_ref[at : at + pairs * TILE, BANDS * piece :] = meta


def by_group(kernel, inputs, outputs, flops, name, scratch=()):
    steps = None
    for value, rows in inputs:
        if isinstance(rows, int) and rows:
            steps = value.shape[0] // (rows * SUB)

    def spec(shape, rows):
        if not isinstance(rows, int):
            return rows
        if rows:
            return pl.BlockSpec((rows * SUB, shape[1]), lambda g: (g, 0))
        return pl.BlockSpec(shape, lambda g: (0, 0))

    moved = sum(value.size * value.dtype.itemsize for value, _ in inputs)
    moved += sum(math.prod(shape) * dtype.itemsize for shape, dtype, _ in outputs)
    return pl.pallas_call(
        kernel,
        grid=(steps,),
        in_specs=[spec(value.shape, rows) for value, rows in inputs],
        out_specs=[spec(shape, rows) for shape, _, rows in outputs],
        out_shape=[jax.ShapeDtypeStruct(shape, dtype) for shape, dtype, _ in outputs],
        scratch_shapes=list(scratch),
        compiler_params=params(1),
        cost_estimate=cost(flops, moved),
        name=name,
    )(*[value for value, _ in inputs])


def forward_kernel(own_ref, other_ref, up_ref, down_ref, out_ref, own_hidden, slope_ref, acc_ref, hidden_ref):
    step = pl.program_id(0)
    half = pl.num_programs(0) // 2
    count = own_ref.shape[0]
    sides = ((slice(0, count), own_ref), (slice(count, 2 * count), other_ref))

    @pl.when(step == 0)
    def _():
        for rows, x_ref in sides:
            acc_ref[rows] = dot(x_ref[...], up_ref[...])

    @pl.when((step > 0) & (step < half))
    def _():
        for rows, x_ref in sides:
            acc_ref[rows] += dot(x_ref[...], up_ref[...])

    @pl.when(step == half - 1)
    def _():
        root = math.sqrt(2.0 / math.pi)
        for (rows, _), kept in zip(sides, (own_hidden, hidden_ref)):
            pre = acc_ref[rows]
            square = pre * pre
            bend = jnp.tanh(root * (pre + 0.044715 * (square * pre)))
            share = 0.5 * (1.0 + bend)
            kept[...] = (pre * share).astype(BF16)
            inner = root * (1.0 + (3.0 * 0.044715) * square)
            slope_ref[rows] = share + 0.5 * pre * (1.0 - bend * bend) * inner

    @pl.when(step >= half)
    def _():
        out_ref[...] = dot(hidden_ref[...], down_ref[...]).astype(BF16)


def backward_kernel(own_ref, other_ref, down_ref, up_ref, slope_ref, out_ref, own_grad, acc_ref, grad_ref):
    step = pl.program_id(0)
    half = pl.num_programs(0) // 2
    count = own_ref.shape[0]
    sides = ((slice(0, count), own_ref), (slice(count, 2 * count), other_ref))

    @pl.when(step == 0)
    def _():
        for rows, cot_ref in sides:
            acc_ref[rows] = dot_nt(cot_ref[...], down_ref[...])

    @pl.when((step > 0) & (step < half))
    def _():
        for rows, cot_ref in sides:
            acc_ref[rows] += dot_nt(cot_ref[...], down_ref[...])

    @pl.when(step == half - 1)
    def _():
        for (rows, _), kept in zip(sides, (own_grad, grad_ref)):
            kept[...] = (acc_ref[rows] * slope_ref[rows]).astype(BF16)

    @pl.when(step >= half)
    def _():
        out_ref[...] = dot_nt(grad_ref[...], up_ref[...]).astype(BF16)


def expert_call(kernel, own, other, up, down, slope, name):
    count, features = own.shape
    hidden = up.shape[2]
    block = features // PARTS
    half = features // block

    def first(i):
        return jnp.minimum(i, half - 1)

    def second(i):
        return jnp.maximum(i - half, 0)

    rows_spec = pl.BlockSpec((count, block), lambda i: (0, first(i)))
    slope_spec = pl.BlockSpec((2 * count, hidden), lambda i: (0, 0))
    out_specs = [
        pl.BlockSpec((count, block), lambda i: (0, second(i))),
        pl.BlockSpec((count, hidden), lambda i: (0, 0)),
    ]
    out_shapes = [
        jax.ShapeDtypeStruct((count, features), BF16),
        jax.ShapeDtypeStruct((count, hidden), BF16),
    ]
    forward = slope is None
    early, late = (first, second) if forward else (second, first)
    up_spec = pl.BlockSpec((None, block, hidden), lambda i: (0, early(i), 0))
    down_spec = pl.BlockSpec((None, hidden, block), lambda i: (0, 0, late(i)))
    if forward:
        args, in_specs = (own, other, up, down), [rows_spec, rows_spec, up_spec, down_spec]
        out_specs.append(slope_spec)
        out_shapes.append(jax.ShapeDtypeStruct((2 * count, hidden), F32))
    else:
        args = (own, other, down, up, slope)
        in_specs = [rows_spec, rows_spec, down_spec, up_spec, slope_spec]
    return pl.pallas_call(
        kernel,
        grid=(2 * half,),
        in_specs=in_specs,
        out_specs=out_specs,
        out_shape=out_shapes,
        scratch_shapes=[pltpu.VMEM((2 * count, hidden), F32), pltpu.VMEM((count, hidden), BF16)],
        compiler_params=params(1),
        cost_estimate=cost(6 * count * features * hidden, 4 * features * (2 * count + hidden)),
        name=name,
    )(*args)


def last_kernel(x_ref, weight_ref, out_ref, *, product):
    out_ref[...] = product(x_ref[...], weight_ref[...]).astype(BF16)


def last_call(product, x, weight, name):
    count, hidden = x.shape
    features = weight.shape[2] if product is dot else weight.shape[1]
    block = features // PARTS
    if product is dot:
        weight_spec = pl.BlockSpec((None, hidden, block), lambda i: (0, 0, i))
    else:
        weight_spec = pl.BlockSpec((None, block, hidden), lambda i: (0, i, 0))
    return pl.pallas_call(
        functools.partial(last_kernel, product=product),
        grid=(PARTS,),
        in_specs=[pl.BlockSpec((count, hidden), lambda i: (0, 0)), weight_spec],
        out_specs=pl.BlockSpec((count, block), lambda i: (0, i)),
        out_shape=jax.ShapeDtypeStruct((count, features), BF16),
        compiler_params=params(1),
        cost_estimate=cost(2 * count * features * hidden * LOUD, 2 * features * (count + hidden) * LOUD),
        name=name,
    )(x, weight)


def exchange(messages):
    blocks = messages.reshape(-1, TILE, messages.shape[1])
    blocks = lax.all_to_all(blocks, CHIPS, split_axis=0, concat_axis=0, tiled=True)
    return blocks.reshape(messages.shape)


def swap(value):
    return lax.ppermute(value, "core", [(0, 1), (1, 0)])


def body(tokens, norm_gain, router_weight, up_weight, down_weight, expert_ids, cotangent):
    toks, features = tokens.shape
    eps, pairs, cores = (lax.axis_size(name) for name in EVERY)
    experts = eps * pairs
    shard = features // (pairs * cores)
    rows = experts * CAP
    devices = experts * cores

    core = jnp.full((1, 1), lax.axis_index("core"), jnp.int32)
    matrix = shuffle_matrix()
    shuffle, shuffle_back = jnp.asarray(matrix, BF16), jnp.asarray(matrix.T, BF16)
    ids_t = expert_ids.T
    group_rows, group_tiles = GROUP * CAP, GROUP * TILE
    row_shape, tiles, width = (rows, features), experts * TILE, features * CAP // TILE
    wide, line, fold = (rows, 128), (1, features), (8, features)
    shuffling = 2 * rows * features * CAP * PARTS * GROUP // PARTS
    b16, f32 = jnp.dtype(BF16), jnp.dtype(F32)
    meta_spec = pl.BlockSpec((pairs * TILE, META), lambda g: (0, width // META))

    cot_sent = pack(ids_t, cotangent, experts)
    arrived = exchange(pack(ids_t, tokens, experts, (norm_gain, router_weight.T, core)))
    arrived, cot_sent = lax.optimization_barrier((arrived, cot_sent))
    arrived_other = swap(arrived)
    cot_arrived = exchange(cot_sent)
    normed, normed_other, gate, gate_other, scale, gain, column = by_group(
        norm_kernel,
        [
            (arrived, group_tiles),
            (arrived_other, group_tiles),
            (arrived, meta_spec),
            (arrived_other, meta_spec),
            (core, SMALL),
            (shuffle, 0),
        ],
        [
            (row_shape, b16, group_rows),
            (row_shape, b16, group_rows),
            (wide, f32, group_rows),
            (wide, f32, group_rows),
            (wide, f32, group_rows),
            (line, f32, 0),
            (line, f32, 0),
        ],
        2 * shuffling,
        "norm",
    )
    other_part, hidden, slope = expert_call(
        forward_kernel, normed, normed_other, up_weight, down_weight, None, "forward"
    )
    other_part = swap(other_part)
    own_part = last_call(dot, hidden, down_weight, "forward_own")
    result, result_sent = by_group(
        out_kernel,
        [(own_part, group_rows), (other_part, group_rows), (gate, group_rows), (shuffle_back, 0)],
        [(row_shape, b16, group_rows), ((tiles, width), b16, group_tiles)],
        shuffling,
        "out",
    )
    cot_arrived, result_sent = lax.optimization_barrier((cot_arrived, result_sent))
    cot_other = swap(cot_arrived)
    result_back = exchange(result_sent)
    gated, gated_other, choice, router_sum = by_group(
        cot_kernel,
        [
            (cot_arrived, group_tiles),
            (cot_other, group_tiles),
            (gate, group_rows),
            (gate_other, group_rows),
            (result, group_rows),
            (normed, group_rows),
            (shuffle, 0),
        ],
        [
            (row_shape, b16, group_rows),
            (row_shape, b16, group_rows),
            (wide, f32, group_rows),
            (fold, f32, 0),
        ],
        2 * shuffling,
        "cot",
    )
    router_other = swap(router_sum)
    other_grad, grad_hidden = expert_call(
        backward_kernel, gated, gated_other, up_weight, down_weight, slope, "backward"
    )
    other_grad = swap(other_grad)
    own_grad = last_call(dot_nt, grad_hidden, up_weight, "backward_own")
    (grad_sent,) = by_group(
        grad_kernel,
        [
            (own_grad, group_rows),
            (other_grad, group_rows),
            (choice, group_rows),
            (scale, group_rows),
            (normed, group_rows),
            (column, 0),
            (gain, 0),
            (router_sum, 0),
            (router_other, 0),
            (core, SMALL),
            (shuffle_back, 0),
        ],
        [((tiles, width + META), b16, 0)],
        shuffling,
        "grad",
        [pltpu.VMEM(fold, F32), pltpu.VMEM((pairs * TILE, META), F32), pltpu.VMEM(line, F32)],
    )
    grad_back = exchange(grad_sent)
    out_rows = jax.ShapeDtypeStruct((toks, features), BF16)
    choosing = jax.ShapeDtypeStruct((BANDS, 2 * toks, tiles), BF16)
    mixed, choose = token_side(
        mixed_kernel, [expert_ids, tokens], result_back, [out_rows, choosing], "mixed"
    )
    (grad_tokens,) = token_side(
        grad_tokens_kernel, [choose, cotangent], grad_back, [out_rows], "grad_tokens"
    )
    grad_router, own_gain, other_gain = summed(grad_back, core, shard, 1.0 / math.sqrt(toks * devices))
    grad_gain = (own_gain + swap(other_gain)).reshape(shard)
    grad_router = grad_router.T
    return mixed, grad_tokens, grad_router, grad_gain


def solution(mesh):
    eps, fsdp = mesh.devices.shape
    fine = Mesh(mesh.devices.reshape(eps, fsdp // 2, 2), EVERY)
    in_specs = (
        P(EVERY, None),
        P(FSDP),
        P(FSDP, None),
        P(EVERY, None, None),
        P(EVERY, None, None),
        P(EVERY, None),
        P(EVERY, None),
    )
    out_specs = (P(EVERY, None), P(EVERY, None), P(FSDP, None), P(FSDP))
    return jax.shard_map(body, mesh=fine, in_specs=in_specs, out_specs=out_specs, check_vma=False)
```

```python
import functools
import math

import jax
import jax.numpy as jnp
import numpy as np
from jax import lax
from jax.experimental import pallas as pl
from jax.experimental.pallas import tpu as pltpu
from jax.sharding import Mesh
from jax.sharding import PartitionSpec as P

EPS = 1e-06
CAP = 6
PARTS = 4
TILE = 8
BANDS = CAP * PARTS // TILE
GROUP = 8
BF16 = jnp.bfloat16
F32 = jnp.float32
LOUD = 64
PACK_STEPS = 2
META = 128
SUB = 4
VMEM_LIMIT = 56 * 1024 * 1024
CHIPS = ("pair", "ep")
FSDP = ("pair", "core")
EVERY = ("ep", "pair", "core")


def params(steps):
    return pltpu.CompilerParams(
        dimension_semantics=("arbitrary",) * steps, vmem_limit_bytes=VMEM_LIMIT
    )


def cost(flops, bytes_accessed):
    return pl.CostEstimate(flops=flops, bytes_accessed=bytes_accessed, transcendentals=0)


def iota(shape, dim):
    return lax.broadcasted_iota(jnp.int32, shape, dim)


def dot(a, b):
    return jnp.dot(a, b, preferred_element_type=F32)


def dot_nt(a, b):
    return lax.dot_general(a, b, (((1,), (1,)), ((), ())), preferred_element_type=F32)


def message_of(expert, eps, pairs):
    return expert % pairs * eps + expert // pairs


def as_bf16(mask):
    return mask.astype(F32).astype(BF16)


def shuffle_matrix():
    size = CAP * PARTS * GROUP
    matrix = np.zeros((size, size), np.float32)
    for message in range(GROUP):
        for number in range(CAP * PARTS):
            piece, slot = divmod(number, CAP)
            band, row = divmod(number, TILE)
            matrix[
                piece * GROUP * CAP + message * CAP + slot,
                band * GROUP * TILE + message * TILE + row,
            ] = 1.0
    return matrix


def slot_target(band, column):
    row = column & (TILE - 1)
    limit = CAP - 2 * band
    low = row < limit
    slot = 2 * band + row - jnp.where(low, 0, CAP)
    return (column >> 3) * CAP + slot, low


def pack_kernel(eps, pairs, ids_ref, rows_ref, *refs):
    *meta_refs, out_ref, pos_ref = refs
    step = pl.program_id(0)
    toks, features = rows_ref.shape
    count = out_ref.shape[0]
    piece = features // PARTS
    experts = eps * pairs

    @pl.when(step == 0)
    def _():
        first, second = (message_of(ids_ref[k : k + 1, :], eps, pairs) for k in range(2))
        expert = iota((experts, toks), 0)
        in_first, in_second = expert == first, expert == second
        both = as_bf16(in_first | in_second)
        earlier = as_bf16(iota((toks, toks), 0) < iota((toks, toks), 1))
        earlier_count = dot(both, earlier)
        slot_first = jnp.sum(jnp.where(in_first, earlier_count, 0.0), axis=0, keepdims=True)
        slot_second = jnp.sum(jnp.where(in_second, earlier_count, 0.0), axis=0, keepdims=True)
        pos_ref[0:1, :] = first * CAP + slot_first.astype(jnp.int32)
        pos_ref[1:2, :] = second * CAP + slot_second.astype(jnp.int32)

    row = step * count + iota((count, toks), 0)
    for band in range(BANDS):
        target, low = slot_target(band, row)
        hit = (target == pos_ref[0:1, :]) | (target == pos_ref[1:2, :])
        placing = jnp.concatenate([as_bf16(hit & low), as_bf16(hit & ~low)], axis=1)
        pieces = [rows_ref[:, p * piece : (p + 1) * piece] for p in (band, band + 1)]
        out_ref[:, band * piece : (band + 1) * piece] = dot(
            placing, jnp.concatenate(pieces, axis=0)
        ).astype(BF16)

    if meta_refs:
        gain_ref, router_ref, core_ref = meta_refs
        shard = router_ref.shape[1]
        shift = core_ref[0, 0] * (META // 2)
        shifted = as_bf16(iota((shard, 3 * META), 1) == iota((shard, 3 * META), 0) + shift)
        gain = dot(gain_ref[...].reshape(1, shard), shifted)
        columns = dot(router_ref[...], shifted).astype(BF16)
        tile_row = iota((count, META), 0) & (TILE - 1)
        pick_row = step * count + iota((count, experts), 0)
        pick_column = message_of(iota((count, experts), 1), eps, pairs)
        total = jnp.zeros((count, META), F32)
        for r in range(3):
            lanes = slice(r * META, (r + 1) * META)
            total = jnp.where(tile_row == r, gain[0:1, lanes], total)
            total = total + dot(as_bf16(pick_row == pick_column * TILE + 3 + r), columns[:, lanes])
        out_ref[:, BANDS * piece :] = total.astype(BF16)


SMALL = pl.BlockSpec(memory_space=pltpu.SMEM)


def pack(ids_t, rows, eps, pairs, meta=()):
    toks, features = rows.shape
    width = features * CAP // TILE + (META if meta else 0)
    out_rows = eps * pairs * TILE
    steps = PACK_STEPS
    meta_specs = []
    if meta:
        gain, router, _ = meta
        meta_specs = [
            pl.BlockSpec(gain.shape, lambda i: (0,)),
            pl.BlockSpec(router.shape, lambda i: (0, 0)),
            SMALL,
        ]
    return pl.pallas_call(
        functools.partial(pack_kernel, eps, pairs),
        grid=(steps,),
        in_specs=[
            pl.BlockSpec((2, toks), lambda i: (0, 0)),
            pl.BlockSpec((toks, features), lambda i: (0, 0)),
            *meta_specs,
        ],
        out_specs=pl.BlockSpec((out_rows // steps, width), lambda i: (i, 0)),
        out_shape=jax.ShapeDtypeStruct((out_rows, width), BF16),
        scratch_shapes=[pltpu.VMEM((8, toks), jnp.int32)],
        compiler_params=params(1),
        cost_estimate=cost(2 * out_rows * 2 * toks * width, 2 * out_rows * width),
        name="pack",
    )(ids_t, rows, *meta)


def fill_choosing(eps, pairs, ids_ref, choose_ref):
    toks = ids_ref.shape[0]
    columns = choose_ref.shape[2]
    experts = eps * pairs
    first, second = (message_of(ids_ref[:, k : k + 1], eps, pairs) for k in range(2))
    expert = iota((toks, experts), 1)
    in_first, in_second = expert == first, expert == second
    both = as_bf16(in_first | in_second)
    earlier = as_bf16(iota((toks, toks), 1) < iota((toks, toks), 0))
    count = dot(earlier, both)
    pos_first = first * CAP + jnp.sum(
        jnp.where(in_first, count, 0.0), axis=1, keepdims=True
    ).astype(jnp.int32)
    pos_second = second * CAP + jnp.sum(
        jnp.where(in_second, count, 0.0), axis=1, keepdims=True
    ).astype(jnp.int32)
    for band in range(BANDS):
        target, low = slot_target(band, iota((toks, columns), 1))
        hit = (target == pos_first) | (target == pos_second)
        choose_ref[band, :toks, :] = as_bf16(hit & low)
        choose_ref[band, toks:, :] = as_bf16(hit & ~low)


def summed_pieces(choose_ref, band_refs):
    toks = choose_ref.shape[1] // 2
    sums = [dot(choose_ref[band], band_refs[band][...]) for band in range(BANDS)]
    pieces = [sums[0][:toks]]
    for band in range(1, BANDS):
        pieces.append(sums[band - 1][toks:] + sums[band][:toks])
    pieces.append(sums[BANDS - 1][toks:])
    return pieces


def add_pieces(base_ref, choose_ref, band_refs, out_ref):
    piece = base_ref.shape[1] // PARTS
    for number, value in enumerate(summed_pieces(choose_ref, band_refs)):
        cols = slice(number * piece, (number + 1) * piece)
        out_ref[:, cols] = (base_ref[:, cols].astype(F32) + value).astype(BF16)


def mixed_kernel(eps, pairs, ids_ref, tokens_ref, band0, band1, band2, out_ref, choose_ref):
    fill_choosing(eps, pairs, ids_ref, choose_ref)
    add_pieces(tokens_ref, choose_ref, (band0, band1, band2), out_ref)


def grad_tokens_kernel(choose_ref, cot_ref, band0, band1, band2, out_ref):
    add_pieces(cot_ref, choose_ref, (band0, band1, band2), out_ref)


def token_side(kernel, inputs, bands, out_shapes, name):
    columns = bands.shape[0]
    piece = inputs[-1].shape[1] // PARTS

    def whole(shape):
        return pl.BlockSpec(shape, lambda c: (0,) * len(shape))

    def band_spec(band):
        return pl.BlockSpec((columns, piece), lambda c: (0, band))

    return pl.pallas_call(
        kernel,
        grid=(1,),
        in_specs=[whole(value.shape) for value in inputs] + [band_spec(b) for b in range(BANDS)],
        out_specs=[whole(shape.shape) for shape in out_shapes],
        out_shape=out_shapes,
        compiler_params=params(1),
        cost_estimate=cost(columns * columns * BANDS * piece, 2 * columns * BANDS * piece),
        name=name,
    )(*inputs, *([bands] * BANDS))


def sums_kernel(scale, eps, pairs, meta_ref, core_ref, router_ref, own_ref, other_ref):
    messages = meta_ref[...]
    tiles = messages.shape[0]
    experts, shard = router_ref.shape
    lower = core_ref[0, 0] == 0
    start = message_of(iota((experts, tiles), 0), eps, pairs) * TILE
    rows = [dot(as_bf16(iota((experts, tiles), 1) == start + 5 + r), messages) for r in range(3)]
    router = jnp.concatenate(rows, axis=1) * scale
    router_ref[...] = jnp.where(lower, router[:, :shard], router[:, META // 2 : META // 2 + shard])
    total = dot(as_bf16((iota((TILE, tiles), 1) & (TILE - 1)) == iota((TILE, tiles), 0)), messages)
    total = jnp.concatenate([total[r : r + 1] for r in range(5)], axis=1) * scale
    first, second = total[:, :shard], total[:, shard : 2 * shard]
    own_ref[...] = jnp.where(lower, first, second)
    other_ref[...] = jnp.where(lower, second, first)


def summed(messages, core, eps, pairs, shard, scale):
    tiles, width = messages.shape
    row = jax.ShapeDtypeStruct((1, shard), F32)
    return pl.pallas_call(
        functools.partial(sums_kernel, scale, eps, pairs),
        grid=(1,),
        in_specs=[pl.BlockSpec((tiles, META), lambda i: (0, width // META - 1)), SMALL],
        out_specs=[
            pl.BlockSpec((tiles // TILE, shard), lambda i: (0, 0)),
            pl.BlockSpec((1, shard), lambda i: (0, 0)),
            pl.BlockSpec((1, shard), lambda i: (0, 0)),
        ],
        out_shape=[jax.ShapeDtypeStruct((tiles // TILE, shard), F32), row, row],
        compiler_params=params(1),
        cost_estimate=cost(10**6, 2 * tiles * META),
        name="sums",
    )(messages, core)


def unpacked(block, shuffle, width):
    piece = width // BANDS
    stacked = jnp.concatenate([block[:, b * piece : (b + 1) * piece] for b in range(BANDS)], axis=0)
    rows = dot(shuffle, stacked)
    count = GROUP * CAP
    return [rows[q * count : (q + 1) * count] for q in range(PARTS)]


def spread(column, ref, rows):
    ref[rows] = jnp.broadcast_to(column, (GROUP * CAP, ref.shape[1]))


def row_fold(value):
    total = value[0:8]
    for at in range(8, value.shape[0], 8):
        total = total + value[at : at + 8]
    return total


def group_slices():
    for sub in range(SUB):
        yield (
            slice(sub * GROUP * TILE, (sub + 1) * GROUP * TILE),
            slice(sub * GROUP * CAP, (sub + 1) * GROUP * CAP),
        )


def norm_kernel(
    own_ref, other_ref, own_meta, other_meta, core_ref, shuffle_ref,
    own_normed, other_normed, own_gate, other_gate, scale_ref, gain_ref, column_ref,
):
    features = own_normed.shape[1]
    width = own_ref.shape[1] - META
    piece = features // PARTS

    @pl.when(pl.program_id(0) == 0)
    def _():
        own, other = own_meta[...].astype(F32), other_meta[...].astype(F32)
        lower = core_ref[0, 0] == 0
        first, second = jnp.where(lower, own, other), jnp.where(lower, other, own)
        for part, ref in ((0, gain_ref), (3, column_ref)):
            pairs = features // (5 * META)
            for pair in range(pairs):
                at = pair * (own.shape[0] // pairs) + part
                rows = [first[at + r : at + r + 1] for r in range(3)]
                rows += [second[at + r : at + r + 1] for r in range(3)]
                rows = [rows[0], rows[1], rows[2] + rows[3], rows[4], rows[5]]
                ref[:, pair * 5 * META : (pair + 1) * 5 * META] = jnp.concatenate(rows, axis=1)

    for block_ref, normed_ref, gate_ref in (
        (own_ref, own_normed, own_gate),
        (other_ref, other_normed, other_gate),
    ):
        for tiles, rows in group_slices():
            pieces = unpacked(block_ref[tiles, :width], shuffle_ref[...], width)
            square = sum(jnp.sum(x * x, axis=1, keepdims=True) for x in pieces)
            scale = lax.rsqrt(square / features + EPS)
            if block_ref is own_ref:
                spread(scale, scale_ref, rows)
            logit = 0.0
            for q, x in enumerate(pieces):
                cols = slice(q * piece, (q + 1) * piece)
                normed = (x * scale * gain_ref[:, cols]).astype(BF16)
                normed_ref[rows, cols] = normed
                logit = logit + jnp.sum(
                    normed.astype(F32) * column_ref[:, cols], axis=1, keepdims=True
                )
            spread(jax.nn.sigmoid(logit), gate_ref, rows)


def out_kernel(own_ref, other_ref, gate_ref, back_ref, result_ref, send_ref):
    piece = own_ref.shape[1] // PARTS
    for tiles, rows in group_slices():
        gate = gate_ref[rows, 0:1]
        gated = []
        for q in range(PARTS):
            cols = slice(q * piece, (q + 1) * piece)
            result = (own_ref[rows, cols].astype(F32) + other_ref[rows, cols].astype(F32)).astype(BF16)
            result_ref[rows, cols] = result
            gated.append((gate * result.astype(F32)).astype(BF16))
        bands = dot(back_ref[...], jnp.concatenate(gated, axis=0)).astype(BF16)
        for b in range(BANDS):
            send_ref[tiles, b * piece : (b + 1) * piece] = bands[
                b * GROUP * TILE : (b + 1) * GROUP * TILE
            ]


def cot_kernel(
    own_ref, other_ref, own_gate, other_gate, result_ref, normed_ref, shuffle_ref,
    own_gated, other_gated, choice_ref, router_ref,
):
    width = own_ref.shape[1]
    piece = width // BANDS

    @pl.when(pl.program_id(0) == 0)
    def _():
        router_ref[...] = jnp.zeros_like(router_ref)

    for tiles, rows in group_slices():
        pieces = unpacked(other_ref[tiles], shuffle_ref[...], width)
        gate = other_gate[rows, 0:1]
        for q, cot in enumerate(pieces):
            other_gated[rows, q * piece : (q + 1) * piece] = (gate * cot).astype(BF16)
        pieces = unpacked(own_ref[tiles], shuffle_ref[...], width)
        gate = own_gate[rows, 0:1]
        total = 0.0
        for q, cot in enumerate(pieces):
            cols = slice(q * piece, (q + 1) * piece)
            own_gated[rows, cols] = (gate * cot).astype(BF16)
            total = total + jnp.sum(cot * result_ref[rows, cols].astype(F32), axis=1, keepdims=True)
        choice = total * gate * (1.0 - gate)
        spread(choice, choice_ref, rows)
        for q in range(PARTS):
            cols = slice(q * piece, (q + 1) * piece)
            router_ref[:, cols] += row_fold(normed_ref[rows, cols].astype(F32) * choice)


def grad_kernel(
    own_ref, other_ref, choice_ref, scale_ref, normed_ref, column_ref, gain_ref, own_router, other_router,
    core_ref, back_ref, send_ref, sums_ref, meta_ref, inverse_ref,
):
    step = pl.program_id(0)
    features = own_ref.shape[1]
    piece = features // PARTS

    @pl.when(step == 0)
    def _():
        sums_ref[...] = jnp.zeros_like(sums_ref)
        inverse_ref[...] = 1.0 / gain_ref[...]

    for sub, (_, rows) in enumerate(group_slices()):
        choice = choice_ref[rows, 0:1]
        scale = scale_ref[rows, 0:1]
        total = 0.0
        grads = []
        for q in range(PARTS):
            cols = slice(q * piece, (q + 1) * piece)
            grad = own_ref[rows, cols].astype(F32) + other_ref[rows, cols].astype(F32)
            grad = grad + choice * column_ref[:, cols]
            cross = grad * normed_ref[rows, cols].astype(F32)
            sums_ref[:, cols] += row_fold(cross)
            total = total + jnp.sum(cross, axis=1, keepdims=True)
            grads.append(grad * gain_ref[:, cols])
        mean = total / features
        moved = []
        for q, grad in enumerate(grads):
            cols = slice(q * piece, (q + 1) * piece)
            unit = normed_ref[rows, cols].astype(F32) * inverse_ref[:, cols]
            moved.append((scale * (grad - mean * unit)).astype(BF16))
        bands = dot(back_ref[...], jnp.concatenate(moved, axis=0)).astype(BF16)
        count = GROUP * TILE
        tiles = pl.ds(pl.multiple_of((step * SUB + sub) * count, count), count)
        for b in range(BANDS):
            send_ref[tiles, b * piece : (b + 1) * piece] = bands[b * count : (b + 1) * count]

    @pl.when(step == pl.num_programs(0) - 1)
    def _():
        gain_sum = jnp.sum(sums_ref[...], axis=0, keepdims=True) * inverse_ref[...]
        router_sum = jnp.sum(own_router[...] + other_router[...], axis=0, keepdims=True)
        lower = core_ref[0, 0] == 0

        def lanes(value, number):
            return value[:, number * META : (number + 1) * META]

        pairs = features // (5 * META)
        for pair in range(pairs):
            for r in range(5):
                meta_ref[pair * TILE + r : pair * TILE + r + 1, :] = lanes(gain_sum, pair * 5 + r)
            for r in range(3):
                at = pair * 5 + r
                meta_ref[pair * TILE + 5 + r : pair * TILE + 6 + r, :] = jnp.where(
                    lower, lanes(router_sum, at), lanes(router_sum, at + 2)
                )
        count = send_ref.shape[0] // pairs
        for pair in range(pairs):
            meta = meta_ref[pair * TILE : (pair + 1) * TILE]
            meta = jnp.concatenate([meta] * (count // TILE), axis=0).astype(BF16)
            send_ref[pair * count : (pair + 1) * count, BANDS * piece :] = meta


def by_group(kernel, inputs, outputs, flops, name, scratch=()):
    steps = None
    for value, rows in inputs:
        if isinstance(rows, int) and rows:
            steps = value.shape[0] // (rows * SUB)

    def spec(shape, rows):
        if not isinstance(rows, int):
            return rows
        if rows:
            return pl.BlockSpec((rows * SUB, shape[1]), lambda g: (g, 0))
        return pl.BlockSpec(shape, lambda g: (0, 0))

    moved = sum(value.size * value.dtype.itemsize for value, _ in inputs)
    moved += sum(math.prod(shape) * dtype.itemsize for shape, dtype, _ in outputs)
    return pl.pallas_call(
        kernel,
        grid=(steps,),
        in_specs=[spec(value.shape, rows) for value, rows in inputs],
        out_specs=[spec(shape, rows) for shape, _, rows in outputs],
        out_shape=[jax.ShapeDtypeStruct(shape, dtype) for shape, dtype, _ in outputs],
        scratch_shapes=list(scratch),
        compiler_params=params(1),
        cost_estimate=cost(flops, moved),
        name=name,
    )(*[value for value, _ in inputs])


def forward_kernel(own_ref, other_ref, up_ref, down_ref, out_ref, own_hidden, slope_ref, acc_ref, hidden_ref):
    step = pl.program_id(0)
    half = pl.num_programs(0) // 2
    count = own_ref.shape[0]
    sides = ((slice(0, count), own_ref), (slice(count, 2 * count), other_ref))

    @pl.when(step == 0)
    def _():
        for rows, x_ref in sides:
            acc_ref[rows] = dot(x_ref[...], up_ref[...])

    @pl.when((step > 0) & (step < half))
    def _():
        for rows, x_ref in sides:
            acc_ref[rows] += dot(x_ref[...], up_ref[...])

    @pl.when(step == half - 1)
    def _():
        root = math.sqrt(2.0 / math.pi)
        for (rows, _), kept in zip(sides, (own_hidden, hidden_ref)):
            pre = acc_ref[rows]
            square = pre * pre
            bend = jnp.tanh(root * (pre + 0.044715 * (square * pre)))
            share = 0.5 * (1.0 + bend)
            kept[...] = (pre * share).astype(BF16)
            inner = root * (1.0 + (3.0 * 0.044715) * square)
            slope_ref[rows] = share + 0.5 * pre * (1.0 - bend * bend) * inner

    @pl.when(step >= half)
    def _():
        out_ref[...] = dot(hidden_ref[...], down_ref[...]).astype(BF16)


def backward_kernel(own_ref, other_ref, down_ref, up_ref, slope_ref, out_ref, own_grad, acc_ref, grad_ref):
    step = pl.program_id(0)
    half = pl.num_programs(0) // 2
    count = own_ref.shape[0]
    sides = ((slice(0, count), own_ref), (slice(count, 2 * count), other_ref))

    @pl.when(step == 0)
    def _():
        for rows, cot_ref in sides:
            acc_ref[rows] = dot_nt(cot_ref[...], down_ref[...])

    @pl.when((step > 0) & (step < half))
    def _():
        for rows, cot_ref in sides:
            acc_ref[rows] += dot_nt(cot_ref[...], down_ref[...])

    @pl.when(step == half - 1)
    def _():
        for (rows, _), kept in zip(sides, (own_grad, grad_ref)):
            kept[...] = (acc_ref[rows] * slope_ref[rows]).astype(BF16)

    @pl.when(step >= half)
    def _():
        out_ref[...] = dot_nt(grad_ref[...], up_ref[...]).astype(BF16)


def expert_call(kernel, own, other, up, down, slope, name):
    count, features = own.shape
    hidden = up.shape[2]
    block = features // PARTS
    half = features // block

    def first(i):
        return jnp.minimum(i, half - 1)

    def second(i):
        return jnp.maximum(i - half, 0)

    rows_spec = pl.BlockSpec((count, block), lambda i: (0, first(i)))
    slope_spec = pl.BlockSpec((2 * count, hidden), lambda i: (0, 0))
    out_specs = [
        pl.BlockSpec((count, block), lambda i: (0, second(i))),
        pl.BlockSpec((count, hidden), lambda i: (0, 0)),
    ]
    out_shapes = [
        jax.ShapeDtypeStruct((count, features), BF16),
        jax.ShapeDtypeStruct((count, hidden), BF16),
    ]
    forward = slope is None
    early, late = (first, second) if forward else (second, first)
    up_spec = pl.BlockSpec((None, block, hidden), lambda i: (0, early(i), 0))
    down_spec = pl.BlockSpec((None, hidden, block), lambda i: (0, 0, late(i)))
    if forward:
        args, in_specs = (own, other, up, down), [rows_spec, rows_spec, up_spec, down_spec]
        out_specs.append(slope_spec)
        out_shapes.append(jax.ShapeDtypeStruct((2 * count, hidden), F32))
    else:
        args = (own, other, down, up, slope)
        in_specs = [rows_spec, rows_spec, down_spec, up_spec, slope_spec]
    return pl.pallas_call(
        kernel,
        grid=(2 * half,),
        in_specs=in_specs,
        out_specs=out_specs,
        out_shape=out_shapes,
        scratch_shapes=[pltpu.VMEM((2 * count, hidden), F32), pltpu.VMEM((count, hidden), BF16)],
        compiler_params=params(1),
        cost_estimate=cost(6 * count * features * hidden, 4 * features * (2 * count + hidden)),
        name=name,
    )(*args)


def last_kernel(x_ref, weight_ref, out_ref, *, product):
    out_ref[...] = product(x_ref[...], weight_ref[...]).astype(BF16)


def last_call(product, x, weight, name):
    count, hidden = x.shape
    features = weight.shape[2] if product is dot else weight.shape[1]
    block = features // PARTS
    if product is dot:
        weight_spec = pl.BlockSpec((None, hidden, block), lambda i: (0, 0, i))
    else:
        weight_spec = pl.BlockSpec((None, block, hidden), lambda i: (0, i, 0))
    return pl.pallas_call(
        functools.partial(last_kernel, product=product),
        grid=(PARTS,),
        in_specs=[pl.BlockSpec((count, hidden), lambda i: (0, 0)), weight_spec],
        out_specs=pl.BlockSpec((count, block), lambda i: (0, i)),
        out_shape=jax.ShapeDtypeStruct((count, features), BF16),
        compiler_params=params(1),
        cost_estimate=cost(2 * count * features * hidden * LOUD, 2 * features * (count + hidden) * LOUD),
        name=name,
    )(x, weight)


def exchange(messages):
    blocks = messages.reshape(-1, TILE, messages.shape[1])
    blocks = lax.all_to_all(blocks, CHIPS, split_axis=0, concat_axis=0, tiled=True)
    return blocks.reshape(messages.shape)


def swap(value):
    return lax.ppermute(value, "core", [(0, 1), (1, 0)])


def body(tokens, norm_gain, router_weight, up_weight, down_weight, expert_ids, cotangent):
    toks, features = tokens.shape
    eps, pairs, cores = (lax.axis_size(name) for name in EVERY)
    experts = eps * pairs
    shard = features // (pairs * cores)
    rows = experts * CAP
    devices = experts * cores

    core = jnp.full((1, 1), lax.axis_index("core"), jnp.int32)
    matrix = shuffle_matrix()
    shuffle, shuffle_back = jnp.asarray(matrix, BF16), jnp.asarray(matrix.T, BF16)
    ids_t = expert_ids.T
    group_rows, group_tiles = GROUP * CAP, GROUP * TILE
    row_shape, tiles, width = (rows, features), experts * TILE, features * CAP // TILE
    wide, line, fold = (rows, 128), (1, features), (8, features)
    shuffling = 2 * rows * features * CAP * PARTS * GROUP // PARTS
    b16, f32 = jnp.dtype(BF16), jnp.dtype(F32)
    meta_spec = pl.BlockSpec((tiles, META), lambda g: (0, width // META))

    cot_sent = pack(ids_t, cotangent, eps, pairs)
    arrived = exchange(pack(ids_t, tokens, eps, pairs, (norm_gain, router_weight.T, core)))
    arrived, cot_sent = lax.optimization_barrier((arrived, cot_sent))
    arrived_other = swap(arrived)
    cot_arrived = exchange(cot_sent)
    normed, normed_other, gate, gate_other, scale, gain, column = by_group(
        norm_kernel,
        [
            (arrived, group_tiles),
            (arrived_other, group_tiles),
            (arrived, meta_spec),
            (arrived_other, meta_spec),
            (core, SMALL),
            (shuffle, 0),
        ],
        [
            (row_shape, b16, group_rows),
            (row_shape, b16, group_rows),
            (wide, f32, group_rows),
            (wide, f32, group_rows),
            (wide, f32, group_rows),
            (line, f32, 0),
            (line, f32, 0),
        ],
        2 * shuffling,
        "norm",
    )
    other_part, hidden, slope = expert_call(
        forward_kernel, normed, normed_other, up_weight, down_weight, None, "forward"
    )
    other_part = swap(other_part)
    own_part = last_call(dot, hidden, down_weight, "forward_own")
    result, result_sent = by_group(
        out_kernel,
        [(own_part, group_rows), (other_part, group_rows), (gate, group_rows), (shuffle_back, 0)],
        [(row_shape, b16, group_rows), ((tiles, width), b16, group_tiles)],
        shuffling,
        "out",
    )
    cot_arrived, result_sent = lax.optimization_barrier((cot_arrived, result_sent))
    cot_other = swap(cot_arrived)
    result_back = exchange(result_sent)
    gated, gated_other, choice, router_sum = by_group(
        cot_kernel,
        [
            (cot_arrived, group_tiles),
            (cot_other, group_tiles),
            (gate, group_rows),
            (gate_other, group_rows),
            (result, group_rows),
            (normed, group_rows),
            (shuffle, 0),
        ],
        [
            (row_shape, b16, group_rows),
            (row_shape, b16, group_rows),
            (wide, f32, group_rows),
            (fold, f32, 0),
        ],
        2 * shuffling,
        "cot",
    )
    router_other = swap(router_sum)
    other_grad, grad_hidden = expert_call(
        backward_kernel, gated, gated_other, up_weight, down_weight, slope, "backward"
    )
    other_grad = swap(other_grad)
    own_grad = last_call(dot_nt, grad_hidden, up_weight, "backward_own")
    (grad_sent,) = by_group(
        grad_kernel,
        [
            (own_grad, group_rows),
            (other_grad, group_rows),
            (choice, group_rows),
            (scale, group_rows),
            (normed, group_rows),
            (column, 0),
            (gain, 0),
            (router_sum, 0),
            (router_other, 0),
            (core, SMALL),
            (shuffle_back, 0),
        ],
        [((tiles, width + META), b16, 0)],
        shuffling,
        "grad",
        [pltpu.VMEM(fold, F32), pltpu.VMEM((pairs * TILE, META), F32), pltpu.VMEM(line, F32)],
    )
    grad_back = exchange(grad_sent)
    out_rows = jax.ShapeDtypeStruct((toks, features), BF16)
    choosing = jax.ShapeDtypeStruct((BANDS, 2 * toks, tiles), BF16)
    mixed, choose = token_side(
        functools.partial(mixed_kernel, eps, pairs),
        [expert_ids, tokens],
        result_back,
        [out_rows, choosing],
        "mixed",
    )
    (grad_tokens,) = token_side(
        grad_tokens_kernel, [choose, cotangent], grad_back, [out_rows], "grad_tokens"
    )
    grad_router, own_gain, other_gain = summed(grad_back, core, eps, pairs, shard, 1.0 / math.sqrt(toks * devices))
    grad_gain = (own_gain + swap(other_gain)).reshape(shard)
    grad_router = grad_router.T
    return mixed, grad_tokens, grad_router, grad_gain


def solution(mesh):
    eps, fsdp = mesh.devices.shape
    fine = Mesh(mesh.devices.reshape(eps, fsdp // 2, 2), EVERY)
    in_specs = (
        P(EVERY, None),
        P(FSDP),
        P(FSDP, None),
        P(EVERY, None, None),
        P(EVERY, None, None),
        P(EVERY, None),
        P(EVERY, None),
    )
    out_specs = (P(EVERY, None), P(EVERY, None), P(FSDP, None), P(FSDP))
    return jax.shard_map(body, mesh=fine, in_specs=in_specs, out_specs=out_specs, check_vma=False)
```

```python
import functools
import math

import jax
import jax.numpy as jnp
import numpy as np
from jax import lax
from jax.experimental import pallas as pl
from jax.experimental.pallas import tpu as pltpu
from jax.sharding import Mesh
from jax.sharding import PartitionSpec as P

EPS = 1e-06
CAP = 6
PARTS = 4
TILE = 8
BANDS = CAP * PARTS // TILE
GROUP = 8
BF16 = jnp.bfloat16
F32 = jnp.float32
LOUD = 64
PACK_STEPS = 2
META = 128
SUB = 4
VMEM_LIMIT = 56 * 1024 * 1024
CHIPS = ("side", "line", "ep")
FSDP = ("line", "side", "core")
EVERY = ("ep", "line", "side", "core")


def params(steps):
    return pltpu.CompilerParams(
        dimension_semantics=("arbitrary",) * steps, vmem_limit_bytes=VMEM_LIMIT
    )


def cost(flops, bytes_accessed):
    return pl.CostEstimate(flops=flops, bytes_accessed=bytes_accessed, transcendentals=0)


def iota(shape, dim):
    return lax.broadcasted_iota(jnp.int32, shape, dim)


def dot(a, b):
    return jnp.dot(a, b, preferred_element_type=F32)


def dot_nt(a, b):
    return lax.dot_general(a, b, (((1,), (1,)), ((), ())), preferred_element_type=F32)


def message_of(expert, eps, pairs):
    return place_of(expert % pairs, pairs) * eps + expert // pairs


def place_of(pair, pairs):
    return pair % 2 * (pairs // 2) + pair // 2


def as_bf16(mask):
    return mask.astype(F32).astype(BF16)


def shuffle_matrix():
    size = CAP * PARTS * GROUP
    matrix = np.zeros((size, size), np.float32)
    for message in range(GROUP):
        for number in range(CAP * PARTS):
            piece, slot = divmod(number, CAP)
            band, row = divmod(number, TILE)
            matrix[
                piece * GROUP * CAP + message * CAP + slot,
                band * GROUP * TILE + message * TILE + row,
            ] = 1.0
    return matrix


def slot_target(band, column):
    row = column & (TILE - 1)
    limit = CAP - 2 * band
    low = row < limit
    slot = 2 * band + row - jnp.where(low, 0, CAP)
    return (column >> 3) * CAP + slot, low


def pack_kernel(eps, pairs, ids_ref, rows_ref, *refs):
    *meta_refs, out_ref, pos_ref = refs
    step = pl.program_id(0)
    toks, features = rows_ref.shape
    count = out_ref.shape[0]
    piece = features // PARTS
    experts = eps * pairs

    @pl.when(step == 0)
    def _():
        first, second = (message_of(ids_ref[k : k + 1, :], eps, pairs) for k in range(2))
        expert = iota((experts, toks), 0)
        in_first, in_second = expert == first, expert == second
        both = as_bf16(in_first | in_second)
        earlier = as_bf16(iota((toks, toks), 0) < iota((toks, toks), 1))
        earlier_count = dot(both, earlier)
        slot_first = jnp.sum(jnp.where(in_first, earlier_count, 0.0), axis=0, keepdims=True)
        slot_second = jnp.sum(jnp.where(in_second, earlier_count, 0.0), axis=0, keepdims=True)
        pos_ref[0:1, :] = first * CAP + slot_first.astype(jnp.int32)
        pos_ref[1:2, :] = second * CAP + slot_second.astype(jnp.int32)

    row = step * count + iota((count, toks), 0)
    for band in range(BANDS):
        target, low = slot_target(band, row)
        hit = (target == pos_ref[0:1, :]) | (target == pos_ref[1:2, :])
        placing = jnp.concatenate([as_bf16(hit & low), as_bf16(hit & ~low)], axis=1)
        pieces = [rows_ref[:, p * piece : (p + 1) * piece] for p in (band, band + 1)]
        out_ref[:, band * piece : (band + 1) * piece] = dot(
            placing, jnp.concatenate(pieces, axis=0)
        ).astype(BF16)

    if meta_refs:
        gain_ref, router_ref, core_ref = meta_refs
        shard = router_ref.shape[1]
        shift = core_ref[0, 0] * (META // 2)
        shifted = as_bf16(iota((shard, 3 * META), 1) == iota((shard, 3 * META), 0) + shift)
        gain = dot(gain_ref[...].reshape(1, shard), shifted)
        columns = dot(router_ref[...], shifted).astype(BF16)
        tile_row = iota((count, META), 0) & (TILE - 1)
        pick_row = step * count + iota((count, experts), 0)
        pick_column = message_of(iota((count, experts), 1), eps, pairs)
        total = jnp.zeros((count, META), F32)
        for r in range(3):
            lanes = slice(r * META, (r + 1) * META)
            total = jnp.where(tile_row == r, gain[0:1, lanes], total)
            total = total + dot(as_bf16(pick_row == pick_column * TILE + 3 + r), columns[:, lanes])
        out_ref[:, BANDS * piece :] = total.astype(BF16)


SMALL = pl.BlockSpec(memory_space=pltpu.SMEM)


def pack(ids_t, rows, eps, pairs, meta=()):
    toks, features = rows.shape
    width = features * CAP // TILE + (META if meta else 0)
    out_rows = eps * pairs * TILE
    steps = PACK_STEPS
    meta_specs = []
    if meta:
        gain, router, _ = meta
        meta_specs = [
            pl.BlockSpec(gain.shape, lambda i: (0,)),
            pl.BlockSpec(router.shape, lambda i: (0, 0)),
            SMALL,
        ]
    return pl.pallas_call(
        functools.partial(pack_kernel, eps, pairs),
        grid=(steps,),
        in_specs=[
            pl.BlockSpec((2, toks), lambda i: (0, 0)),
            pl.BlockSpec((toks, features), lambda i: (0, 0)),
            *meta_specs,
        ],
        out_specs=pl.BlockSpec((out_rows // steps, width), lambda i: (i, 0)),
        out_shape=jax.ShapeDtypeStruct((out_rows, width), BF16),
        scratch_shapes=[pltpu.VMEM((8, toks), jnp.int32)],
        compiler_params=params(1),
        cost_estimate=cost(2 * out_rows * 2 * toks * width, 2 * out_rows * width),
        name="pack",
    )(ids_t, rows, *meta)


def fill_choosing(eps, pairs, ids_ref, choose_ref):
    toks = ids_ref.shape[0]
    columns = choose_ref.shape[2]
    experts = eps * pairs
    first, second = (message_of(ids_ref[:, k : k + 1], eps, pairs) for k in range(2))
    expert = iota((toks, experts), 1)
    in_first, in_second = expert == first, expert == second
    both = as_bf16(in_first | in_second)
    earlier = as_bf16(iota((toks, toks), 1) < iota((toks, toks), 0))
    count = dot(earlier, both)
    pos_first = first * CAP + jnp.sum(
        jnp.where(in_first, count, 0.0), axis=1, keepdims=True
    ).astype(jnp.int32)
    pos_second = second * CAP + jnp.sum(
        jnp.where(in_second, count, 0.0), axis=1, keepdims=True
    ).astype(jnp.int32)
    for band in range(BANDS):
        target, low = slot_target(band, iota((toks, columns), 1))
        hit = (target == pos_first) | (target == pos_second)
        choose_ref[band, :toks, :] = as_bf16(hit & low)
        choose_ref[band, toks:, :] = as_bf16(hit & ~low)


def summed_pieces(choose_ref, band_refs):
    toks = choose_ref.shape[1] // 2
    sums = [dot(choose_ref[band], band_refs[band][...]) for band in range(BANDS)]
    pieces = [sums[0][:toks]]
    for band in range(1, BANDS):
        pieces.append(sums[band - 1][toks:] + sums[band][:toks])
    pieces.append(sums[BANDS - 1][toks:])
    return pieces


def add_pieces(base_ref, choose_ref, band_refs, out_ref):
    piece = base_ref.shape[1] // PARTS
    for number, value in enumerate(summed_pieces(choose_ref, band_refs)):
        cols = slice(number * piece, (number + 1) * piece)
        out_ref[:, cols] = (base_ref[:, cols].astype(F32) + value).astype(BF16)


def mixed_kernel(eps, pairs, ids_ref, tokens_ref, band0, band1, band2, out_ref, choose_ref):
    fill_choosing(eps, pairs, ids_ref, choose_ref)
    add_pieces(tokens_ref, choose_ref, (band0, band1, band2), out_ref)


def grad_tokens_kernel(choose_ref, cot_ref, band0, band1, band2, out_ref):
    add_pieces(cot_ref, choose_ref, (band0, band1, band2), out_ref)


def token_side(kernel, inputs, bands, out_shapes, name):
    columns = bands.shape[0]
    piece = inputs[-1].shape[1] // PARTS

    def whole(shape):
        return pl.BlockSpec(shape, lambda c: (0,) * len(shape))

    def band_spec(band):
        return pl.BlockSpec((columns, piece), lambda c: (0, band))

    return pl.pallas_call(
        kernel,
        grid=(1,),
        in_specs=[whole(value.shape) for value in inputs] + [band_spec(b) for b in range(BANDS)],
        out_specs=[whole(shape.shape) for shape in out_shapes],
        out_shape=out_shapes,
        compiler_params=params(1),
        cost_estimate=cost(columns * columns * BANDS * piece, 2 * columns * BANDS * piece),
        name=name,
    )(*inputs, *([bands] * BANDS))


def sums_kernel(scale, eps, pairs, meta_ref, core_ref, router_ref, own_ref, other_ref):
    messages = meta_ref[...]
    tiles = messages.shape[0]
    experts, shard = router_ref.shape
    lower = core_ref[0, 0] == 0
    start = message_of(iota((experts, tiles), 0), eps, pairs) * TILE
    rows = [dot(as_bf16(iota((experts, tiles), 1) == start + 5 + r), messages) for r in range(3)]
    router = jnp.concatenate(rows, axis=1) * scale
    router_ref[...] = jnp.where(lower, router[:, :shard], router[:, META // 2 : META // 2 + shard])
    total = dot(as_bf16((iota((TILE, tiles), 1) & (TILE - 1)) == iota((TILE, tiles), 0)), messages)
    total = jnp.concatenate([total[r : r + 1] for r in range(5)], axis=1) * scale
    first, second = total[:, :shard], total[:, shard : 2 * shard]
    own_ref[...] = jnp.where(lower, first, second)
    other_ref[...] = jnp.where(lower, second, first)


def summed(messages, core, eps, pairs, shard, scale):
    tiles, width = messages.shape
    row = jax.ShapeDtypeStruct((1, shard), F32)
    return pl.pallas_call(
        functools.partial(sums_kernel, scale, eps, pairs),
        grid=(1,),
        in_specs=[pl.BlockSpec((tiles, META), lambda i: (0, width // META - 1)), SMALL],
        out_specs=[
            pl.BlockSpec((tiles // TILE, shard), lambda i: (0, 0)),
            pl.BlockSpec((1, shard), lambda i: (0, 0)),
            pl.BlockSpec((1, shard), lambda i: (0, 0)),
        ],
        out_shape=[jax.ShapeDtypeStruct((tiles // TILE, shard), F32), row, row],
        compiler_params=params(1),
        cost_estimate=cost(10**6, 2 * tiles * META),
        name="sums",
    )(messages, core)


def unpacked(block, shuffle, width):
    piece = width // BANDS
    stacked = jnp.concatenate([block[:, b * piece : (b + 1) * piece] for b in range(BANDS)], axis=0)
    rows = dot(shuffle, stacked)
    count = GROUP * CAP
    return [rows[q * count : (q + 1) * count] for q in range(PARTS)]


def spread(column, ref, rows):
    ref[rows] = jnp.broadcast_to(column, (GROUP * CAP, ref.shape[1]))


def row_fold(value):
    total = value[0:8]
    for at in range(8, value.shape[0], 8):
        total = total + value[at : at + 8]
    return total


def group_slices():
    for sub in range(SUB):
        yield (
            slice(sub * GROUP * TILE, (sub + 1) * GROUP * TILE),
            slice(sub * GROUP * CAP, (sub + 1) * GROUP * CAP),
        )


def norm_kernel(
    own_ref, other_ref, own_meta, other_meta, core_ref, shuffle_ref,
    own_normed, other_normed, own_gate, other_gate, scale_ref, gain_ref, column_ref,
):
    features = own_normed.shape[1]
    width = own_ref.shape[1] - META
    piece = features // PARTS

    @pl.when(pl.program_id(0) == 0)
    def _():
        own, other = own_meta[...].astype(F32), other_meta[...].astype(F32)
        lower = core_ref[0, 0] == 0
        first, second = jnp.where(lower, own, other), jnp.where(lower, other, own)
        for part, ref in ((0, gain_ref), (3, column_ref)):
            pairs = features // (5 * META)
            for pair in range(pairs):
                at = place_of(pair, pairs) * (own.shape[0] // pairs) + part
                rows = [first[at + r : at + r + 1] for r in range(3)]
                rows += [second[at + r : at + r + 1] for r in range(3)]
                rows = [rows[0], rows[1], rows[2] + rows[3], rows[4], rows[5]]
                ref[:, pair * 5 * META : (pair + 1) * 5 * META] = jnp.concatenate(rows, axis=1)

    for block_ref, normed_ref, gate_ref in (
        (own_ref, own_normed, own_gate),
        (other_ref, other_normed, other_gate),
    ):
        for tiles, rows in group_slices():
            pieces = unpacked(block_ref[tiles, :width], shuffle_ref[...], width)
            square = sum(jnp.sum(x * x, axis=1, keepdims=True) for x in pieces)
            scale = lax.rsqrt(square / features + EPS)
            if block_ref is own_ref:
                spread(scale, scale_ref, rows)
            logit = 0.0
            for q, x in enumerate(pieces):
                cols = slice(q * piece, (q + 1) * piece)
                normed = (x * scale * gain_ref[:, cols]).astype(BF16)
                normed_ref[rows, cols] = normed
                logit = logit + jnp.sum(
                    normed.astype(F32) * column_ref[:, cols], axis=1, keepdims=True
                )
            spread(jax.nn.sigmoid(logit), gate_ref, rows)


def out_kernel(own_ref, other_ref, gate_ref, back_ref, result_ref, send_ref):
    piece = own_ref.shape[1] // PARTS
    for tiles, rows in group_slices():
        gate = gate_ref[rows, 0:1]
        gated = []
        for q in range(PARTS):
            cols = slice(q * piece, (q + 1) * piece)
            result = (own_ref[rows, cols].astype(F32) + other_ref[rows, cols].astype(F32)).astype(BF16)
            result_ref[rows, cols] = result
            gated.append((gate * result.astype(F32)).astype(BF16))
        bands = dot(back_ref[...], jnp.concatenate(gated, axis=0)).astype(BF16)
        for b in range(BANDS):
            send_ref[tiles, b * piece : (b + 1) * piece] = bands[
                b * GROUP * TILE : (b + 1) * GROUP * TILE
            ]


def cot_kernel(
    own_ref, other_ref, own_gate, other_gate, result_ref, normed_ref, shuffle_ref,
    own_gated, other_gated, choice_ref, router_ref,
):
    width = own_ref.shape[1]
    piece = width // BANDS

    @pl.when(pl.program_id(0) == 0)
    def _():
        router_ref[...] = jnp.zeros_like(router_ref)

    for tiles, rows in group_slices():
        pieces = unpacked(other_ref[tiles], shuffle_ref[...], width)
        gate = other_gate[rows, 0:1]
        for q, cot in enumerate(pieces):
            other_gated[rows, q * piece : (q + 1) * piece] = (gate * cot).astype(BF16)
        pieces = unpacked(own_ref[tiles], shuffle_ref[...], width)
        gate = own_gate[rows, 0:1]
        total = 0.0
        for q, cot in enumerate(pieces):
            cols = slice(q * piece, (q + 1) * piece)
            own_gated[rows, cols] = (gate * cot).astype(BF16)
            total = total + jnp.sum(cot * result_ref[rows, cols].astype(F32), axis=1, keepdims=True)
        choice = total * gate * (1.0 - gate)
        spread(choice, choice_ref, rows)
        for q in range(PARTS):
            cols = slice(q * piece, (q + 1) * piece)
            router_ref[:, cols] += row_fold(normed_ref[rows, cols].astype(F32) * choice)


def grad_kernel(
    own_ref, other_ref, choice_ref, scale_ref, normed_ref, column_ref, gain_ref, own_router, other_router,
    core_ref, back_ref, send_ref, sums_ref, meta_ref, inverse_ref,
):
    step = pl.program_id(0)
    features = own_ref.shape[1]
    piece = features // PARTS

    @pl.when(step == 0)
    def _():
        sums_ref[...] = jnp.zeros_like(sums_ref)
        inverse_ref[...] = 1.0 / gain_ref[...]

    for sub, (_, rows) in enumerate(group_slices()):
        choice = choice_ref[rows, 0:1]
        scale = scale_ref[rows, 0:1]
        total = 0.0
        grads = []
        for q in range(PARTS):
            cols = slice(q * piece, (q + 1) * piece)
            grad = own_ref[rows, cols].astype(F32) + other_ref[rows, cols].astype(F32)
            grad = grad + choice * column_ref[:, cols]
            cross = grad * normed_ref[rows, cols].astype(F32)
            sums_ref[:, cols] += row_fold(cross)
            total = total + jnp.sum(cross, axis=1, keepdims=True)
            grads.append(grad * gain_ref[:, cols])
        mean = total / features
        moved = []
        for q, grad in enumerate(grads):
            cols = slice(q * piece, (q + 1) * piece)
            unit = normed_ref[rows, cols].astype(F32) * inverse_ref[:, cols]
            moved.append((scale * (grad - mean * unit)).astype(BF16))
        bands = dot(back_ref[...], jnp.concatenate(moved, axis=0)).astype(BF16)
        count = GROUP * TILE
        tiles = pl.ds(pl.multiple_of((step * SUB + sub) * count, count), count)
        for b in range(BANDS):
            send_ref[tiles, b * piece : (b + 1) * piece] = bands[b * count : (b + 1) * count]

    @pl.when(step == pl.num_programs(0) - 1)
    def _():
        gain_sum = jnp.sum(sums_ref[...], axis=0, keepdims=True) * inverse_ref[...]
        router_sum = jnp.sum(own_router[...] + other_router[...], axis=0, keepdims=True)
        lower = core_ref[0, 0] == 0

        def lanes(value, number):
            return value[:, number * META : (number + 1) * META]

        pairs = features // (5 * META)
        for pair in range(pairs):
            for r in range(5):
                meta_ref[pair * TILE + r : pair * TILE + r + 1, :] = lanes(gain_sum, pair * 5 + r)
            for r in range(3):
                at = pair * 5 + r
                meta_ref[pair * TILE + 5 + r : pair * TILE + 6 + r, :] = jnp.where(
                    lower, lanes(router_sum, at), lanes(router_sum, at + 2)
                )
        count = send_ref.shape[0] // pairs
        for pair in range(pairs):
            meta = meta_ref[pair * TILE : (pair + 1) * TILE]
            meta = jnp.concatenate([meta] * (count // TILE), axis=0).astype(BF16)
            at = place_of(pair, pairs) * count
            send_ref[at : at + count, BANDS * piece :] = meta


def by_group(kernel, inputs, outputs, flops, name, scratch=()):
    steps = None
    for value, rows in inputs:
        if isinstance(rows, int) and rows:
            steps = value.shape[0] // (rows * SUB)

    def spec(shape, rows):
        if not isinstance(rows, int):
            return rows
        if rows:
            return pl.BlockSpec((rows * SUB, shape[1]), lambda g: (g, 0))
        return pl.BlockSpec(shape, lambda g: (0, 0))

    moved = sum(value.size * value.dtype.itemsize for value, _ in inputs)
    moved += sum(math.prod(shape) * dtype.itemsize for shape, dtype, _ in outputs)
    return pl.pallas_call(
        kernel,
        grid=(steps,),
        in_specs=[spec(value.shape, rows) for value, rows in inputs],
        out_specs=[spec(shape, rows) for shape, _, rows in outputs],
        out_shape=[jax.ShapeDtypeStruct(shape, dtype) for shape, dtype, _ in outputs],
        scratch_shapes=list(scratch),
        compiler_params=params(1),
        cost_estimate=cost(flops, moved),
        name=name,
    )(*[value for value, _ in inputs])


def forward_kernel(own_ref, other_ref, up_ref, down_ref, out_ref, own_hidden, slope_ref, acc_ref, hidden_ref):
    step = pl.program_id(0)
    half = pl.num_programs(0) // 2
    count = own_ref.shape[0]
    sides = ((slice(0, count), own_ref), (slice(count, 2 * count), other_ref))

    @pl.when(step == 0)
    def _():
        for rows, x_ref in sides:
            acc_ref[rows] = dot(x_ref[...], up_ref[...])

    @pl.when((step > 0) & (step < half))
    def _():
        for rows, x_ref in sides:
            acc_ref[rows] += dot(x_ref[...], up_ref[...])

    @pl.when(step == half - 1)
    def _():
        root = math.sqrt(2.0 / math.pi)
        for (rows, _), kept in zip(sides, (own_hidden, hidden_ref)):
            pre = acc_ref[rows]
            square = pre * pre
            bend = jnp.tanh(root * (pre + 0.044715 * (square * pre)))
            share = 0.5 * (1.0 + bend)
            kept[...] = (pre * share).astype(BF16)
            inner = root * (1.0 + (3.0 * 0.044715) * square)
            slope_ref[rows] = share + 0.5 * pre * (1.0 - bend * bend) * inner

    @pl.when(step >= half)
    def _():
        out_ref[...] = dot(hidden_ref[...], down_ref[...]).astype(BF16)


def backward_kernel(own_ref, other_ref, down_ref, up_ref, slope_ref, out_ref, own_grad, acc_ref, grad_ref):
    step = pl.program_id(0)
    half = pl.num_programs(0) // 2
    count = own_ref.shape[0]
    sides = ((slice(0, count), own_ref), (slice(count, 2 * count), other_ref))

    @pl.when(step == 0)
    def _():
        for rows, cot_ref in sides:
            acc_ref[rows] = dot_nt(cot_ref[...], down_ref[...])

    @pl.when((step > 0) & (step < half))
    def _():
        for rows, cot_ref in sides:
            acc_ref[rows] += dot_nt(cot_ref[...], down_ref[...])

    @pl.when(step == half - 1)
    def _():
        for (rows, _), kept in zip(sides, (own_grad, grad_ref)):
            kept[...] = (acc_ref[rows] * slope_ref[rows]).astype(BF16)

    @pl.when(step >= half)
    def _():
        out_ref[...] = dot_nt(grad_ref[...], up_ref[...]).astype(BF16)


def expert_call(kernel, own, other, up, down, slope, name):
    count, features = own.shape
    hidden = up.shape[2]
    block = features // PARTS
    half = features // block

    def first(i):
        return jnp.minimum(i, half - 1)

    def second(i):
        return jnp.maximum(i - half, 0)

    rows_spec = pl.BlockSpec((count, block), lambda i: (0, first(i)))
    slope_spec = pl.BlockSpec((2 * count, hidden), lambda i: (0, 0))
    out_specs = [
        pl.BlockSpec((count, block), lambda i: (0, second(i))),
        pl.BlockSpec((count, hidden), lambda i: (0, 0)),
    ]
    out_shapes = [
        jax.ShapeDtypeStruct((count, features), BF16),
        jax.ShapeDtypeStruct((count, hidden), BF16),
    ]
    forward = slope is None
    early, late = (first, second) if forward else (second, first)
    up_spec = pl.BlockSpec((None, block, hidden), lambda i: (0, early(i), 0))
    down_spec = pl.BlockSpec((None, hidden, block), lambda i: (0, 0, late(i)))
    if forward:
        args, in_specs = (own, other, up, down), [rows_spec, rows_spec, up_spec, down_spec]
        out_specs.append(slope_spec)
        out_shapes.append(jax.ShapeDtypeStruct((2 * count, hidden), F32))
    else:
        args = (own, other, down, up, slope)
        in_specs = [rows_spec, rows_spec, down_spec, up_spec, slope_spec]
    return pl.pallas_call(
        kernel,
        grid=(2 * half,),
        in_specs=in_specs,
        out_specs=out_specs,
        out_shape=out_shapes,
        scratch_shapes=[pltpu.VMEM((2 * count, hidden), F32), pltpu.VMEM((count, hidden), BF16)],
        compiler_params=params(1),
        cost_estimate=cost(6 * count * features * hidden, 4 * features * (2 * count + hidden)),
        name=name,
    )(*args)


def last_kernel(x_ref, weight_ref, out_ref, *, product):
    out_ref[...] = product(x_ref[...], weight_ref[...]).astype(BF16)


def last_call(product, x, weight, name):
    count, hidden = x.shape
    features = weight.shape[2] if product is dot else weight.shape[1]
    block = features // PARTS
    if product is dot:
        weight_spec = pl.BlockSpec((None, hidden, block), lambda i: (0, 0, i))
    else:
        weight_spec = pl.BlockSpec((None, block, hidden), lambda i: (0, i, 0))
    return pl.pallas_call(
        functools.partial(last_kernel, product=product),
        grid=(PARTS,),
        in_specs=[pl.BlockSpec((count, hidden), lambda i: (0, 0)), weight_spec],
        out_specs=pl.BlockSpec((count, block), lambda i: (0, i)),
        out_shape=jax.ShapeDtypeStruct((count, features), BF16),
        compiler_params=params(1),
        cost_estimate=cost(2 * count * features * hidden * LOUD, 2 * features * (count + hidden) * LOUD),
        name=name,
    )(x, weight)


def exchange(messages):
    blocks = messages.reshape(-1, TILE, messages.shape[1])
    blocks = lax.all_to_all(blocks, CHIPS, split_axis=0, concat_axis=0, tiled=True)
    return blocks.reshape(messages.shape)


def swap(value):
    return lax.ppermute(value, "core", [(0, 1), (1, 0)])


def body(tokens, norm_gain, router_weight, up_weight, down_weight, expert_ids, cotangent):
    toks, features = tokens.shape
    eps, lines, sides, cores = (lax.axis_size(name) for name in EVERY)
    pairs = lines * sides
    experts = eps * pairs
    shard = features // (pairs * cores)
    rows = experts * CAP
    devices = experts * cores

    core = jnp.full((1, 1), lax.axis_index("core"), jnp.int32)
    matrix = shuffle_matrix()
    shuffle, shuffle_back = jnp.asarray(matrix, BF16), jnp.asarray(matrix.T, BF16)
    ids_t = expert_ids.T
    group_rows, group_tiles = GROUP * CAP, GROUP * TILE
    row_shape, tiles, width = (rows, features), experts * TILE, features * CAP // TILE
    wide, line, fold = (rows, 128), (1, features), (8, features)
    shuffling = 2 * rows * features * CAP * PARTS * GROUP // PARTS
    b16, f32 = jnp.dtype(BF16), jnp.dtype(F32)
    meta_spec = pl.BlockSpec((tiles, META), lambda g: (0, width // META))

    cot_sent = pack(ids_t, cotangent, eps, pairs)
    arrived = exchange(pack(ids_t, tokens, eps, pairs, (norm_gain, router_weight.T, core)))
    arrived, cot_sent = lax.optimization_barrier((arrived, cot_sent))
    arrived_other = swap(arrived)
    cot_arrived = exchange(cot_sent)
    normed, normed_other, gate, gate_other, scale, gain, column = by_group(
        norm_kernel,
        [
            (arrived, group_tiles),
            (arrived_other, group_tiles),
            (arrived, meta_spec),
            (arrived_other, meta_spec),
            (core, SMALL),
            (shuffle, 0),
        ],
        [
            (row_shape, b16, group_rows),
            (row_shape, b16, group_rows),
            (wide, f32, group_rows),
            (wide, f32, group_rows),
            (wide, f32, group_rows),
            (line, f32, 0),
            (line, f32, 0),
        ],
        2 * shuffling,
        "norm",
    )
    other_part, hidden, slope = expert_call(
        forward_kernel, normed, normed_other, up_weight, down_weight, None, "forward"
    )
    other_part = swap(other_part)
    own_part = last_call(dot, hidden, down_weight, "forward_own")
    result, result_sent = by_group(
        out_kernel,
        [(own_part, group_rows), (other_part, group_rows), (gate, group_rows), (shuffle_back, 0)],
        [(row_shape, b16, group_rows), ((tiles, width), b16, group_tiles)],
        shuffling,
        "out",
    )
    cot_arrived, result_sent = lax.optimization_barrier((cot_arrived, result_sent))
    cot_other = swap(cot_arrived)
    result_back = exchange(result_sent)
    gated, gated_other, choice, router_sum = by_group(
        cot_kernel,
        [
            (cot_arrived, group_tiles),
            (cot_other, group_tiles),
            (gate, group_rows),
            (gate_other, group_rows),
            (result, group_rows),
            (normed, group_rows),
            (shuffle, 0),
        ],
        [
            (row_shape, b16, group_rows),
            (row_shape, b16, group_rows),
            (wide, f32, group_rows),
            (fold, f32, 0),
        ],
        2 * shuffling,
        "cot",
    )
    router_other = swap(router_sum)
    other_grad, grad_hidden = expert_call(
        backward_kernel, gated, gated_other, up_weight, down_weight, slope, "backward"
    )
    other_grad = swap(other_grad)
    own_grad = last_call(dot_nt, grad_hidden, up_weight, "backward_own")
    (grad_sent,) = by_group(
        grad_kernel,
        [
            (own_grad, group_rows),
            (other_grad, group_rows),
            (choice, group_rows),
            (scale, group_rows),
            (normed, group_rows),
            (column, 0),
            (gain, 0),
            (router_sum, 0),
            (router_other, 0),
            (core, SMALL),
            (shuffle_back, 0),
        ],
        [((tiles, width + META), b16, 0)],
        shuffling,
        "grad",
        [pltpu.VMEM(fold, F32), pltpu.VMEM((pairs * TILE, META), F32), pltpu.VMEM(line, F32)],
    )
    grad_back = exchange(grad_sent)
    out_rows = jax.ShapeDtypeStruct((toks, features), BF16)
    choosing = jax.ShapeDtypeStruct((BANDS, 2 * toks, tiles), BF16)
    mixed, choose = token_side(
        functools.partial(mixed_kernel, eps, pairs),
        [expert_ids, tokens],
        result_back,
        [out_rows, choosing],
        "mixed",
    )
    (grad_tokens,) = token_side(
        grad_tokens_kernel, [choose, cotangent], grad_back, [out_rows], "grad_tokens"
    )
    grad_router, own_gain, other_gain = summed(grad_back, core, eps, pairs, shard, 1.0 / math.sqrt(toks * devices))
    grad_gain = (own_gain + swap(other_gain)).reshape(shard)
    grad_router = grad_router.T
    return mixed, grad_tokens, grad_router, grad_gain


def solution(mesh):
    eps, fsdp = mesh.devices.shape
    fine = Mesh(mesh.devices.reshape(eps, fsdp // 4, 2, 2), EVERY)
    in_specs = (
        P(EVERY, None),
        P(FSDP),
        P(FSDP, None),
        P(EVERY, None, None),
        P(EVERY, None, None),
        P(EVERY, None),
        P(EVERY, None),
    )
    out_specs = (P(EVERY, None), P(EVERY, None), P(FSDP, None), P(FSDP))
    return jax.shard_map(body, mesh=fine, in_specs=in_specs, out_specs=out_specs, check_vma=False)
```

```python
import functools
import math

import jax
import jax.numpy as jnp
import numpy as np
from jax import lax
from jax.experimental import pallas as pl
from jax.experimental.pallas import tpu as pltpu
from jax.sharding import Mesh
from jax.sharding import PartitionSpec as P

EPS = 1e-06
CAP = 6
PARTS = 4
TILE = 8
BANDS = CAP * PARTS // TILE
GROUP = 8
BF16 = jnp.bfloat16
F32 = jnp.float32
LOUD = 64
PACK_STEPS = 2
META = 128
SUB = 4
VMEM_LIMIT = 56 * 1024 * 1024
CHIPS = ("pair", "ep")
FSDP = ("pair", "core")
EVERY = ("ep", "pair", "core")


def params(steps):
    return pltpu.CompilerParams(
        dimension_semantics=("arbitrary",) * steps, vmem_limit_bytes=VMEM_LIMIT
    )


def cost(flops, bytes_accessed):
    return pl.CostEstimate(flops=flops, bytes_accessed=bytes_accessed, transcendentals=0)


def iota(shape, dim):
    return lax.broadcasted_iota(jnp.int32, shape, dim)


def dot(a, b):
    return jnp.dot(a, b, preferred_element_type=F32)


def dot_nt(a, b):
    return lax.dot_general(a, b, (((1,), (1,)), ((), ())), preferred_element_type=F32)


def message_of(expert, eps, pairs):
    return expert % pairs * eps + expert // pairs


def as_bf16(mask):
    return mask.astype(F32).astype(BF16)


def shuffle_matrix():
    size = CAP * PARTS * GROUP
    matrix = np.zeros((size, size), np.float32)
    for message in range(GROUP):
        for number in range(CAP * PARTS):
            piece, slot = divmod(number, CAP)
            band, row = divmod(number, TILE)
            matrix[
                piece * GROUP * CAP + message * CAP + slot,
                band * GROUP * TILE + message * TILE + row,
            ] = 1.0
    return matrix


def slot_target(band, column):
    row = column & (TILE - 1)
    limit = CAP - 2 * band
    low = row < limit
    slot = 2 * band + row - jnp.where(low, 0, CAP)
    return (column >> 3) * CAP + slot, low


def pack_kernel(eps, pairs, ids_ref, rows_ref, *refs):
    *meta_refs, out_ref, pos_ref = refs
    step = pl.program_id(0)
    toks, features = rows_ref.shape
    count = out_ref.shape[0]
    piece = features // PARTS
    experts = eps * pairs

    @pl.when(step == 0)
    def _():
        first, second = (message_of(ids_ref[k : k + 1, :], eps, pairs) for k in range(2))
        expert = iota((experts, toks), 0)
        in_first, in_second = expert == first, expert == second
        both = as_bf16(in_first | in_second)
        earlier = as_bf16(iota((toks, toks), 0) < iota((toks, toks), 1))
        earlier_count = dot(both, earlier)
        slot_first = jnp.sum(jnp.where(in_first, earlier_count, 0.0), axis=0, keepdims=True)
        slot_second = jnp.sum(jnp.where(in_second, earlier_count, 0.0), axis=0, keepdims=True)
        pos_ref[0:1, :] = first * CAP + slot_first.astype(jnp.int32)
        pos_ref[1:2, :] = second * CAP + slot_second.astype(jnp.int32)

    row = step * count + iota((count, toks), 0)
    for band in range(BANDS):
        target, low = slot_target(band, row)
        hit = (target == pos_ref[0:1, :]) | (target == pos_ref[1:2, :])
        placing = jnp.concatenate([as_bf16(hit & low), as_bf16(hit & ~low)], axis=1)
        pieces = [rows_ref[:, p * piece : (p + 1) * piece] for p in (band, band + 1)]
        out_ref[:, band * piece : (band + 1) * piece] = dot(
            placing, jnp.concatenate(pieces, axis=0)
        ).astype(BF16)

    if meta_refs:
        gain_ref, router_ref, core_ref = meta_refs
        shard = router_ref.shape[1]
        shift = core_ref[0, 0] * (META // 2)
        shifted = as_bf16(iota((shard, 3 * META), 1) == iota((shard, 3 * META), 0) + shift)
        gain = dot(gain_ref[...].reshape(1, shard), shifted)
        columns = dot(router_ref[...], shifted).astype(BF16)
        tile_row = iota((count, META), 0) & (TILE - 1)
        pick_row = step * count + iota((count, experts), 0)
        pick_column = message_of(iota((count, experts), 1), eps, pairs)
        total = jnp.zeros((count, META), F32)
        for r in range(3):
            lanes = slice(r * META, (r + 1) * META)
            total = jnp.where(tile_row == r, gain[0:1, lanes], total)
            total = total + dot(as_bf16(pick_row == pick_column * TILE + 3 + r), columns[:, lanes])
        out_ref[:, BANDS * piece :] = total.astype(BF16)


SMALL = pl.BlockSpec(memory_space=pltpu.SMEM)


def pack(ids_t, rows, eps, pairs, meta=()):
    toks, features = rows.shape
    width = features * CAP // TILE + (META if meta else 0)
    out_rows = eps * pairs * TILE
    steps = PACK_STEPS
    meta_specs = []
    if meta:
        gain, router, _ = meta
        meta_specs = [
            pl.BlockSpec(gain.shape, lambda i: (0,)),
            pl.BlockSpec(router.shape, lambda i: (0, 0)),
            SMALL,
        ]
    return pl.pallas_call(
        functools.partial(pack_kernel, eps, pairs),
        grid=(steps,),
        in_specs=[
            pl.BlockSpec((2, toks), lambda i: (0, 0)),
            pl.BlockSpec((toks, features), lambda i: (0, 0)),
            *meta_specs,
        ],
        out_specs=pl.BlockSpec((out_rows // steps, width), lambda i: (i, 0)),
        out_shape=jax.ShapeDtypeStruct((out_rows, width), BF16),
        scratch_shapes=[pltpu.VMEM((8, toks), jnp.int32)],
        compiler_params=params(1),
        cost_estimate=cost(2 * out_rows * 2 * toks * width, 2 * out_rows * width),
        name="pack",
    )(ids_t, rows, *meta)


def fill_choosing(eps, pairs, ids_ref, choose_ref):
    toks = ids_ref.shape[0]
    columns = choose_ref.shape[2]
    experts = eps * pairs
    first, second = (message_of(ids_ref[:, k : k + 1], eps, pairs) for k in range(2))
    expert = iota((toks, experts), 1)
    in_first, in_second = expert == first, expert == second
    both = as_bf16(in_first | in_second)
    earlier = as_bf16(iota((toks, toks), 1) < iota((toks, toks), 0))
    count = dot(earlier, both)
    pos_first = first * CAP + jnp.sum(
        jnp.where(in_first, count, 0.0), axis=1, keepdims=True
    ).astype(jnp.int32)
    pos_second = second * CAP + jnp.sum(
        jnp.where(in_second, count, 0.0), axis=1, keepdims=True
    ).astype(jnp.int32)
    for band in range(BANDS):
        target, low = slot_target(band, iota((toks, columns), 1))
        hit = (target == pos_first) | (target == pos_second)
        choose_ref[band, :toks, :] = as_bf16(hit & low)
        choose_ref[band, toks:, :] = as_bf16(hit & ~low)


def summed_pieces(choose_ref, band_refs):
    toks = choose_ref.shape[1] // 2
    sums = [dot(choose_ref[band], band_refs[band][...]) for band in range(BANDS)]
    pieces = [sums[0][:toks]]
    for band in range(1, BANDS):
        pieces.append(sums[band - 1][toks:] + sums[band][:toks])
    pieces.append(sums[BANDS - 1][toks:])
    return pieces


def add_pieces(base_ref, choose_ref, band_refs, out_ref):
    piece = base_ref.shape[1] // PARTS
    for number, value in enumerate(summed_pieces(choose_ref, band_refs)):
        cols = slice(number * piece, (number + 1) * piece)
        out_ref[:, cols] = (base_ref[:, cols].astype(F32) + value).astype(BF16)


def mixed_kernel(eps, pairs, ids_ref, tokens_ref, band0, band1, band2, out_ref, choose_ref):
    fill_choosing(eps, pairs, ids_ref, choose_ref)
    add_pieces(tokens_ref, choose_ref, (band0, band1, band2), out_ref)


def grad_tokens_kernel(choose_ref, cot_ref, band0, band1, band2, out_ref):
    add_pieces(cot_ref, choose_ref, (band0, band1, band2), out_ref)


def token_side(kernel, inputs, bands, out_shapes, name):
    columns = bands.shape[0]
    piece = inputs[-1].shape[1] // PARTS

    def whole(shape):
        return pl.BlockSpec(shape, lambda c: (0,) * len(shape))

    def band_spec(band):
        return pl.BlockSpec((columns, piece), lambda c: (0, band))

    return pl.pallas_call(
        kernel,
        grid=(1,),
        in_specs=[whole(value.shape) for value in inputs] + [band_spec(b) for b in range(BANDS)],
        out_specs=[whole(shape.shape) for shape in out_shapes],
        out_shape=out_shapes,
        compiler_params=params(1),
        cost_estimate=cost(columns * columns * BANDS * piece, 2 * columns * BANDS * piece),
        name=name,
    )(*inputs, *([bands] * BANDS))


def sums_kernel(scale, eps, pairs, meta_ref, core_ref, router_ref, own_ref, other_ref):
    messages = meta_ref[...]
    tiles = messages.shape[0]
    experts, shard = router_ref.shape
    lower = core_ref[0, 0] == 0
    start = message_of(iota((experts, tiles), 0), eps, pairs) * TILE
    picks = [as_bf16(iota((experts, tiles), 1) == start + 5 + r) for r in range(3)]
    picks.append(as_bf16((iota((2 * TILE, tiles), 1) & (TILE - 1)) == iota((2 * TILE, tiles), 0)))
    picked = dot(jnp.concatenate(picks, axis=0), messages)
    rows = [picked[r * experts : (r + 1) * experts] for r in range(3)]
    router = jnp.concatenate(rows, axis=1) * scale
    router_ref[...] = jnp.where(lower, router[:, :shard], router[:, META // 2 : META // 2 + shard])
    total = picked[3 * experts :]
    total = jnp.concatenate([total[r : r + 1] for r in range(5)], axis=1) * scale
    first, second = total[:, :shard], total[:, shard : 2 * shard]
    own_ref[...] = jnp.where(lower, first, second)
    other_ref[...] = jnp.where(lower, second, first)


def summed(messages, core, eps, pairs, shard, scale):
    tiles, width = messages.shape
    row = jax.ShapeDtypeStruct((1, shard), F32)
    return pl.pallas_call(
        functools.partial(sums_kernel, scale, eps, pairs),
        grid=(1,),
        in_specs=[pl.BlockSpec((tiles, META), lambda i: (0, width // META - 1)), SMALL],
        out_specs=[
            pl.BlockSpec((tiles // TILE, shard), lambda i: (0, 0)),
            pl.BlockSpec((1, shard), lambda i: (0, 0)),
            pl.BlockSpec((1, shard), lambda i: (0, 0)),
        ],
        out_shape=[jax.ShapeDtypeStruct((tiles // TILE, shard), F32), row, row],
        compiler_params=params(1),
        cost_estimate=cost(10**6, 2 * tiles * META),
        name="sums",
    )(messages, core)


def unpacked(block, shuffle, width):
    piece = width // BANDS
    stacked = jnp.concatenate([block[:, b * piece : (b + 1) * piece] for b in range(BANDS)], axis=0)
    rows = dot(shuffle, stacked)
    count = GROUP * CAP
    return [rows[q * count : (q + 1) * count] for q in range(PARTS)]


def spread(column, ref, rows):
    ref[rows] = jnp.broadcast_to(column, (GROUP * CAP, ref.shape[1]))


def row_fold(value):
    total = value[0:8]
    for at in range(8, value.shape[0], 8):
        total = total + value[at : at + 8]
    return total


def group_slices():
    for sub in range(SUB):
        yield (
            slice(sub * GROUP * TILE, (sub + 1) * GROUP * TILE),
            slice(sub * GROUP * CAP, (sub + 1) * GROUP * CAP),
        )


def norm_kernel(
    own_ref, other_ref, own_meta, other_meta, core_ref, shuffle_ref,
    own_normed, other_normed, own_gate, other_gate, scale_ref, gain_ref, column_ref,
):
    features = own_normed.shape[1]
    width = own_ref.shape[1] - META
    piece = features // PARTS

    @pl.when(pl.program_id(0) == 0)
    def _():
        own, other = own_meta[...].astype(F32), other_meta[...].astype(F32)
        lower = core_ref[0, 0] == 0
        first, second = jnp.where(lower, own, other), jnp.where(lower, other, own)
        for part, ref in ((0, gain_ref), (3, column_ref)):
            pairs = features // (5 * META)
            for pair in range(pairs):
                at = pair * (own.shape[0] // pairs) + part
                rows = [first[at + r : at + r + 1] for r in range(3)]
                rows += [second[at + r : at + r + 1] for r in range(3)]
                rows = [rows[0], rows[1], rows[2] + rows[3], rows[4], rows[5]]
                ref[:, pair * 5 * META : (pair + 1) * 5 * META] = jnp.concatenate(rows, axis=1)

    for block_ref, normed_ref, gate_ref in (
        (own_ref, own_normed, own_gate),
        (other_ref, other_normed, other_gate),
    ):
        for tiles, rows in group_slices():
            pieces = unpacked(block_ref[tiles, :width], shuffle_ref[...], width)
            square = sum(jnp.sum(x * x, axis=1, keepdims=True) for x in pieces)
            scale = lax.rsqrt(square / features + EPS)
            if block_ref is own_ref:
                spread(scale, scale_ref, rows)
            logit = 0.0
            for q, x in enumerate(pieces):
                cols = slice(q * piece, (q + 1) * piece)
                normed = (x * scale * gain_ref[:, cols]).astype(BF16)
                normed_ref[rows, cols] = normed
                logit = logit + jnp.sum(
                    normed.astype(F32) * column_ref[:, cols], axis=1, keepdims=True
                )
            spread(jax.nn.sigmoid(logit), gate_ref, rows)


def out_kernel(own_ref, other_ref, gate_ref, back_ref, result_ref, send_ref):
    piece = own_ref.shape[1] // PARTS
    for tiles, rows in group_slices():
        gate = gate_ref[rows, 0:1]
        gated = []
        for q in range(PARTS):
            cols = slice(q * piece, (q + 1) * piece)
            result = (own_ref[rows, cols].astype(F32) + other_ref[rows, cols].astype(F32)).astype(BF16)
            result_ref[rows, cols] = result
            gated.append((gate * result.astype(F32)).astype(BF16))
        bands = dot(back_ref[...], jnp.concatenate(gated, axis=0)).astype(BF16)
        for b in range(BANDS):
            send_ref[tiles, b * piece : (b + 1) * piece] = bands[
                b * GROUP * TILE : (b + 1) * GROUP * TILE
            ]


def cot_kernel(
    own_ref, other_ref, own_gate, other_gate, result_ref, normed_ref, shuffle_ref,
    own_gated, other_gated, choice_ref, router_ref,
):
    width = own_ref.shape[1]
    piece = width // BANDS

    @pl.when(pl.program_id(0) == 0)
    def _():
        router_ref[...] = jnp.zeros_like(router_ref)

    for tiles, rows in group_slices():
        pieces = unpacked(other_ref[tiles], shuffle_ref[...], width)
        gate = other_gate[rows, 0:1]
        for q, cot in enumerate(pieces):
            other_gated[rows, q * piece : (q + 1) * piece] = (gate * cot).astype(BF16)
        pieces = unpacked(own_ref[tiles], shuffle_ref[...], width)
        gate = own_gate[rows, 0:1]
        total = 0.0
        for q, cot in enumerate(pieces):
            cols = slice(q * piece, (q + 1) * piece)
            own_gated[rows, cols] = (gate * cot).astype(BF16)
            total = total + jnp.sum(cot * result_ref[rows, cols].astype(F32), axis=1, keepdims=True)
        choice = total * gate * (1.0 - gate)
        spread(choice, choice_ref, rows)
        for q in range(PARTS):
            cols = slice(q * piece, (q + 1) * piece)
            router_ref[:, cols] += row_fold(normed_ref[rows, cols].astype(F32) * choice)


def grad_kernel(
    own_ref, other_ref, choice_ref, scale_ref, normed_ref, column_ref, gain_ref, own_router, other_router,
    core_ref, back_ref, send_ref, sums_ref, meta_ref, inverse_ref,
):
    step = pl.program_id(0)
    features = own_ref.shape[1]
    piece = features // PARTS

    @pl.when(step == 0)
    def _():
        sums_ref[...] = jnp.zeros_like(sums_ref)
        inverse_ref[...] = 1.0 / gain_ref[...]

    for sub, (_, rows) in enumerate(group_slices()):
        choice = choice_ref[rows, 0:1]
        scale = scale_ref[rows, 0:1]
        total = 0.0
        grads = []
        for q in range(PARTS):
            cols = slice(q * piece, (q + 1) * piece)
            grad = own_ref[rows, cols].astype(F32) + other_ref[rows, cols].astype(F32)
            grad = grad + choice * column_ref[:, cols]
            cross = grad * normed_ref[rows, cols].astype(F32)
            sums_ref[:, cols] += row_fold(cross)
            total = total + jnp.sum(cross, axis=1, keepdims=True)
            grads.append(grad * gain_ref[:, cols])
        mean = total / features
        moved = []
        for q, grad in enumerate(grads):
            cols = slice(q * piece, (q + 1) * piece)
            unit = normed_ref[rows, cols].astype(F32) * inverse_ref[:, cols]
            moved.append((scale * (grad - mean * unit)).astype(BF16))
        bands = dot(back_ref[...], jnp.concatenate(moved, axis=0)).astype(BF16)
        count = GROUP * TILE
        tiles = pl.ds(pl.multiple_of((step * SUB + sub) * count, count), count)
        for b in range(BANDS):
            send_ref[tiles, b * piece : (b + 1) * piece] = bands[b * count : (b + 1) * count]

    @pl.when(step == pl.num_programs(0) - 1)
    def _():
        gain_sum = jnp.sum(sums_ref[...], axis=0, keepdims=True) * inverse_ref[...]
        router_sum = jnp.sum(own_router[...] + other_router[...], axis=0, keepdims=True)
        lower = core_ref[0, 0] == 0

        def lanes(value, number):
            return value[:, number * META : (number + 1) * META]

        pairs = features // (5 * META)
        for pair in range(pairs):
            for r in range(5):
                meta_ref[pair * TILE + r : pair * TILE + r + 1, :] = lanes(gain_sum, pair * 5 + r)
            for r in range(3):
                at = pair * 5 + r
                meta_ref[pair * TILE + 5 + r : pair * TILE + 6 + r, :] = jnp.where(
                    lower, lanes(router_sum, at), lanes(router_sum, at + 2)
                )
        count = send_ref.shape[0] // pairs
        for pair in range(pairs):
            meta = meta_ref[pair * TILE : (pair + 1) * TILE]
            meta = jnp.concatenate([meta] * (count // TILE), axis=0).astype(BF16)
            send_ref[pair * count : (pair + 1) * count, BANDS * piece :] = meta


def by_group(kernel, inputs, outputs, flops, name, scratch=()):
    steps = None
    for value, rows in inputs:
        if isinstance(rows, int) and rows:
            steps = value.shape[0] // (rows * SUB)

    def spec(shape, rows):
        if not isinstance(rows, int):
            return rows
        if rows:
            return pl.BlockSpec((rows * SUB, shape[1]), lambda g: (g, 0))
        return pl.BlockSpec(shape, lambda g: (0, 0))

    moved = sum(value.size * value.dtype.itemsize for value, _ in inputs)
    moved += sum(math.prod(shape) * dtype.itemsize for shape, dtype, _ in outputs)
    return pl.pallas_call(
        kernel,
        grid=(steps,),
        in_specs=[spec(value.shape, rows) for value, rows in inputs],
        out_specs=[spec(shape, rows) for shape, _, rows in outputs],
        out_shape=[jax.ShapeDtypeStruct(shape, dtype) for shape, dtype, _ in outputs],
        scratch_shapes=list(scratch),
        compiler_params=params(1),
        cost_estimate=cost(flops, moved),
        name=name,
    )(*[value for value, _ in inputs])


def forward_kernel(own_ref, other_ref, up_ref, down_ref, out_ref, own_hidden, slope_ref, acc_ref, hidden_ref):
    step = pl.program_id(0)
    half = pl.num_programs(0) // 2
    count = own_ref.shape[0]
    sides = ((slice(0, count), own_ref), (slice(count, 2 * count), other_ref))

    @pl.when(step == 0)
    def _():
        for rows, x_ref in sides:
            acc_ref[rows] = dot(x_ref[...], up_ref[...])

    @pl.when((step > 0) & (step < half))
    def _():
        for rows, x_ref in sides:
            acc_ref[rows] += dot(x_ref[...], up_ref[...])

    @pl.when(step == half - 1)
    def _():
        root = math.sqrt(2.0 / math.pi)
        for (rows, _), kept in zip(sides, (own_hidden, hidden_ref)):
            pre = acc_ref[rows]
            square = pre * pre
            bend = jnp.tanh(root * (pre + 0.044715 * (square * pre)))
            share = 0.5 * (1.0 + bend)
            kept[...] = (pre * share).astype(BF16)
            inner = root * (1.0 + (3.0 * 0.044715) * square)
            slope_ref[rows] = share + 0.5 * pre * (1.0 - bend * bend) * inner

    @pl.when(step >= half)
    def _():
        out_ref[...] = dot(hidden_ref[...], down_ref[...]).astype(BF16)


def backward_kernel(own_ref, other_ref, down_ref, up_ref, slope_ref, out_ref, own_grad, acc_ref, grad_ref):
    step = pl.program_id(0)
    half = pl.num_programs(0) // 2
    count = own_ref.shape[0]
    sides = ((slice(0, count), own_ref), (slice(count, 2 * count), other_ref))

    @pl.when(step == 0)
    def _():
        for rows, cot_ref in sides:
            acc_ref[rows] = dot_nt(cot_ref[...], down_ref[...])

    @pl.when((step > 0) & (step < half))
    def _():
        for rows, cot_ref in sides:
            acc_ref[rows] += dot_nt(cot_ref[...], down_ref[...])

    @pl.when(step == half - 1)
    def _():
        for (rows, _), kept in zip(sides, (own_grad, grad_ref)):
            kept[...] = (acc_ref[rows] * slope_ref[rows]).astype(BF16)

    @pl.when(step >= half)
    def _():
        out_ref[...] = dot_nt(grad_ref[...], up_ref[...]).astype(BF16)


def expert_call(kernel, own, other, up, down, slope, name):
    count, features = own.shape
    hidden = up.shape[2]
    block = features // PARTS
    half = features // block

    def first(i):
        return jnp.minimum(i, half - 1)

    def second(i):
        return jnp.maximum(i - half, 0)

    rows_spec = pl.BlockSpec((count, block), lambda i: (0, first(i)))
    slope_spec = pl.BlockSpec((2 * count, hidden), lambda i: (0, 0))
    out_specs = [
        pl.BlockSpec((count, block), lambda i: (0, second(i))),
        pl.BlockSpec((count, hidden), lambda i: (0, 0)),
    ]
    out_shapes = [
        jax.ShapeDtypeStruct((count, features), BF16),
        jax.ShapeDtypeStruct((count, hidden), BF16),
    ]
    forward = slope is None
    early, late = (first, second) if forward else (second, first)
    up_spec = pl.BlockSpec((None, block, hidden), lambda i: (0, early(i), 0))
    down_spec = pl.BlockSpec((None, hidden, block), lambda i: (0, 0, late(i)))
    if forward:
        args, in_specs = (own, other, up, down), [rows_spec, rows_spec, up_spec, down_spec]
        out_specs.append(slope_spec)
        out_shapes.append(jax.ShapeDtypeStruct((2 * count, hidden), F32))
    else:
        args = (own, other, down, up, slope)
        in_specs = [rows_spec, rows_spec, down_spec, up_spec, slope_spec]
    return pl.pallas_call(
        kernel,
        grid=(2 * half,),
        in_specs=in_specs,
        out_specs=out_specs,
        out_shape=out_shapes,
        scratch_shapes=[pltpu.VMEM((2 * count, hidden), F32), pltpu.VMEM((count, hidden), BF16)],
        compiler_params=params(1),
        cost_estimate=cost(6 * count * features * hidden, 4 * features * (2 * count + hidden)),
        name=name,
    )(*args)


def last_kernel(x_ref, weight_ref, out_ref, *, product):
    out_ref[...] = product(x_ref[...], weight_ref[...]).astype(BF16)


def last_call(product, x, weight, name):
    count, hidden = x.shape
    features = weight.shape[2] if product is dot else weight.shape[1]
    block = features // PARTS
    if product is dot:
        weight_spec = pl.BlockSpec((None, hidden, block), lambda i: (0, 0, i))
    else:
        weight_spec = pl.BlockSpec((None, block, hidden), lambda i: (0, i, 0))
    return pl.pallas_call(
        functools.partial(last_kernel, product=product),
        grid=(PARTS,),
        in_specs=[pl.BlockSpec((count, hidden), lambda i: (0, 0)), weight_spec],
        out_specs=pl.BlockSpec((count, block), lambda i: (0, i)),
        out_shape=jax.ShapeDtypeStruct((count, features), BF16),
        compiler_params=params(1),
        cost_estimate=cost(2 * count * features * hidden * LOUD, 2 * features * (count + hidden) * LOUD),
        name=name,
    )(x, weight)


def exchange(messages):
    blocks = messages.reshape(-1, TILE, messages.shape[1])
    blocks = lax.all_to_all(blocks, CHIPS, split_axis=0, concat_axis=0, tiled=True)
    return blocks.reshape(messages.shape)


def swap(value):
    return lax.ppermute(value, "core", [(0, 1), (1, 0)])


def body(tokens, norm_gain, router_weight, up_weight, down_weight, expert_ids, cotangent):
    toks, features = tokens.shape
    eps, pairs, cores = (lax.axis_size(name) for name in EVERY)
    experts = eps * pairs
    shard = features // (pairs * cores)
    rows = experts * CAP
    devices = experts * cores

    core = jnp.full((1, 1), lax.axis_index("core"), jnp.int32)
    matrix = shuffle_matrix()
    shuffle, shuffle_back = jnp.asarray(matrix, BF16), jnp.asarray(matrix.T, BF16)
    ids_t = expert_ids.T
    group_rows, group_tiles = GROUP * CAP, GROUP * TILE
    row_shape, tiles, width = (rows, features), experts * TILE, features * CAP // TILE
    wide, line, fold = (rows, 128), (1, features), (8, features)
    shuffling = 2 * rows * features * CAP * PARTS * GROUP // PARTS
    b16, f32 = jnp.dtype(BF16), jnp.dtype(F32)
    meta_spec = pl.BlockSpec((tiles, META), lambda g: (0, width // META))

    cot_sent = pack(ids_t, cotangent, eps, pairs)
    arrived = exchange(pack(ids_t, tokens, eps, pairs, (norm_gain, router_weight.T, core)))
    arrived, cot_sent = lax.optimization_barrier((arrived, cot_sent))
    arrived_other = swap(arrived)
    cot_arrived = exchange(cot_sent)
    normed, normed_other, gate, gate_other, scale, gain, column = by_group(
        norm_kernel,
        [
            (arrived, group_tiles),
            (arrived_other, group_tiles),
            (arrived, meta_spec),
            (arrived_other, meta_spec),
            (core, SMALL),
            (shuffle, 0),
        ],
        [
            (row_shape, b16, group_rows),
            (row_shape, b16, group_rows),
            (wide, f32, group_rows),
            (wide, f32, group_rows),
            (wide, f32, group_rows),
            (line, f32, 0),
            (line, f32, 0),
        ],
        2 * shuffling,
        "norm",
    )
    other_part, hidden, slope = expert_call(
        forward_kernel, normed, normed_other, up_weight, down_weight, None, "forward"
    )
    other_part = swap(other_part)
    own_part = last_call(dot, hidden, down_weight, "forward_own")
    result, result_sent = by_group(
        out_kernel,
        [(own_part, group_rows), (other_part, group_rows), (gate, group_rows), (shuffle_back, 0)],
        [(row_shape, b16, group_rows), ((tiles, width), b16, group_tiles)],
        shuffling,
        "out",
    )
    cot_arrived, result_sent = lax.optimization_barrier((cot_arrived, result_sent))
    cot_other = swap(cot_arrived)
    result_back = exchange(result_sent)
    gated, gated_other, choice, router_sum = by_group(
        cot_kernel,
        [
            (cot_arrived, group_tiles),
            (cot_other, group_tiles),
            (gate, group_rows),
            (gate_other, group_rows),
            (result, group_rows),
            (normed, group_rows),
            (shuffle, 0),
        ],
        [
            (row_shape, b16, group_rows),
            (row_shape, b16, group_rows),
            (wide, f32, group_rows),
            (fold, f32, 0),
        ],
        2 * shuffling,
        "cot",
    )
    router_other = swap(router_sum)
    other_grad, grad_hidden = expert_call(
        backward_kernel, gated, gated_other, up_weight, down_weight, slope, "backward"
    )
    other_grad = swap(other_grad)
    own_grad = last_call(dot_nt, grad_hidden, up_weight, "backward_own")
    (grad_sent,) = by_group(
        grad_kernel,
        [
            (own_grad, group_rows),
            (other_grad, group_rows),
            (choice, group_rows),
            (scale, group_rows),
            (normed, group_rows),
            (column, 0),
            (gain, 0),
            (router_sum, 0),
            (router_other, 0),
            (core, SMALL),
            (shuffle_back, 0),
        ],
        [((tiles, width + META), b16, 0)],
        shuffling,
        "grad",
        [pltpu.VMEM(fold, F32), pltpu.VMEM((pairs * TILE, META), F32), pltpu.VMEM(line, F32)],
    )
    grad_back = exchange(grad_sent)
    out_rows = jax.ShapeDtypeStruct((toks, features), BF16)
    choosing = jax.ShapeDtypeStruct((BANDS, 2 * toks, tiles), BF16)
    mixed, choose = token_side(
        functools.partial(mixed_kernel, eps, pairs),
        [expert_ids, tokens],
        result_back,
        [out_rows, choosing],
        "mixed",
    )
    (grad_tokens,) = token_side(
        grad_tokens_kernel, [choose, cotangent], grad_back, [out_rows], "grad_tokens"
    )
    grad_router, own_gain, other_gain = summed(grad_back, core, eps, pairs, shard, 1.0 / math.sqrt(toks * devices))
    grad_gain = (own_gain + swap(other_gain)).reshape(shard)
    grad_router = grad_router.T
    return mixed, grad_tokens, grad_router, grad_gain


def solution(mesh):
    eps, fsdp = mesh.devices.shape
    fine = Mesh(mesh.devices.reshape(eps, fsdp // 2, 2), EVERY)
    in_specs = (
        P(EVERY, None),
        P(FSDP),
        P(FSDP, None),
        P(EVERY, None, None),
        P(EVERY, None, None),
        P(EVERY, None),
        P(EVERY, None),
    )
    out_specs = (P(EVERY, None), P(EVERY, None), P(FSDP, None), P(FSDP))
    return jax.shard_map(body, mesh=fine, in_specs=in_specs, out_specs=out_specs, check_vma=False)
```
